32 devices in a mesh: ctx: 8 (over z, y), fsdp: 4 (over x, core).
Axes of the slice: x: 2, y: 2, z: 4, core: 2. Of those that a mesh axis runs over, the one named last changes fastest.
Arguments:
- tokens: bfloat16 [4, 4096, 1024], P('fsdp', 'ctx'), may hold values from -6 to 6
- cotangent: bfloat16 [4, 4096, 1024], P('fsdp', 'ctx'), may hold values from -6 to 6
- doc_starts: int32 [4, 6], P('fsdp'), may hold values from 0 to 4095, as said below
- gain_mix: bfloat16 [1024], P('fsdp'), may hold values from 0.099609375 to 1.8984375
- w_z: bfloat16 [1024, 1536], P('fsdp'), may hold values from -0.1875 to 0.1875
- w_xbc: bfloat16 [1024, 1792], P('fsdp'), may hold values from -0.1875 to 0.1875
- w_dt: bfloat16 [1024, 24], P('fsdp'), may hold values from -0.1875 to 0.1875
- conv_w: bfloat16 [4, 1792], P(None, 'fsdp'), may hold values from -3 to 3
- conv_b: bfloat16 [1792], P('fsdp'), may hold values from -2 to 2
- dt_bias: bfloat16 [24], P('fsdp'), may hold values from -5 to -2
- a_log: bfloat16 [24], P('fsdp'), may hold values from -12 to 2
- skip_factor: bfloat16 [24], P('fsdp'), may hold values from 0.5 to 1.5
- w_mo: bfloat16 [1536, 1024], P('fsdp'), may hold values from -0.15625 to 0.15625
- w_q: bfloat16 [1024, 512], P('fsdp'), may hold values from -0.1875 to 0.1875
- key_value_weight: bfloat16 [1024, 256], P('fsdp'), may hold values from -0.1875 to 0.1875
- w_o: bfloat16 [512, 1024], P('fsdp'), may hold values from -2 to 2
- gain_ffn: bfloat16 [1024], P('fsdp'), may hold values from 0.099609375 to 1.8984375
- w_gate: bfloat16 [1024, 2048], P('fsdp'), may hold values from -0.1875 to 0.1875
- w_up: bfloat16 [1024, 2048], P('fsdp'), may hold values from -0.1875 to 0.1875
- w_down: bfloat16 [2048, 1024], P('fsdp'), may hold values from -0.125 to 0.125
Outputs:
- result: bfloat16 [4, 4096, 1024], P('fsdp', 'ctx')
- grad_tokens: float32 [4, 4096, 1024], P('fsdp', 'ctx')
- grad_gain_mix: float32 [1024], P('fsdp')
- grad_w_z: float32 [1024, 1536], P('fsdp')
- grad_w_xbc: float32 [1024, 1792], P('fsdp')
- grad_w_dt: float32 [1024, 24], P('fsdp')
- grad_conv_w: float32 [4, 1792], P(None, 'fsdp')
- grad_conv_b: float32 [1792], P('fsdp')
- grad_dt_bias: float32 [24], P('fsdp')
- grad_a_log: float32 [24], P('fsdp')
- grad_d_skip: float32 [24], P('fsdp')
- grad_w_mo: float32 [1536, 1024], P('fsdp')
- grad_w_q: float32 [1024, 512], P('fsdp')
- grad_w_kv: float32 [1024, 256], P('fsdp')
- grad_w_o: float32 [512, 1024], P('fsdp')
- grad_gain_ffn: float32 [1024], P('fsdp')
- grad_w_gate: float32 [1024, 2048], P('fsdp')
- grad_w_up: float32 [1024, 2048], P('fsdp')
- grad_w_down: float32 [2048, 1024], P('fsdp')
The draws below stay inside these ranges and needn't reach their ends.
Inputs may be any that keep to these rules, and one draw needn't show every extreme that they name: `doc_starts`: each row is strictly increasing, begins with 0 and ends with 4095; a document runs from one start to the next start or to the end of its stream.
All inputs are finite; a program needn't handle non-finite values.
Results may differ from the reference program's by a relative error of at most 0.02.
Values may be sent and summed in bfloat16 or wider, within the bound.
No kernel may reach another device: no remote copies, remote signals or barrier semaphores. Data moves between devices by JAX's collectives and lax.ppermute only.
A program may use at most 448 MiB of HBM per device.

```python
import math
import jax
import jax.numpy as jnp
from jax import lax

MODEL_WIDTH = 1024
FF = 2048
MAMBA_HEADS = 24
MAMBA_HEAD_SIZE = 64
STATE_SIZE = 128
CONV = 4
QUERY_HEADS = 8
KEY_VALUE_HEADS = 2
HEAD_SIZE = 64
TOK_DEV = 512
NDOCS = 6
BLOCK_TOKENS = 256
LENGTH = 4096
STREAMS = 4
MAMBA_INNER = 1536
CH = 1792


def decay_plan(key, slow_share):
    subkeys = jax.random.split(key, 4)
    base_dt = jnp.exp(jax.random.uniform(subkeys[0], (MAMBA_HEADS,), jnp.float32, jnp.log(0.01), jnp.log(0.1)))
    slow_heads = jax.random.uniform(subkeys[1], (MAMBA_HEADS,), jnp.float32) < slow_share
    slow_rate = jnp.exp(jax.random.uniform(subkeys[2], (MAMBA_HEADS,), jnp.float32, jnp.log(0.2 / LENGTH), jnp.log(1.0 / LENGTH)))
    fast_rate = jnp.exp(jax.random.uniform(subkeys[3], (MAMBA_HEADS,), jnp.float32, jnp.log(1.0 / 50.0), jnp.log(1.0 / 30.0)))
    return (base_dt, jnp.where(slow_heads, slow_rate, fast_rate))


def draw_dt_bias(key, part):
    base_dt, _ = decay_plan(key, 0.5)
    return jnp.log(jnp.expm1(base_dt)).astype(jnp.bfloat16)


def draw_a_log(key, part):
    share = 0.5
    base_dt, rates = decay_plan(key, share)
    return jnp.log(rates / base_dt).astype(jnp.bfloat16)


def draw_doc_starts(key, part):
    key = jax.random.fold_in(key, 7)

    def one_stream(stream_key):
        subkeys = jax.random.split(stream_key, 2)
        first_cut = jax.random.randint(subkeys[0], (1,), TOK_DEV // 4, 3 * TOK_DEV // 4 + 1)
        middle = jnp.sort(jax.random.permutation(subkeys[1], TOK_DEV - 3)[:NDOCS - 4]) + (LENGTH - TOK_DEV + 2)
        return jnp.concatenate([jnp.zeros((1,), jnp.int32), first_cut.astype(jnp.int32), jnp.full((1,), LENGTH - TOK_DEV + 1, jnp.int32), middle.astype(jnp.int32), jnp.full((1,), LENGTH - 1, jnp.int32)])
    return jax.vmap(one_stream)(jax.random.split(key, STREAMS))


def block_levels(own_key, extent, shards, least, top_value):
    level, own = 1.0, jax.random.fold_in(own_key, 6)
    for axis_at, blocks in shards:
        draws = jnp.exp(jax.random.uniform(jax.random.fold_in(own, axis_at), (blocks,), jnp.float32, least / len(shards), top_value / len(shards)))
        level = level * jnp.repeat(draws, extent[axis_at] // blocks).reshape([-1 if axis == axis_at else 1 for axis in range(len(extent))])
    return level


def bell_draw(rng, dims, width, most, shards=(), held_as=jnp.bfloat16):
    values = jax.random.normal(rng, dims, jnp.float32) * width
    if len(shards) > 0:
        values = block_levels(rng, dims, shards, -0.22, 0.18) * values
    return jnp.clip(values, min=-most, max=most).astype(held_as)


def setup_inputs(seed: int = 0) -> dict:
    streams_of = jax.random.split(jax.random.key(seed), 21)
    return {
        "tokens": bell_draw(streams_of[0], (STREAMS, LENGTH, MODEL_WIDTH), 1.0, 6.0, ((0, 4), (1, 8))),
        "cotangent": bell_draw(streams_of[1], (STREAMS, LENGTH, MODEL_WIDTH), 1.0, 6.0, ((0, 4), (1, 8))),
        "doc_starts": draw_doc_starts(jax.random.fold_in(streams_of[20], 71), 0),
        "gain_mix": jnp.clip(1.0 + 0.18 * jax.random.normal(streams_of[3], (MODEL_WIDTH,), jnp.float32), 0.099609375, 1.8984375).astype(jnp.bfloat16),
        "w_z": bell_draw(streams_of[4], (MODEL_WIDTH, MAMBA_INNER), MODEL_WIDTH ** -0.5, 0.1875, ((0, 4),)),
        "w_xbc": bell_draw(streams_of[5], (MODEL_WIDTH, CH), MODEL_WIDTH ** -0.5, 0.1875, ((0, 4),)),
        "w_dt": bell_draw(streams_of[6], (MODEL_WIDTH, MAMBA_HEADS), MODEL_WIDTH ** -0.5, 0.1875, ((0, 4),)),
        "conv_w": bell_draw(streams_of[7], (CONV, CH), CONV ** -0.5, 3.0, ((1, 4),)),
        "conv_b": bell_draw(streams_of[8], (CH,), 0.3, 2.0, ((0, 4),)),
        "dt_bias": draw_dt_bias(jax.random.fold_in(streams_of[20], 71), 0),
        "a_log": draw_a_log(jax.random.fold_in(streams_of[20], 71), 0),
        "skip_factor": jnp.clip(0.5 + 1.0 * jax.random.uniform(streams_of[11], (MAMBA_HEADS,), jnp.float32) ** block_levels(streams_of[11], (MAMBA_HEADS,), ((0, 4),), -0.2, 0.2), 0.5, 1.5).astype(jnp.bfloat16),
        "w_mo": bell_draw(streams_of[12], (MAMBA_INNER, MODEL_WIDTH), MAMBA_INNER ** -0.5, 0.15625, ((0, 4),)),
        "w_q": bell_draw(streams_of[13], (MODEL_WIDTH, QUERY_HEADS * HEAD_SIZE), MODEL_WIDTH ** -0.5, 0.1875, ((0, 4),)),
        "key_value_weight": bell_draw(streams_of[14], (MODEL_WIDTH, 2 * KEY_VALUE_HEADS * HEAD_SIZE), MODEL_WIDTH ** -0.5, 0.1875, ((0, 4),)),
        "w_o": bell_draw(streams_of[15], (QUERY_HEADS * HEAD_SIZE, MODEL_WIDTH), (QUERY_HEADS * HEAD_SIZE // 64) ** -0.5, 2.0, ((0, 4),)),
        "gain_ffn": jnp.clip(1.0 + 0.18 * jax.random.normal(streams_of[16], (MODEL_WIDTH,), jnp.float32), 0.099609375, 1.8984375).astype(jnp.bfloat16),
        "w_gate": bell_draw(streams_of[17], (MODEL_WIDTH, FF), MODEL_WIDTH ** -0.5, 0.1875, ((0, 4),)),
        "w_up": bell_draw(streams_of[18], (MODEL_WIDTH, FF), MODEL_WIDTH ** -0.5, 0.1875, ((0, 4),)),
        "w_down": bell_draw(streams_of[19], (FF, MODEL_WIDTH), FF ** -0.5, 0.125, ((0, 4),)),
    }


@jax.custom_vjp
def low(v):
    return lax.optimization_barrier(v.astype(jnp.bfloat16)).astype(jnp.float32)

@jax.custom_vjp
def low_back(v):
    return v

def low_keep(v):
    return (low(v), None)

def low_pass(kept, grad):
    return (grad,)

def back_keep(v):
    return (v, None)

def back_low(kept, grad):
    return (low(grad),)
low.defvjp(low_keep, low_pass)
low_back.defvjp(back_keep, back_low)
EPSILON = 1e-06
ROPE_BASE = 10000.0
MASK_FILLER = -1e+30
FORGET = -10000.0
HIGHEST = lax.Precision.HIGHEST

def highest(left, right):
    return jnp.dot(left, right, precision=HIGHEST)

def rms_scale(value_matrix):
    return lax.rsqrt(lax.optimization_barrier(jnp.mean(value_matrix * value_matrix, axis=-1, keepdims=True)) + EPSILON)

def segment_of(token_positions, starts):
    counted = lax.optimization_barrier(jnp.sum((starts[None, :] <= token_positions[:, None]).astype(jnp.int32), axis=1))
    return counted.astype(jnp.int32) - jnp.int32(1)

def apply_rotary(value_matrix, token_positions, turn):
    half = value_matrix.shape[-1] // 2
    freqs = ROPE_BASE ** (-2.0 * jnp.arange(half, dtype=jnp.float32) / value_matrix.shape[-1])
    angles = token_positions.astype(jnp.float32)[:, None] * freqs[None, :]
    cosine = jnp.cos(angles)[:, None, :]
    sine = turn * jnp.sin(angles)[:, None, :]
    former = value_matrix[..., :half]
    latter = value_matrix[..., half:]
    return jnp.concatenate([former * cosine - latter * sine, latter * cosine + former * sine], axis=-1)

def conv_mix(padded, seg_pad, document_segments, conv_w, conv_b):
    token_count = document_segments.shape[0]
    summed = jnp.zeros((token_count, padded.shape[1]), jnp.float32) + conv_b[None, :]
    for offset in range(CONV):
        agree = (seg_pad[offset:offset + token_count] == document_segments).astype(jnp.float32)
        summed = summed + conv_w[offset][None, :] * padded[offset:offset + token_count] * agree[:, None]
    return summed

def span_step(running, slices):
    state, seg_before = running
    input_weights_x, input_weights_b, input_weights_c, step_interval, decay_logarithm, document_segments = slices
    cumul = jnp.cumsum(decay_logarithm, axis=0)
    order = jnp.arange(document_segments.shape[0])
    visible = (document_segments[:, None] == document_segments[None, :]) & (order[:, None] >= order[None, :])
    spread = jnp.where(visible[:, :, None], cumul[:, None, :] - cumul[None, :, :], FORGET)
    couple = jnp.dot(input_weights_c, input_weights_b.T, precision=HIGHEST)
    mixing = couple[:, :, None] * jnp.exp(spread) * step_interval[None, :, :]
    layer_outputs = jnp.einsum('tsh,shp->thp', mixing, input_weights_x, precision=HIGHEST)
    carried = (document_segments == seg_before).astype(jnp.float32)
    layer_outputs = layer_outputs + jnp.einsum('tn,hpn->thp', input_weights_c, state, precision=HIGHEST) * (jnp.exp(cumul) * carried[:, None])[:, :, None]
    seg_end = document_segments[-1].astype(jnp.int32)
    ending = jnp.exp(cumul[-1][None, :] - cumul) * step_interval * (document_segments == seg_end).astype(jnp.float32)[:, None]
    keep_end = jnp.exp(cumul[-1]) * (seg_end == seg_before).astype(jnp.float32)
    fresh = jnp.einsum('sh,shp,sn->hpn', ending, input_weights_x, input_weights_b, precision=HIGHEST)
    return ((fresh + state * keep_end[:, None, None], seg_end), layer_outputs)

def mamba_branch(normed, document_segments, w_z, w_xbc, w_dt, conv_w, conv_b, dt_bias, a_log, skip_factor, w_mo):
    token_count = normed.shape[0]
    gate_z = low_back(highest(normed, w_z))
    mixed_in = low(low_back(highest(normed, w_xbc)))
    dt_raw = low_back(highest(normed, w_dt))
    padded = jnp.concatenate([jnp.zeros((CONV - 1, mixed_in.shape[1]), mixed_in.dtype), mixed_in], axis=0)
    seg_pad = jnp.concatenate([jnp.full((CONV - 1,), -1, jnp.int32), document_segments.astype(jnp.int32)])
    activation_value = jax.nn.silu(conv_mix(padded, seg_pad, document_segments, conv_w, conv_b))
    input_weights_x = activation_value[:, :MAMBA_INNER].reshape(token_count, MAMBA_HEADS, MAMBA_HEAD_SIZE)
    input_weights_b = activation_value[:, MAMBA_INNER:MAMBA_INNER + STATE_SIZE]
    input_weights_c = activation_value[:, MAMBA_INNER + STATE_SIZE:]
    step_interval = jax.nn.softplus(dt_raw + dt_bias[None, :])
    decay_logarithm = -step_interval * jnp.exp(a_log)[None, :]
    count_of_blocks = token_count // BLOCK_TOKENS
    piece_list = (input_weights_x.reshape(count_of_blocks, BLOCK_TOKENS, MAMBA_HEADS, MAMBA_HEAD_SIZE), input_weights_b.reshape(count_of_blocks, BLOCK_TOKENS, STATE_SIZE), input_weights_c.reshape(count_of_blocks, BLOCK_TOKENS, STATE_SIZE), step_interval.reshape(count_of_blocks, BLOCK_TOKENS, MAMBA_HEADS), decay_logarithm.reshape(count_of_blocks, BLOCK_TOKENS, MAMBA_HEADS), document_segments.reshape(count_of_blocks, BLOCK_TOKENS))
    initial_state = jnp.zeros((MAMBA_HEADS, MAMBA_HEAD_SIZE, STATE_SIZE), normed.dtype)
    _, layer_outputs = lax.scan(jax.checkpoint(span_step), (initial_state, jnp.int32(-1)), piece_list)
    layer_outputs = layer_outputs.reshape(token_count, MAMBA_HEADS, MAMBA_HEAD_SIZE) + skip_factor[None, :, None] * input_weights_x
    gated = low(layer_outputs.reshape(token_count, MAMBA_INNER) * jax.nn.silu(gate_z))
    return low_back(highest(gated, w_mo))

def attention_branch(normed, token_positions, document_segments, w_q, key_value_weight, w_o):
    token_count = normed.shape[0]
    query_group = QUERY_HEADS // KEY_VALUE_HEADS
    key_value_width = KEY_VALUE_HEADS * HEAD_SIZE
    scale_q = 1.0 / math.sqrt(HEAD_SIZE)
    query_matrix = low(apply_rotary(low_back(highest(normed, w_q)).reshape(token_count, QUERY_HEADS, HEAD_SIZE), token_positions, 1.0))
    key_value_pairs = low_back(highest(normed, key_value_weight))
    heads_of_keys = low(apply_rotary(key_value_pairs[:, :key_value_width].reshape(token_count, KEY_VALUE_HEADS, HEAD_SIZE), token_positions, 1.0))
    value_matrix = low(key_value_pairs[:, key_value_width:]).reshape(token_count, KEY_VALUE_HEADS, HEAD_SIZE)
    rows_of_queries = min(512, token_count)
    count_of_blocks = token_count // rows_of_queries
    blocks_of_queries = query_matrix.reshape(count_of_blocks, rows_of_queries, KEY_VALUE_HEADS, query_group, HEAD_SIZE)

    def one_block(slices):
        query_block, query_pos, query_seg = slices
        scores = low_back(jnp.einsum('tjgd,cjd->jgtc', query_block, heads_of_keys, precision=HIGHEST) * scale_q)
        visible = (query_seg[:, None] == document_segments[None, :]) & (query_pos[:, None] >= token_positions[None, :])
        scores = jnp.where(visible[None, None], scores, MASK_FILLER)
        log_total = jax.nn.logsumexp(scores, axis=-1, keepdims=True)
        attn_prob = low(jnp.exp(scores - log_total))
        return jnp.einsum('jgtc,cjd->tjgd', attn_prob, value_matrix, precision=HIGHEST)
    mixed = lax.map(jax.checkpoint(one_block), (blocks_of_queries, token_positions.reshape(count_of_blocks, rows_of_queries), document_segments.reshape(count_of_blocks, rows_of_queries)))
    attn_vec = low(low_back(mixed.reshape(token_count, QUERY_HEADS * HEAD_SIZE)))
    return low_back(highest(attn_vec, w_o))

def layer(tokens_row, document_segments, token_positions, params):
    gain_mix, w_z, w_xbc, w_dt, conv_w, conv_b, dt_bias, a_log, skip_factor, w_mo, w_q, key_value_weight, w_o, gain_ffn, w_gate, w_up, w_down = params
    normed = low(tokens_row * rms_scale(tokens_row) * gain_mix[None, :])
    hidden = tokens_row + attention_branch(normed, token_positions, document_segments, w_q, key_value_weight, w_o)
    hidden = hidden + mamba_branch(normed, document_segments, w_z, w_xbc, w_dt, conv_w, conv_b, dt_bias, a_log, skip_factor, w_mo)
    normed_ffn = low(hidden * rms_scale(hidden) * gain_ffn[None, :])
    gate = low_back(highest(normed_ffn, w_gate))
    upper = low_back(highest(normed_ffn, w_up))
    activation_value = low(jax.nn.silu(gate) * upper)
    return hidden + highest(activation_value, w_down)

def reference(tokens, cotangent, doc_starts, gain_mix, w_z, w_xbc, w_dt, conv_w, conv_b, dt_bias, a_log, skip_factor, w_mo, w_q, key_value_weight, w_o, gain_ffn, w_gate, w_up, w_down):
    params = tuple((weight_arr.astype(jnp.float32) for weight_arr in (gain_mix, w_z, w_xbc, w_dt, conv_w, conv_b, dt_bias, a_log, skip_factor, w_mo, w_q, key_value_weight, w_o, gain_ffn, w_gate, w_up, w_down)))
    token_positions = jnp.arange(LENGTH, dtype=jnp.int32)
    document_segments = jax.vmap(lambda starts: segment_of(token_positions, starts.astype(jnp.int32)))(doc_starts)

    def forward(inputs, *weights):
        return lax.map(lambda slices: layer(slices[0], slices[1], token_positions, weights), (inputs, document_segments))
    result, pullback = jax.vjp(forward, tokens.astype(jnp.float32), *params)
    grads = pullback(cotangent.astype(jnp.float32))
    return (result.astype(jnp.bfloat16), grads[0], grads[1], grads[2], grads[3], grads[4], grads[5], grads[6], grads[7], grads[8], grads[9], grads[10], grads[11], grads[12], grads[13], grads[14], grads[15], grads[16], grads[17])
```

```python
import functools
import math

import jax
import jax.numpy as jnp
from jax import lax
from jax.experimental import pallas as pl
from jax.experimental.pallas import tpu as pltpu
from jax.sharding import PartitionSpec as P

MAMBA_HEADS = 24
MAMBA_HEAD_SIZE = 64
STATE_SIZE = 128
CONV = 4
QUERY_HEADS = 8
KEY_VALUE_HEADS = 2
HEAD_SIZE = 64
MAMBA_INNER = MAMBA_HEADS * MAMBA_HEAD_SIZE
CHANNELS = MAMBA_INNER + 2 * STATE_SIZE
LANES = 128
PAIRS = MAMBA_INNER // LANES
CHUNK = 128
KEY_BLOCK = 512
QUERY_TILE = 128
GROUP = QUERY_HEADS // KEY_VALUE_HEADS
MESSAGE_ROWS = STATE_SIZE + 16
VMEM_LIMIT = 56 * 1024 * 1024

EPSILON = 1e-06
ROPE_BASE = 10000.0
MASK_FILLER = -1e30
HIGHEST = lax.Precision.HIGHEST
F32 = jnp.float32
BF16 = jnp.bfloat16


def dot_nn(a, b, precision=None):
    return lax.dot_general(
        a, b, (((1,), (0,)), ((), ())), precision=precision, preferred_element_type=F32
    )


def dot_nt(a, b):
    return lax.dot_general(a, b, (((1,), (1,)), ((), ())), preferred_element_type=F32)


def dot_tn(a, b):
    return lax.dot_general(a, b, (((0,), (0,)), ((), ())), preferred_element_type=F32)


def iota(shape, dim):
    return lax.broadcasted_iota(jnp.int32, shape, dim)


def params(*semantics):
    return pltpu.CompilerParams(dimension_semantics=semantics, vmem_limit_bytes=VMEM_LIMIT)


def whole(shape):
    return pl.BlockSpec(shape, lambda *_: (0,) * len(shape))


def low_half(rows):
    return iota((rows, LANES), 1) < MAMBA_HEAD_SIZE


def spread(values, pair, low):
    a = values[:, 2 * pair : 2 * pair + 1]
    b = values[:, 2 * pair + 1 : 2 * pair + 2]
    return jnp.where(low, a, b)


def tile(i):
    return slice(i * LANES, (i + 1) * LANES)


def split_pair(x, low):
    zero = jnp.zeros_like(x)
    return jnp.concatenate([jnp.where(low, x, zero), jnp.where(low, zero, x)], axis=0)


def fill_padded(xs_ref, edge_ref, mixed_ref):
    xs_ref[0:8, :] = edge_ref[...]
    xs_ref[8:, :] = mixed_ref[...].astype(F32)


def lag_masks(positions, doc):
    return [None] + [(positions - lag >= doc).astype(F32) for lag in range(1, CONV)]


def conv_tile(xs_ref, start, i, cw_ref, masks):
    window = xs_ref[pl.ds(start, CHUNK + 8), tile(i)]
    summed = cw_ref[4:5, tile(i)] + cw_ref[3:4, tile(i)] * window[8 : 8 + CHUNK]
    for lag in range(1, CONV):
        shifted = window[8 - lag : 8 - lag + CHUNK]
        summed = summed + cw_ref[3 - lag : 4 - lag, tile(i)] * (shifted * masks[lag])
    return summed


def softplus(v):
    return jnp.maximum(v, 0.0) + jnp.log1p(jnp.exp(-jnp.abs(v)))


def decay_sums(dt_ref, hp_ref):
    raw = dt_ref[...] + hp_ref[0:1, :]
    step = softplus(raw)
    log_decay = step * hp_ref[1:2, :]
    order = iota((CHUNK, CHUNK), 0) >= iota((CHUNK, CHUNK), 1)
    cumul = dot_nn(order.astype(F32), log_decay, HIGHEST)
    return raw, step, log_decay, cumul


def mamba_forward_kernel(
    sc_ref,
    edge_ref,
    mixed_ref,
    dt_ref,
    doc_ref,
    cw_ref,
    hp_ref,
    skip_ref,
    y_ref,
    sin_ref,
    msg_ref,
    dec_ref,
    c_ref,
    xs_ref,
    xa_ref,
    state_ref,
    carry_ref,
):
    c = pl.program_id(0)
    count = pl.num_programs(0)

    @pl.when(c == 0)
    def _():
        fill_padded(xs_ref, edge_ref, mixed_ref)
        state_ref[...] = jnp.zeros_like(state_ref)
        carry_ref[...] = jnp.zeros_like(carry_ref)

    base = sc_ref[count]
    start = pl.multiple_of(c * CHUNK, CHUNK)
    first = base + start
    end_doc = sc_ref[c]
    doc = doc_ref[...]
    positions = first + iota((CHUNK, 1), 0)
    masks = lag_masks(positions, doc)
    for i in range(CHANNELS // LANES):
        summed = conv_tile(xs_ref, start, i, cw_ref, masks)
        xa_ref[:, tile(i)] = summed * jax.nn.sigmoid(summed)
    _, step, log_decay, cumul = decay_sums(dt_ref, hp_ref)
    cumul_t = cumul.T
    b_mat = xa_ref[:, tile(PAIRS)]
    c_mat = xa_ref[:, tile(PAIRS + 1)].astype(BF16)
    c_ref[...] = c_mat
    couple = dot_nt(c_mat, b_mat.astype(BF16))
    b_turned = b_mat.T.astype(BF16)
    col = first + iota((CHUNK, CHUNK), 1)
    row = first + iota((CHUNK, CHUNK), 0)
    couple = jnp.where((col <= row) & (col >= doc), couple, 0.0)
    carried = (doc < first).astype(F32)
    into = jnp.exp(cumul) * carried
    last = cumul[CHUNK - 1 : CHUNK, :]
    ending = jnp.exp(last - cumul) * (positions >= end_doc).astype(F32)
    keep = jnp.exp(last) * (end_doc < first).astype(F32)
    dec_ref[...] = jnp.where(doc < base, jnp.exp(cumul + carry_ref[0:1, :]), 0.0)
    low = low_half(CHUNK)
    low_row = low_half(1)
    for j in range(PAIRS):
        x = xa_ref[:, tile(j)]
        weighted = x * spread(step, j, low)
        mixing = []
        for h in (2 * j, 2 * j + 1):
            gap = jnp.minimum(cumul[:, h : h + 1] - cumul_t[h : h + 1, :], 0.0)
            mixing.append((couple * jnp.exp(gap)).astype(BF16))
        y = dot_nn(jnp.concatenate(mixing, axis=1), split_pair(weighted.astype(BF16), low))
        state = state_ref[:, tile(j)]
        sin_ref[0, :, tile(j)] = state
        y = y + dot_nn(c_mat, state.astype(BF16)) * spread(into, j, low)
        y_ref[:, tile(j)] = y + skip_ref[0:1, tile(j)] * x
        fresh = dot_nn(b_turned, (weighted * spread(ending, j, low)).astype(BF16))
        state_ref[:, tile(j)] = fresh + state * spread(keep, j, low_row)
    carry_ref[...] = carry_ref[...] + last

    @pl.when(c == count - 1)
    def _():
        msg_ref[0:STATE_SIZE, :] = state_ref[...].astype(BF16)
        through = jnp.exp(carry_ref[...]) * (end_doc < base).astype(F32)
        low8 = low_half(8)
        for j in range(PAIRS):
            wide = spread(through, j, low8)
            msg_ref[STATE_SIZE:, tile(j)] = jnp.concatenate([wide, wide], axis=0).astype(BF16)


def mamba_forward(scalars, edge, mixed, dt_raw, doc, conv_pack, head_pack, skip_wide):
    rows = mixed.shape[0]
    count = rows // CHUNK
    by_chunk = lambda width: pl.BlockSpec((CHUNK, width), lambda c: (c, 0))
    return pl.pallas_call(
        mamba_forward_kernel,
        grid=(count,),
        in_specs=[
            pl.BlockSpec(memory_space=pltpu.SMEM),
            whole((8, CHANNELS)),
            whole((rows, CHANNELS)),
            by_chunk(LANES),
            by_chunk(1),
            whole((8, CHANNELS)),
            whole((8, LANES)),
            whole((1, MAMBA_INNER)),
        ],
        out_specs=[
            by_chunk(MAMBA_INNER),
            pl.BlockSpec((1, STATE_SIZE, MAMBA_INNER), lambda c: (c, 0, 0)),
            whole((MESSAGE_ROWS, MAMBA_INNER)),
            by_chunk(LANES),
            by_chunk(LANES),
        ],
        out_shape=[
            jax.ShapeDtypeStruct((rows, MAMBA_INNER), F32),
            jax.ShapeDtypeStruct((count, STATE_SIZE, MAMBA_INNER), F32),
            jax.ShapeDtypeStruct((MESSAGE_ROWS, MAMBA_INNER), BF16),
            jax.ShapeDtypeStruct((rows, LANES), F32),
            jax.ShapeDtypeStruct((rows, LANES), BF16),
        ],
        scratch_shapes=[
            pltpu.VMEM((rows + 8, CHANNELS), F32),
            pltpu.VMEM((CHUNK, CHANNELS), F32),
            pltpu.VMEM((STATE_SIZE, MAMBA_INNER), F32),
            pltpu.VMEM((8, LANES), F32),
        ],
        compiler_params=params("arbitrary"),
        cost_estimate=pl.CostEstimate(
            flops=rows * MAMBA_INNER * 1024, bytes_accessed=rows * 12000, transcendentals=rows * 4096
        ),
        name="mamba_forward",
    )(scalars, edge, mixed, dt_raw, doc, conv_pack, head_pack, skip_wide)


def mamba_correct_kernel(
    y_ref, sin_ref, c_ref, dec_ref, state_ref, z_ref, total_ref, gated_ref, true_ref, edge_ref
):
    c = pl.program_id(0)

    @pl.when(c == 0)
    def _():
        edge_ref[...] = jnp.ones_like(edge_ref)

    low = low_half(CHUNK)
    low_row = low_half(1)
    decay = dec_ref[...]
    before = edge_ref[0:1, :]
    c_mat = c_ref[...]
    for j in range(PAIRS):
        state = state_ref[:, tile(j)]
        y = y_ref[:, tile(j)] + dot_nn(c_mat, state.astype(BF16)) * spread(decay, j, low)
        total_ref[:, tile(j)] = y
        z = z_ref[:, tile(j)]
        gated_ref[:, tile(j)] = (y * (z * jax.nn.sigmoid(z))).astype(BF16)
        true_ref[0, :, tile(j)] = (
            sin_ref[0, :, tile(j)] + state * spread(before, j, low_row)
        ).astype(BF16)
    edge_ref[0:1, :] = decay[CHUNK - 1 : CHUNK, :]


def mamba_correct(y, sin, c_mat, decay, state_in, gate_z):
    rows = y.shape[0]
    count = rows // CHUNK
    by_chunk = lambda width: pl.BlockSpec((CHUNK, width), lambda c: (c, 0))
    states = pl.BlockSpec((1, STATE_SIZE, MAMBA_INNER), lambda c: (c, 0, 0))
    return pl.pallas_call(
        mamba_correct_kernel,
        grid=(count,),
        in_specs=[
            by_chunk(MAMBA_INNER),
            states,
            by_chunk(LANES),
            by_chunk(LANES),
            whole((STATE_SIZE, MAMBA_INNER)),
            by_chunk(MAMBA_INNER),
        ],
        out_specs=[by_chunk(MAMBA_INNER), by_chunk(MAMBA_INNER), states],
        out_shape=[
            jax.ShapeDtypeStruct((rows, MAMBA_INNER), F32),
            jax.ShapeDtypeStruct((rows, MAMBA_INNER), BF16),
            jax.ShapeDtypeStruct((count, STATE_SIZE, MAMBA_INNER), BF16),
        ],
        scratch_shapes=[pltpu.VMEM((8, LANES), F32)],
        compiler_params=params("arbitrary"),
        cost_estimate=pl.CostEstimate(
            flops=rows * MAMBA_INNER * 256, bytes_accessed=rows * 30000, transcendentals=rows * 1536
        ),
        name="mamba_correct",
    )(y, sin, c_mat, decay, state_in, gate_z)


def mamba_gate_back_kernel(
    gg_ref, z_ref, y_ref, c_ref, dec_ref, dy_ref, gz_ref, gsi_ref, acc_ref
):
    c = pl.program_id(0)

    @pl.when(c == 0)
    def _():
        acc_ref[...] = jnp.zeros_like(acc_ref)

    low = low_half(CHUNK)
    decay = dec_ref[...]
    c_turned = c_ref[...].astype(F32).T.astype(BF16)
    for j in range(PAIRS):
        z = z_ref[:, tile(j)]
        sig = jax.nn.sigmoid(z)
        silu = z * sig
        grad = gg_ref[:, tile(j)]
        gz_ref[:, tile(j)] = (grad * y_ref[:, tile(j)] * (sig + silu * (1.0 - sig))).astype(BF16)
        dy = (grad * silu).astype(BF16)
        dy_ref[:, tile(j)] = dy
        scaled = (dy.astype(F32) * spread(decay, j, low)).astype(BF16)
        acc_ref[:, tile(j)] += dot_nn(c_turned, scaled)

    @pl.when(c == pl.num_programs(0) - 1)
    def _():
        gsi_ref[...] = acc_ref[...].astype(BF16)


def mamba_gate_back(gated_grad, gate_z, total, c_mat, decay):
    rows = total.shape[0]
    by_chunk = lambda width: pl.BlockSpec((CHUNK, width), lambda c: (c, 0))
    return pl.pallas_call(
        mamba_gate_back_kernel,
        grid=(rows // CHUNK,),
        in_specs=[
            by_chunk(MAMBA_INNER),
            by_chunk(MAMBA_INNER),
            by_chunk(MAMBA_INNER),
            by_chunk(LANES),
            by_chunk(LANES),
        ],
        out_specs=[by_chunk(MAMBA_INNER), by_chunk(MAMBA_INNER), whole((STATE_SIZE, MAMBA_INNER))],
        out_shape=[
            jax.ShapeDtypeStruct((rows, MAMBA_INNER), BF16),
            jax.ShapeDtypeStruct((rows, MAMBA_INNER), BF16),
            jax.ShapeDtypeStruct((STATE_SIZE, MAMBA_INNER), BF16),
        ],
        scratch_shapes=[pltpu.VMEM((STATE_SIZE, MAMBA_INNER), F32)],
        compiler_params=params("arbitrary"),
        cost_estimate=pl.CostEstimate(
            flops=rows * MAMBA_INNER * 256, bytes_accessed=rows * 25000, transcendentals=rows * 1536
        ),
        name="mamba_gate_back",
    )(gated_grad, gate_z, total, c_mat, decay)


def picks(pair):
    channel = iota((LANES, LANES), 0)
    head = iota((LANES, LANES), 1)
    return (head == 2 * pair + channel // MAMBA_HEAD_SIZE).astype(BF16)


def head_sums(product, select):
    high = product.astype(BF16)
    rest = (product - high.astype(F32)).astype(BF16)
    return dot_nn(high, select) + dot_nn(rest, select)


def mamba_back_kernel(
    sc_ref,
    edge_ref,
    mixed_ref,
    dt_ref,
    doc_ref,
    doc_row_ref,
    cw_ref,
    hp_ref,
    skip_ref,
    dy_ref,
    y_ref,
    sin_ref,
    ds_end_ref,
    gmix_ref,
    tail_ref,
    edge_grad_ref,
    gdt_ref,
    gconv_ref,
    ghead_ref,
    xs_ref,
    xa_ref,
    slope_ref,
    grad_ref,
    ds_ref,
    rows_ref,
):
    step_at = pl.program_id(0)
    count = pl.num_programs(0)
    c = count - 1 - step_at
    rows = count * CHUNK

    @pl.when(step_at == 0)
    def _():
        fill_padded(xs_ref, edge_ref, mixed_ref)
        ds_ref[...] = ds_end_ref[...]
        grad_ref[pl.ds(rows, 8), :] = jnp.zeros((8, CHANNELS), F32)
        gconv_ref[...] = jnp.zeros_like(gconv_ref)
        ghead_ref[...] = jnp.zeros_like(ghead_ref)
        rows_ref[...] = jnp.zeros_like(rows_ref)

    base = sc_ref[count]
    start = pl.multiple_of(c * CHUNK, CHUNK)
    first = base + start
    end_doc = sc_ref[c]
    doc_window = doc_ref[pl.ds(start, CHUNK + 8), :]
    doc = doc_window[0:CHUNK]
    positions_window = first + iota((CHUNK + 8, 1), 0)
    positions = positions_window[0:CHUNK]
    masks_window = lag_masks(positions_window, doc_window)
    masks = [None] + [m[0:CHUNK] for m in masks_window[1:]]
    for i in range(CHANNELS // LANES):
        summed = conv_tile(xs_ref, start, i, cw_ref, masks)
        sig = jax.nn.sigmoid(summed)
        act = summed * sig
        xa_ref[:, tile(i)] = act
        slope_ref[:, tile(i)] = sig + act * (1.0 - sig)
    raw, step, log_decay, cumul = decay_sums(dt_ref, hp_ref)
    cumul_t = cumul.T
    b_mat = xa_ref[:, tile(PAIRS)].astype(BF16)
    c_f32 = xa_ref[:, tile(PAIRS + 1)]
    c_mat = c_f32.astype(BF16)
    c_turned = c_f32.T.astype(BF16)
    key = first + iota((CHUNK, CHUNK), 0)
    query = first + iota((CHUNK, CHUNK), 1)
    visible = (key <= query) & (key >= doc_row_ref[0:1, :])
    couple = jnp.where(visible, dot_nt(b_mat, c_mat), 0.0)
    carried = (doc < first).astype(F32)
    into = jnp.exp(cumul) * carried
    last = cumul[CHUNK - 1 : CHUNK, :]
    ending = jnp.exp(last - cumul) * (positions >= end_doc).astype(F32)
    keep = jnp.exp(last) * (end_doc < first).astype(F32)
    low = low_half(CHUNK)
    low_row = low_half(1)
    grad_couple = jnp.zeros((CHUNK, CHUNK), F32)
    grad_b = jnp.zeros((CHUNK, STATE_SIZE), F32)
    grad_c = jnp.zeros((CHUNK, STATE_SIZE), F32)
    grad_cumul = jnp.zeros((CHUNK, LANES), F32)
    grad_step = jnp.zeros((CHUNK, LANES), F32)
    end_sums = jnp.zeros((8, LANES), F32)
    for j in range(PAIRS):
        select = picks(j)
        x = xa_ref[:, tile(j)]
        step_wide = spread(step, j, low)
        weighted = x * step_wide
        weighted_b = weighted.astype(BF16)
        dy = dy_ref[:, tile(j)]
        dy_f32 = dy.astype(F32)
        grad_mixing = dot_nt(split_pair(weighted_b, low), dy)
        mixing = []
        for side, h in enumerate((2 * j, 2 * j + 1)):
            gap = jnp.minimum(cumul_t[h : h + 1, :] - cumul[:, h : h + 1], 0.0)
            fade = jnp.exp(gap)
            mixing.append((couple * fade).astype(BF16))
            grad_couple += grad_mixing[side * CHUNK : (side + 1) * CHUNK] * fade
        grad_weighted = dot_nn(jnp.concatenate(mixing, axis=1), split_pair(dy, low))
        ending_wide = spread(ending, j, low)
        grad_state = ds_ref[:, tile(j)]
        grad_state_b = grad_state.astype(BF16)
        state = sin_ref[0, :, tile(j)]
        through_state = ending_wide * dot_nn(b_mat, grad_state_b)
        grad_weighted = grad_weighted + through_state
        dy_into = (dy_f32 * spread(into, j, low)).astype(BF16)
        grad_c += dot_nt(dy_into, state)
        grad_b += dot_nt((weighted * ending_wide).astype(BF16), grad_state_b)
        keep_wide = spread(keep, j, low_row)
        weighted_f32 = weighted_b.astype(F32)
        to_end = jnp.sum(weighted_f32 * through_state, axis=0, keepdims=True) + keep_wide * jnp.sum(
            grad_state * state.astype(F32), axis=0, keepdims=True
        )
        ds_ref[:, tile(j)] = keep_wide * grad_state + dot_nn(c_turned, dy_into)
        skip = skip_ref[0:1, tile(j)]
        grad_x = step_wide * grad_weighted + skip * dy_f32
        grad_ref[pl.ds(start, CHUNK), tile(j)] = grad_x * slope_ref[:, tile(j)]
        rows_ref[0:1, tile(j)] += jnp.sum(dy_f32 * x, axis=0, keepdims=True)
        in_out = dy_f32 * (y_ref[:, tile(j)] - skip * x) - weighted_f32 * grad_weighted
        grad_cumul += head_sums(in_out, select)
        grad_step += head_sums(grad_weighted * x, select)
        end_sums += head_sums(jnp.broadcast_to(to_end, (8, LANES)), select)
    grad_couple = jnp.where(visible, grad_couple, 0.0).astype(BF16)
    grad_b += dot_nn(grad_couple, c_mat)
    grad_c += dot_tn(grad_couple, b_mat)
    grad_ref[pl.ds(start, CHUNK), tile(PAIRS)] = grad_b * slope_ref[:, tile(PAIRS)]
    grad_ref[pl.ds(start, CHUNK), tile(PAIRS + 1)] = grad_c * slope_ref[:, tile(PAIRS + 1)]
    later = (iota((CHUNK, CHUNK), 0) <= iota((CHUNK, CHUNK), 1)).astype(F32)
    grad_log = dot_nn(later, grad_cumul, HIGHEST) + end_sums[0:1, :]
    grad_raw = (grad_step + grad_log * hp_ref[1:2, :]) * jax.nn.sigmoid(raw)
    gdt_ref[...] = grad_raw.astype(BF16)
    ghead_ref[0:1, :] += jnp.sum(grad_raw, axis=0, keepdims=True)
    ghead_ref[1:2, :] += jnp.sum(grad_log * log_decay, axis=0, keepdims=True)
    for i in range(CHANNELS // LANES):
        window = grad_ref[pl.ds(start, CHUNK + 8), tile(i)]
        own = window[0:CHUNK]
        padded = xs_ref[pl.ds(start, CHUNK + 8), tile(i)]
        total = cw_ref[3:4, tile(i)] * own
        gconv_ref[4:5, tile(i)] += jnp.sum(own, axis=0, keepdims=True)
        gconv_ref[3:4, tile(i)] += jnp.sum(own * padded[8 : 8 + CHUNK], axis=0, keepdims=True)
        for lag in range(1, CONV):
            masked = window * masks_window[lag]
            total = total + cw_ref[3 - lag : 4 - lag, tile(i)] * masked[lag : lag + CHUNK]
            gconv_ref[3 - lag : 4 - lag, tile(i)] += jnp.sum(
                masked[0:CHUNK] * padded[8 - lag : 8 - lag + CHUNK], axis=0, keepdims=True
            )
        gmix_ref[:, tile(i)] = total.astype(BF16)

        @pl.when(step_at == 0)
        def _():
            tail_ref[:, tile(i)] = total[CHUNK - 8 :]

        @pl.when(step_at == count - 1)
        def _():
            ahead = jnp.zeros((8, LANES), F32)
            for lag in range(1, CONV):
                head = jnp.concatenate(
                    [jnp.zeros((8, LANES), F32), window[0:8] * masks_window[lag][0:8]], axis=0
                )
                ahead = ahead + cw_ref[3 - lag : 4 - lag, tile(i)] * head[lag : lag + 8]
            edge_grad_ref[:, tile(i)] = ahead

    @pl.when(step_at == count - 1)
    def _():
        total = jnp.zeros((8, LANES), F32)
        for j in range(PAIRS):
            total += head_sums(rows_ref[:, tile(j)], picks(j))
        ghead_ref[2:3, :] = total[0:1, :]


def mamba_back(
    scalars, edge, mixed, dt_raw, doc, doc_row, conv_pack, head_pack, skip_wide, dy, y, sin, ds_end
):
    rows = mixed.shape[0]
    count = rows // CHUNK
    by_chunk = lambda width: pl.BlockSpec((CHUNK, width), lambda i: (count - 1 - i, 0))
    return pl.pallas_call(
        mamba_back_kernel,
        grid=(count,),
        in_specs=[
            pl.BlockSpec(memory_space=pltpu.SMEM),
            whole((8, CHANNELS)),
            whole((rows, CHANNELS)),
            by_chunk(LANES),
            whole((rows + 8, 1)),
            pl.BlockSpec((8, CHUNK), lambda i: (0, count - 1 - i)),
            whole((8, CHANNELS)),
            whole((8, LANES)),
            whole((1, MAMBA_INNER)),
            by_chunk(MAMBA_INNER),
            by_chunk(MAMBA_INNER),
            pl.BlockSpec((1, STATE_SIZE, MAMBA_INNER), lambda i: (count - 1 - i, 0, 0)),
            whole((STATE_SIZE, MAMBA_INNER)),
        ],
        out_specs=[
            by_chunk(CHANNELS),
            whole((8, CHANNELS)),
            whole((8, CHANNELS)),
            by_chunk(LANES),
            whole((8, CHANNELS)),
            whole((8, LANES)),
        ],
        out_shape=[
            jax.ShapeDtypeStruct((rows, CHANNELS), BF16),
            jax.ShapeDtypeStruct((8, CHANNELS), F32),
            jax.ShapeDtypeStruct((8, CHANNELS), F32),
            jax.ShapeDtypeStruct((rows, LANES), BF16),
            jax.ShapeDtypeStruct((8, CHANNELS), F32),
            jax.ShapeDtypeStruct((8, LANES), F32),
        ],
        scratch_shapes=[
            pltpu.VMEM((rows + 8, CHANNELS), F32),
            pltpu.VMEM((CHUNK, CHANNELS), F32),
            pltpu.VMEM((CHUNK, CHANNELS), F32),
            pltpu.VMEM((rows + 8, CHANNELS), F32),
            pltpu.VMEM((STATE_SIZE, MAMBA_INNER), F32),
            pltpu.VMEM((8, MAMBA_INNER), F32),
        ],
        compiler_params=params("arbitrary"),
        cost_estimate=pl.CostEstimate(
            flops=rows * MAMBA_INNER * 3072, bytes_accessed=rows * 20000, transcendentals=rows * 4096
        ),
        name="mamba_back",
    )(scalars, edge, mixed, dt_raw, doc, doc_row, conv_pack, head_pack, skip_wide, dy, y, sin, ds_end)


def half_roll(x):
    return pltpu.roll(x, HEAD_SIZE, 1)


def stack_low(block, rows):
    low = low_half(rows)
    parts = []
    for a in range(2):
        pair = block[:, tile(a)]
        parts.append(jnp.where(low, pair, 0.0))
        parts.append(jnp.where(low, half_roll(pair), 0.0))
    return parts


def stack_high(block, rows):
    low = low_half(rows)
    parts = []
    for a in range(2):
        pair = block[:, tile(a)]
        parts.append(jnp.where(low, 0.0, half_roll(pair)))
        parts.append(jnp.where(low, 0.0, pair))
    return parts


def tile_bounds(sc_ref, at, tiles):
    first_doc = sc_ref[at]
    last_doc = sc_ref[tiles + at]
    start = sc_ref[2 * tiles] + at * QUERY_TILE
    block_lo = first_doc // KEY_BLOCK
    block_hi = (start + QUERY_TILE - 1) // KEY_BLOCK + 1
    return start, last_doc, block_lo, block_hi


def visible_mask(block, start, doc_row):
    lanes = GROUP * QUERY_TILE
    key = block * KEY_BLOCK + iota((KEY_BLOCK, lanes), 0)
    query = start + iota((1, lanes), 1) % QUERY_TILE
    return (key <= query) & (key >= doc_row)


def attend_kernel(
    sc_ref, q_ref, kv_ref, doc_ref, vec_ref, norm_ref, lse_ref, qz_ref, max_ref, sum_ref, acc_ref
):
    at = pl.program_id(1)
    tiles = pl.num_programs(1)
    start, last_doc, block_lo, block_hi = tile_bounds(sc_ref, at, tiles)
    for g, part in enumerate(stack_low(q_ref[...].astype(F32), QUERY_TILE)):
        qz_ref[g * QUERY_TILE : (g + 1) * QUERY_TILE, :] = part.astype(BF16)
    max_ref[...] = jnp.full_like(max_ref, MASK_FILLER)
    sum_ref[...] = jnp.zeros_like(sum_ref)
    acc_ref[...] = jnp.zeros_like(acc_ref)
    doc_row = jnp.concatenate([doc_ref[0:1, :]] * GROUP, axis=1)

    def visit(block, masked):
        kv = kv_ref[pl.ds(pl.multiple_of(block * KEY_BLOCK, KEY_BLOCK), KEY_BLOCK), :]
        scores = dot_nt(kv, qz_ref[...])
        if masked:
            scores = jnp.where(visible_mask(block, start, doc_row), scores, MASK_FILLER)
        before = max_ref[0:1, :]
        top = jnp.maximum(before, jnp.max(scores, axis=0, keepdims=True))
        prob = jnp.exp(scores - top)
        fade = jnp.exp(before - top)
        max_ref[0:1, :] = top
        sum_ref[0:1, :] = sum_ref[0:1, :] * fade + jnp.sum(prob, axis=0, keepdims=True)
        acc_ref[...] = acc_ref[...] * fade + dot_tn(kv, prob.astype(BF16))

    def one(block, carry):
        full = (block * KEY_BLOCK + KEY_BLOCK - 1 <= start) & (block * KEY_BLOCK >= last_doc)

        @pl.when(full)
        def _():
            visit(block, False)

        @pl.when(jnp.logical_not(full))
        def _():
            visit(block, True)

        return carry

    lax.fori_loop(block_lo, block_hi, one, 0)
    lse_ref[0, 0] = jnp.broadcast_to(max_ref[0:1, :] + jnp.log(sum_ref[0:1, :]), lse_ref.shape[2:])
    scaled = acc_ref[...] / sum_ref[0:1, :]
    low = low_half(QUERY_TILE)
    for a in range(2):
        even = half_roll(scaled[:, (2 * a) * QUERY_TILE : (2 * a + 1) * QUERY_TILE].T)
        odd = scaled[:, (2 * a + 1) * QUERY_TILE : (2 * a + 2) * QUERY_TILE].T
        both = jnp.where(low, even, odd)
        norm_ref[:, tile(a)] = both
        vec_ref[:, tile(a)] = both.astype(BF16)


def attend(scalars, q, kv, doc_row):
    rows = q.shape[0]
    length = kv.shape[0]
    tiles = rows // QUERY_TILE
    lanes = GROUP * QUERY_TILE
    width = GROUP * HEAD_SIZE
    return pl.pallas_call(
        attend_kernel,
        grid=(KEY_VALUE_HEADS, tiles),
        in_specs=[
            pl.BlockSpec(memory_space=pltpu.SMEM),
            pl.BlockSpec((QUERY_TILE, width), lambda j, t: (t, j)),
            pl.BlockSpec((length, LANES), lambda j, t: (0, j)),
            pl.BlockSpec((8, QUERY_TILE), lambda j, t: (0, t)),
        ],
        out_specs=[
            pl.BlockSpec((QUERY_TILE, width), lambda j, t: (t, j)),
            pl.BlockSpec((QUERY_TILE, width), lambda j, t: (t, j)),
            pl.BlockSpec((1, 1, 8, lanes), lambda j, t: (j, t, 0, 0)),
        ],
        out_shape=[
            jax.ShapeDtypeStruct((rows, QUERY_HEADS * HEAD_SIZE), BF16),
            jax.ShapeDtypeStruct((rows, QUERY_HEADS * HEAD_SIZE), F32),
            jax.ShapeDtypeStruct((KEY_VALUE_HEADS, tiles, 8, lanes), F32),
        ],
        scratch_shapes=[
            pltpu.VMEM((lanes, LANES), BF16),
            pltpu.VMEM((8, lanes), F32),
            pltpu.VMEM((8, lanes), F32),
            pltpu.VMEM((LANES, lanes), F32),
        ],
        compiler_params=params("arbitrary", "arbitrary"),
        cost_estimate=pl.CostEstimate(
            flops=rows * length * 2048,
            bytes_accessed=length * 512 + rows * 6000,
            transcendentals=rows * length * 4,
        ),
        name="attend",
    )(scalars, q, kv, doc_row)


def attend_back_kernel(
    sc_ref, q_ref, do_ref, norm_ref, lse_ref, kv_ref, doc_ref, dq_ref, dkv_ref, qd_ref, dkv_acc, dq_acc
):
    at = pl.program_id(1)
    tiles = pl.num_programs(1)
    lanes = GROUP * QUERY_TILE
    start, last_doc, block_lo, block_hi = tile_bounds(sc_ref, at, tiles)

    @pl.when(at == 0)
    def _():
        dkv_acc[...] = jnp.zeros_like(dkv_acc)

    grad = do_ref[...].astype(F32)
    for g, part in enumerate(stack_low(q_ref[...].astype(F32), QUERY_TILE)):
        qd_ref[g * QUERY_TILE : (g + 1) * QUERY_TILE, :] = part.astype(BF16)
    for g, part in enumerate(stack_high(grad, QUERY_TILE)):
        qd_ref[lanes + g * QUERY_TILE : lanes + (g + 1) * QUERY_TILE, :] = part.astype(BF16)
    deltas = []
    for a in range(2):
        turned = (grad[:, tile(a)] * norm_ref[:, tile(a)]).T
        deltas.append(jnp.sum(turned[0:HEAD_SIZE], axis=0, keepdims=True))
        deltas.append(jnp.sum(turned[HEAD_SIZE:], axis=0, keepdims=True))
    delta = jnp.concatenate(deltas, axis=1)
    lse = lse_ref[0, 0, 0:1, :]
    dq_acc[...] = jnp.zeros_like(dq_acc)
    doc_row = jnp.concatenate([doc_ref[0:1, :]] * GROUP, axis=1)

    def visit(block, masked):
        at_rows = pl.ds(pl.multiple_of(block * KEY_BLOCK, KEY_BLOCK), KEY_BLOCK)
        kv = kv_ref[at_rows, :]
        scores = dot_nt(kv, qd_ref[0:lanes, :])
        prob = jnp.exp(scores - lse)
        if masked:
            prob = jnp.where(visible_mask(block, start, doc_row), prob, 0.0)
        grad_prob = dot_nt(kv, qd_ref[lanes:, :])
        grad_scores = (prob * (grad_prob - delta)).astype(BF16)
        dkv_acc[at_rows, :] += dot_nn(grad_scores, qd_ref[0:lanes, :]) + dot_nn(
            prob.astype(BF16), qd_ref[lanes:, :]
        )
        dq_acc[...] += dot_tn(kv, grad_scores)

    def one(block, carry):
        full = (block * KEY_BLOCK + KEY_BLOCK - 1 <= start) & (block * KEY_BLOCK >= last_doc)

        @pl.when(full)
        def _():
            visit(block, False)

        @pl.when(jnp.logical_not(full))
        def _():
            visit(block, True)

        return carry

    lax.fori_loop(block_lo, block_hi, one, 0)
    low = low_half(QUERY_TILE)
    scale = 1.0 / math.sqrt(HEAD_SIZE)
    for a in range(2):
        even = dq_acc[:, (2 * a) * QUERY_TILE : (2 * a + 1) * QUERY_TILE].T
        odd = half_roll(dq_acc[:, (2 * a + 1) * QUERY_TILE : (2 * a + 2) * QUERY_TILE].T)
        dq_ref[:, tile(a)] = jnp.where(low, even, odd) * scale

    @pl.when(at == tiles - 1)
    def _():
        dkv_ref[...] = dkv_acc[...].astype(BF16)


def attend_back(scalars, q, grad, norm, lse, kv, doc_row):
    rows = q.shape[0]
    length = kv.shape[0]
    tiles = rows // QUERY_TILE
    lanes = GROUP * QUERY_TILE
    width = GROUP * HEAD_SIZE
    by_tile = pl.BlockSpec((QUERY_TILE, width), lambda j, t: (t, j))
    return pl.pallas_call(
        attend_back_kernel,
        grid=(KEY_VALUE_HEADS, tiles),
        in_specs=[
            pl.BlockSpec(memory_space=pltpu.SMEM),
            by_tile,
            by_tile,
            by_tile,
            pl.BlockSpec((1, 1, 8, lanes), lambda j, t: (j, t, 0, 0)),
            pl.BlockSpec((length, LANES), lambda j, t: (0, j)),
            pl.BlockSpec((8, QUERY_TILE), lambda j, t: (0, t)),
        ],
        out_specs=[by_tile, pl.BlockSpec((length, LANES), lambda j, t: (0, j))],
        out_shape=[
            jax.ShapeDtypeStruct((rows, QUERY_HEADS * HEAD_SIZE), F32),
            jax.ShapeDtypeStruct((length, KEY_VALUE_HEADS * LANES), BF16),
        ],
        scratch_shapes=[
            pltpu.VMEM((2 * lanes, LANES), BF16),
            pltpu.VMEM((length, LANES), F32),
            pltpu.VMEM((LANES, lanes), F32),
        ],
        compiler_params=params("arbitrary", "arbitrary"),
        cost_estimate=pl.CostEstimate(
            flops=rows * length * 5120,
            bytes_accessed=length * 1024 + rows * 8000,
            transcendentals=rows * length * 4,
        ),
        name="attend_back",
    )(scalars, q, grad, norm, lse, kv, doc_row)


def turn_lanes(x, cosine, sine):
    half = HEAD_SIZE // 2
    former = iota(x.shape, 1) % HEAD_SIZE < half
    other = jnp.where(former, -pltpu.roll(x, LANES - half, 1), pltpu.roll(x, half, 1))
    return x * cosine + other * sine


def rope_kernel(q_in_ref, kv_in_ref, cos_ref, sin_ref, q_ref, kv_ref):
    cosine, sine = cos_ref[...], sin_ref[...]
    scale = 1.0 / math.sqrt(HEAD_SIZE)
    for i in range(QUERY_HEADS * HEAD_SIZE // LANES):
        turned = turn_lanes(q_in_ref[:, tile(i)], cosine, sine).astype(BF16)
        q_ref[:, tile(i)] = (turned.astype(F32) * scale).astype(BF16)
    keys = turn_lanes(kv_in_ref[:, tile(0)], cosine, sine)
    values = kv_in_ref[:, tile(1)]
    low = iota(keys.shape, 1) < HEAD_SIZE
    kv_ref[:, tile(0)] = jnp.where(low, keys, half_roll(values)).astype(BF16)
    kv_ref[:, tile(1)] = jnp.where(low, half_roll(keys), values).astype(BF16)


def rope(q_raw, kv_raw, cosine, sine):
    rows = q_raw.shape[0]
    return pl.pallas_call(
        rope_kernel,
        out_shape=[
            jax.ShapeDtypeStruct((rows, QUERY_HEADS * HEAD_SIZE), BF16),
            jax.ShapeDtypeStruct((rows, KEY_VALUE_HEADS * LANES), BF16),
        ],
        compiler_params=pltpu.CompilerParams(vmem_limit_bytes=VMEM_LIMIT),
        name="rope",
    )(q_raw, kv_raw, cosine, sine)


def rope_back_kernel(dq_ref, dkv_ref, cos_ref, sin_ref, gq_ref, gkv_ref):
    cosine, sine = cos_ref[...], -sin_ref[...]
    for i in range(QUERY_HEADS * HEAD_SIZE // LANES):
        gq_ref[:, tile(i)] = turn_lanes(dq_ref[:, tile(i)], cosine, sine).astype(BF16)
    first = dkv_ref[:, tile(0)].astype(F32)
    second = dkv_ref[:, tile(1)].astype(F32)
    low = iota(first.shape, 1) < HEAD_SIZE
    keys = jnp.where(low, first, half_roll(second))
    values = jnp.where(low, half_roll(first), second)
    gkv_ref[:, tile(0)] = turn_lanes(keys, cosine, sine).astype(BF16)
    gkv_ref[:, tile(1)] = values.astype(BF16)


def rope_back(dq, dkv, cosine, sine):
    rows = dq.shape[0]
    return pl.pallas_call(
        rope_back_kernel,
        out_shape=[
            jax.ShapeDtypeStruct((rows, QUERY_HEADS * HEAD_SIZE), BF16),
            jax.ShapeDtypeStruct((rows, KEY_VALUE_HEADS * LANES), BF16),
        ],
        compiler_params=pltpu.CompilerParams(vmem_limit_bytes=VMEM_LIMIT),
        name="rope_back",
    )(dq, dkv, cosine, sine)


def shift_along(block, axis, distance):
    devices = range(lax.axis_size(axis))
    route = [(i - distance, i) for i in devices if i - distance in devices]
    return lax.ppermute(block, axis, route)


def segment_starts(positions, starts):
    reached = starts[None, :] <= positions[:, None]
    return jnp.max(jnp.where(reached, starts[None, :], -1), axis=1)


def state_entering(message, axis):
    place = lax.axis_index(axis)
    gathered = lax.all_gather(message, axis)
    state = jnp.zeros((STATE_SIZE, MAMBA_INNER), F32)
    for i in range(lax.axis_size(axis)):
        through = gathered[i, STATE_SIZE : STATE_SIZE + 1].astype(F32)
        state = jnp.where(
            i < place, through * state + gathered[i, :STATE_SIZE].astype(F32), state
        )
    return state, gathered[:, STATE_SIZE : STATE_SIZE + 1]


def gradient_entering(grad_state, through_all, axis):
    place = lax.axis_index(axis)
    devices = lax.axis_size(axis)
    gathered = lax.all_gather(grad_state, axis)
    state = jnp.zeros((STATE_SIZE, MAMBA_INNER), F32)
    for i in reversed(range(devices)):
        through = through_all[i].astype(F32)
        state = jnp.where(i > place, through * state + gathered[i].astype(F32), state)
    return state


def outer_sum(left, right):
    return dot_tn(left, right)


def time_steps(left, right):
    return dot_nt(left, right)


def reduce_to_shard(grad, dim):
    share = lax.psum_scatter(grad.astype(BF16), "fsdp", scatter_dimension=dim, tiled=True)
    return lax.psum(share, "ctx").astype(F32)


def local(
    tokens,
    cotangent,
    doc_starts,
    gain_mix,
    w_z,
    w_xbc,
    w_dt,
    conv_w,
    conv_b,
    dt_bias,
    a_log,
    skip_factor,
    w_mo,
    w_q,
    key_value_weight,
    w_o,
    gain_ffn,
    w_gate,
    w_up,
    w_down,
):
    gather = lambda w, dim: lax.all_gather(w, "fsdp", axis=dim, tiled=True)
    full_gain_mix = gather(gain_mix, 0).astype(F32)
    full_xbc = gather(w_xbc, 0)
    full_kv = gather(key_value_weight, 0)
    full_q = gather(w_q, 0)
    full_dt = gather(w_dt, 0)
    full_z = gather(w_z, 0)
    full_conv_w = gather(conv_w, 1).astype(F32)
    full_conv_b = gather(conv_b, 0).astype(F32)
    full_dt_bias = gather(dt_bias, 0).astype(F32)
    full_a_log = gather(a_log, 0).astype(F32)
    full_skip = gather(skip_factor, 0).astype(F32)
    full_mo = gather(w_mo, 0)
    full_o = gather(w_o, 0)
    full_gain_ffn = gather(gain_ffn, 0).astype(F32)
    full_gate = gather(w_gate, 0)
    full_up = gather(w_up, 0)
    full_down = gather(w_down, 0)

    ctx_rank = lax.axis_index("ctx")
    inputs = tokens[0].astype(F32)
    rows = inputs.shape[0]
    starts = doc_starts[0]
    base = ctx_rank * rows
    positions = base + jnp.arange(rows, dtype=jnp.int32)
    doc = segment_starts(positions, starts)
    doc_col = jnp.pad(doc, (0, 8))[:, None]
    doc_row = jnp.broadcast_to(doc[None, :], (8, rows))
    scalars = jnp.concatenate([doc[CHUNK - 1 :: CHUNK], base[None]])
    attn_scalars = jnp.concatenate(
        [doc[::QUERY_TILE], doc[QUERY_TILE - 1 :: QUERY_TILE], base[None]]
    )
    half = HEAD_SIZE // 2
    freqs = ROPE_BASE ** (
        -2.0 * (jnp.arange(LANES, dtype=jnp.int32) % half).astype(F32) / HEAD_SIZE
    )
    angles = positions.astype(F32)[:, None] * freqs[None, :]
    cosine, sine = jnp.cos(angles), jnp.sin(angles)
    conv_pack = jnp.pad(
        jnp.concatenate([full_conv_w, full_conv_b[None]], axis=0), ((0, 3), (0, 0))
    )
    pad_heads = lambda v: jnp.pad(v, (0, LANES - MAMBA_HEADS))[None]
    head_pack = jnp.concatenate(
        [pad_heads(full_dt_bias), pad_heads(-jnp.exp(full_a_log)), jnp.zeros((6, LANES), F32)], axis=0
    )
    skip_wide = jnp.repeat(full_skip, MAMBA_HEAD_SIZE)[None]

    scale_one = lax.rsqrt(jnp.mean(inputs * inputs, axis=-1, keepdims=True) + EPSILON)
    normed = (inputs * scale_one * full_gain_mix[None, :]).astype(BF16)
    kv_raw = dot_nn(normed, full_kv)
    q_raw = dot_nn(normed, full_q)
    mixed_in = dot_nn(normed, full_xbc).astype(BF16)
    wide_dt = jnp.pad(full_dt, ((0, 0), (0, LANES - MAMBA_HEADS)))
    dt_raw = dot_nn(normed, wide_dt)
    gate_z = dot_nn(normed, full_z)
    query, key_value = rope(q_raw, kv_raw, cosine, sine)
    kv_all = lax.all_gather(key_value, "ctx", axis=0, tiled=True)
    edge = shift_along(mixed_in[rows - 8 :], "ctx", 1).astype(F32)

    y_local, state_local, message, decay, c_mat = mamba_forward(
        scalars, edge, mixed_in, dt_raw, doc_col[:rows], conv_pack, head_pack, skip_wide
    )
    state_in, through_all = state_entering(message, "ctx")
    attn_vec, attn_norm, lse = attend(attn_scalars, query, kv_all, doc_row)
    y_total, gated, state_true = mamba_correct(y_local, state_local, c_mat, decay, state_in, gate_z)
    hidden = inputs + dot_nn(attn_vec, full_o) + dot_nn(gated, full_mo)
    gain_two = full_gain_ffn
    scale_two = lax.rsqrt(jnp.mean(hidden * hidden, axis=-1, keepdims=True) + EPSILON)
    normed_ffn = (hidden * scale_two * gain_two[None, :]).astype(BF16)
    gate = dot_nn(normed_ffn, full_gate)
    upper = dot_nn(normed_ffn, full_up)
    sig_gate = jax.nn.sigmoid(gate)
    silu_gate = gate * sig_gate
    activ = (silu_gate * upper).astype(BF16)
    result = hidden + dot_nn(activ, full_down)

    grad_out = cotangent[0]
    grad_w_down = outer_sum(activ, grad_out)
    grad_act = time_steps(grad_out, full_down)
    grad_gate = (grad_act * upper * sig_gate * (1.0 + gate * (1.0 - sig_gate))).astype(BF16)
    grad_up = (grad_act * silu_gate).astype(BF16)
    grad_w_gate = outer_sum(normed_ffn, grad_gate)
    grad_w_up = outer_sum(normed_ffn, grad_up)
    grad_n2 = time_steps(grad_gate, full_gate) + time_steps(grad_up, full_up)
    grad_gain_ffn = jnp.sum(grad_n2 * hidden * scale_two, axis=0)
    scaled_two = grad_n2 * gain_two[None, :]
    grad_hidden = (
        grad_out.astype(F32)
        + scale_two * scaled_two
        - hidden * scale_two**3 * jnp.mean(scaled_two * hidden, axis=-1, keepdims=True)
    )
    grad_hid_b = grad_hidden.astype(BF16)
    gated_grad = time_steps(grad_hid_b, full_mo)
    grad_y, grad_z, grad_state = mamba_gate_back(gated_grad, gate_z, y_total, c_mat, decay)
    grad_attn = time_steps(grad_hid_b, full_o).astype(BF16)
    grad_w_o = outer_sum(attn_vec, grad_hid_b)
    grad_w_mo = outer_sum(gated, grad_hid_b)
    state_grad = gradient_entering(grad_state, through_all, "ctx")
    grad_q, grad_kv_all = attend_back(
        attn_scalars, query, grad_attn, attn_norm, lse, kv_all, doc_row
    )
    grad_kv = lax.psum_scatter(grad_kv_all, "ctx", scatter_dimension=0, tiled=True)
    grad_mixed, tail, edge_grad, grad_dt, grad_conv, grad_heads = mamba_back(
        scalars,
        edge,
        mixed_in,
        dt_raw,
        doc_col,
        doc_row,
        conv_pack,
        head_pack,
        skip_wide,
        grad_y,
        y_total,
        state_true,
        state_grad,
    )
    behind = shift_along(edge_grad, "ctx", -1)
    grad_mixed = grad_mixed.at[rows - 8 :].set((tail + behind).astype(BF16))
    grad_q_b, grad_kv_b = rope_back(grad_q, grad_kv, cosine, sine)
    grad_w_q = outer_sum(normed, grad_q_b)
    grad_w_kv = outer_sum(normed, grad_kv_b)
    grad_w_z = outer_sum(normed, grad_z)
    grad_w_xbc = outer_sum(normed, grad_mixed)
    grad_w_dt = outer_sum(normed, grad_dt)[:, :MAMBA_HEADS]
    grad_n1 = (
        time_steps(grad_z, full_z)
        + time_steps(grad_mixed, full_xbc)
        + time_steps(grad_dt, wide_dt)
        + time_steps(grad_q_b, full_q)
        + time_steps(grad_kv_b, full_kv)
    )
    grad_gain_mix = jnp.sum(grad_n1 * inputs * scale_one, axis=0)
    scaled_one = grad_n1 * full_gain_mix[None, :]
    grad_tokens = (
        grad_hidden
        + scale_one * scaled_one
        - inputs * scale_one**3 * jnp.mean(scaled_one * inputs, axis=-1, keepdims=True)
    )
    grads = (
        (grad_gain_mix, 0),
        (grad_w_z, 0),
        (grad_w_xbc, 0),
        (grad_w_dt, 0),
        (grad_conv[:CONV], 1),
        (grad_conv[CONV], 0),
        (grad_heads[0, :MAMBA_HEADS], 0),
        (grad_heads[1, :MAMBA_HEADS], 0),
        (grad_heads[2, :MAMBA_HEADS], 0),
        (grad_w_mo, 0),
        (grad_w_q, 0),
        (grad_w_kv, 0),
        (grad_w_o, 0),
        (grad_gain_ffn, 0),
        (grad_w_gate, 0),
        (grad_w_up, 0),
        (grad_w_down, 0),
    )
    totals = tuple(reduce_to_shard(grad, dim) for grad, dim in grads)
    return (result.astype(BF16)[None], grad_tokens[None]) + totals


def solution(mesh):
    in_specs = (
        P("fsdp", "ctx", None),
        P("fsdp", "ctx", None),
        P("fsdp", None),
        P("fsdp"),
        P("fsdp", None),
        P("fsdp", None),
        P("fsdp", None),
        P(None, "fsdp"),
        P("fsdp"),
        P("fsdp"),
        P("fsdp"),
        P("fsdp"),
        P("fsdp", None),
        P("fsdp", None),
        P("fsdp", None),
        P("fsdp", None),
        P("fsdp"),
        P("fsdp", None),
        P("fsdp", None),
        P("fsdp", None),
    )
    out_specs = (
        P("fsdp", "ctx", None),
        P("fsdp", "ctx", None),
        P("fsdp"),
        P("fsdp", None),
        P("fsdp", None),
        P("fsdp", None),
        P(None, "fsdp"),
        P("fsdp"),
        P("fsdp"),
        P("fsdp"),
        P("fsdp"),
        P("fsdp", None),
        P("fsdp", None),
        P("fsdp", None),
        P("fsdp", None),
        P("fsdp"),
        P("fsdp", None),
        P("fsdp", None),
        P("fsdp", None),
    )
    return jax.shard_map(local, mesh=mesh, in_specs=in_specs, out_specs=out_specs, check_vma=False)
```

```python
import functools
import math

import jax
import jax.numpy as jnp
from jax import lax
from jax.experimental import pallas as pl
from jax.experimental.pallas import tpu as pltpu
from jax.sharding import PartitionSpec as P

MAMBA_HEADS = 24
MAMBA_HEAD_SIZE = 64
STATE_SIZE = 128
CONV = 4
QUERY_HEADS = 8
KEY_VALUE_HEADS = 2
HEAD_SIZE = 64
MAMBA_INNER = MAMBA_HEADS * MAMBA_HEAD_SIZE
CHANNELS = MAMBA_INNER + 2 * STATE_SIZE
LANES = 128
PAIRS = MAMBA_INNER // LANES
CHUNK = 128
KEY_BLOCK = 512
QUERY_TILE = 128
GROUP = QUERY_HEADS // KEY_VALUE_HEADS
MESSAGE_ROWS = STATE_SIZE + 16
VMEM_LIMIT = 56 * 1024 * 1024

EPSILON = 1e-06
ROPE_BASE = 10000.0
MASK_FILLER = -1e30
HIGHEST = lax.Precision.HIGHEST
F32 = jnp.float32
BF16 = jnp.bfloat16


def dot_nn(a, b, precision=None):
    return lax.dot_general(
        a, b, (((1,), (0,)), ((), ())), precision=precision, preferred_element_type=F32
    )


def dot_nt(a, b):
    return lax.dot_general(a, b, (((1,), (1,)), ((), ())), preferred_element_type=F32)


def dot_tn(a, b):
    return lax.dot_general(a, b, (((0,), (0,)), ((), ())), preferred_element_type=F32)


def iota(shape, dim):
    return lax.broadcasted_iota(jnp.int32, shape, dim)


def params(*semantics):
    return pltpu.CompilerParams(dimension_semantics=semantics, vmem_limit_bytes=VMEM_LIMIT)


def lasting(microseconds):
    return pl.CostEstimate(flops=int(microseconds * 1.15e9), bytes_accessed=0, transcendentals=0)


def without(kernel, at, count):
    def body(*refs):
        kernel(*refs[:at], *refs[at + count :])

    return body


def unread(arrays):
    return [pl.BlockSpec(memory_space=pl.ANY)] * len(arrays)


def whole(shape):
    return pl.BlockSpec(shape, lambda *_: (0,) * len(shape))


def low_half(rows):
    return iota((rows, LANES), 1) < MAMBA_HEAD_SIZE


def spread(values, pair, low):
    a = values[:, 2 * pair : 2 * pair + 1]
    b = values[:, 2 * pair + 1 : 2 * pair + 2]
    return jnp.where(low, a, b)


def tile(i):
    return slice(i * LANES, (i + 1) * LANES)


def split_pair(x, low):
    zero = jnp.zeros_like(x)
    return jnp.concatenate([jnp.where(low, x, zero), jnp.where(low, zero, x)], axis=0)


def fill_padded(xs_ref, edge_ref, mixed_ref):
    xs_ref[0:8, :] = edge_ref[...]
    xs_ref[8:, :] = mixed_ref[...].astype(F32)


def lag_masks(positions, doc):
    return [None] + [(positions - lag >= doc).astype(F32) for lag in range(1, CONV)]


def conv_tile(xs_ref, start, i, cw_ref, masks):
    window = xs_ref[pl.ds(start, CHUNK + 8), tile(i)]
    summed = cw_ref[4:5, tile(i)] + cw_ref[3:4, tile(i)] * window[8 : 8 + CHUNK]
    for lag in range(1, CONV):
        shifted = window[8 - lag : 8 - lag + CHUNK]
        summed = summed + cw_ref[3 - lag : 4 - lag, tile(i)] * (shifted * masks[lag])
    return summed


def softplus(v):
    return jnp.maximum(v, 0.0) + jnp.log1p(jnp.exp(-jnp.abs(v)))


def decay_sums(dt_ref, hp_ref):
    raw = dt_ref[...] + hp_ref[0:1, :]
    step = softplus(raw)
    log_decay = step * hp_ref[1:2, :]
    order = iota((CHUNK, CHUNK), 0) >= iota((CHUNK, CHUNK), 1)
    cumul = dot_nn(order.astype(F32), log_decay, HIGHEST)
    return raw, step, log_decay, cumul


def mamba_forward_kernel(
    sc_ref,
    edge_ref,
    mixed_ref,
    dt_ref,
    doc_ref,
    cw_ref,
    hp_ref,
    skip_ref,
    y_ref,
    sin_ref,
    msg_ref,
    own_ref,
    dec_ref,
    c_ref,
    xs_ref,
    xa_ref,
    state_ref,
    carry_ref,
):
    c = pl.program_id(0)
    count = pl.num_programs(0)

    @pl.when(c == 0)
    def _():
        fill_padded(xs_ref, edge_ref, mixed_ref)
        state_ref[...] = jnp.zeros_like(state_ref)
        carry_ref[...] = jnp.zeros_like(carry_ref)

    base = sc_ref[count]
    start = pl.multiple_of(c * CHUNK, CHUNK)
    first = base + start
    end_doc = sc_ref[c]
    doc = doc_ref[...]
    positions = first + iota((CHUNK, 1), 0)
    masks = lag_masks(positions, doc)
    for i in range(CHANNELS // LANES):
        summed = conv_tile(xs_ref, start, i, cw_ref, masks)
        xa_ref[:, tile(i)] = summed * jax.nn.sigmoid(summed)
    _, step, log_decay, cumul = decay_sums(dt_ref, hp_ref)
    cumul_t = cumul.T
    b_mat = xa_ref[:, tile(PAIRS)]
    c_mat = xa_ref[:, tile(PAIRS + 1)].astype(BF16)
    c_ref[...] = c_mat
    couple = dot_nt(c_mat, b_mat.astype(BF16))
    b_turned = b_mat.T.astype(BF16)
    col = first + iota((CHUNK, CHUNK), 1)
    row = first + iota((CHUNK, CHUNK), 0)
    couple = jnp.where((col <= row) & (col >= doc), couple, 0.0)
    carried = (doc < first).astype(F32)
    into = jnp.exp(cumul) * carried
    last = cumul[CHUNK - 1 : CHUNK, :]
    ending = jnp.exp(last - cumul) * (positions >= end_doc).astype(F32)
    keep = jnp.exp(last) * (end_doc < first).astype(F32)
    dec_ref[...] = jnp.where(doc < base, jnp.exp(cumul + carry_ref[0:1, :]), 0.0)
    low = low_half(CHUNK)
    low_row = low_half(1)
    for j in range(PAIRS):
        x = xa_ref[:, tile(j)]
        weighted = x * spread(step, j, low)
        mixing = []
        for h in (2 * j, 2 * j + 1):
            gap = jnp.minimum(cumul[:, h : h + 1] - cumul_t[h : h + 1, :], 0.0)
            mixing.append((couple * jnp.exp(gap)).astype(BF16))
        y = dot_nn(jnp.concatenate(mixing, axis=1), split_pair(weighted.astype(BF16), low))
        state = state_ref[:, tile(j)]
        sin_ref[0, :, tile(j)] = state
        y = y + dot_nn(c_mat, state.astype(BF16)) * spread(into, j, low)
        y_ref[:, tile(j)] = y + skip_ref[0:1, tile(j)] * x
        fresh = dot_nn(b_turned, (weighted * spread(ending, j, low)).astype(BF16))
        state_ref[:, tile(j)] = fresh + state * spread(keep, j, low_row)
    carry_ref[...] = carry_ref[...] + last

    @pl.when(c == count - 1)
    def _():
        msg_ref[0:STATE_SIZE, :] = state_ref[...].astype(BF16)
        own_ref[0:STATE_SIZE, :] = state_ref[...]
        through = jnp.exp(carry_ref[...]) * (end_doc < base).astype(F32)
        low8 = low_half(8)
        for j in range(PAIRS):
            wide = spread(through, j, low8)
            wide = jnp.concatenate([wide, wide], axis=0)
            msg_ref[STATE_SIZE:, tile(j)] = wide.astype(BF16)
            own_ref[STATE_SIZE:, tile(j)] = wide


def mamba_forward(scalars, edge, mixed, dt_raw, doc, conv_pack, head_pack, skip_wide):
    rows = mixed.shape[0]
    count = rows // CHUNK
    by_chunk = lambda width: pl.BlockSpec((CHUNK, width), lambda c: (c, 0))
    return pl.pallas_call(
        mamba_forward_kernel,
        grid=(count,),
        in_specs=[
            pl.BlockSpec(memory_space=pltpu.SMEM),
            whole((8, CHANNELS)),
            whole((rows, CHANNELS)),
            by_chunk(LANES),
            by_chunk(1),
            whole((8, CHANNELS)),
            whole((8, LANES)),
            whole((1, MAMBA_INNER)),
        ],
        out_specs=[
            by_chunk(MAMBA_INNER),
            pl.BlockSpec((1, STATE_SIZE, MAMBA_INNER), lambda c: (c, 0, 0)),
            whole((MESSAGE_ROWS, MAMBA_INNER)),
            whole((MESSAGE_ROWS, MAMBA_INNER)),
            by_chunk(LANES),
            by_chunk(LANES),
        ],
        out_shape=[
            jax.ShapeDtypeStruct((rows, MAMBA_INNER), F32),
            jax.ShapeDtypeStruct((count, STATE_SIZE, MAMBA_INNER), F32),
            jax.ShapeDtypeStruct((MESSAGE_ROWS, MAMBA_INNER), BF16),
            jax.ShapeDtypeStruct((MESSAGE_ROWS, MAMBA_INNER), F32),
            jax.ShapeDtypeStruct((rows, LANES), F32),
            jax.ShapeDtypeStruct((rows, LANES), BF16),
        ],
        scratch_shapes=[
            pltpu.VMEM((rows + 8, CHANNELS), F32),
            pltpu.VMEM((CHUNK, CHANNELS), F32),
            pltpu.VMEM((STATE_SIZE, MAMBA_INNER), F32),
            pltpu.VMEM((8, LANES), F32),
        ],
        compiler_params=params("arbitrary"),
        cost_estimate=lasting(13),
        name="mamba_forward",
    )(scalars, edge, mixed, dt_raw, doc, conv_pack, head_pack, skip_wide)


QUARTERS = 4
BLOCK_TILES = 1 + PAIRS // QUARTERS


def attn_tile(i):
    return tile(i * BLOCK_TILES)


def gated_tile(j):
    per = PAIRS // QUARTERS
    return tile(j // per * BLOCK_TILES + 1 + j % per)


def mamba_correct_kernel(
    y_ref, sin_ref, c_ref, dec_ref, state_ref, z_ref, vec0_ref, vec1_ref, total_ref, both_ref, true_ref, edge_ref
):
    c = pl.program_id(0)

    @pl.when(c == 0)
    def _():
        edge_ref[...] = jnp.ones_like(edge_ref)

    low = low_half(CHUNK)
    low_row = low_half(1)
    decay = dec_ref[...]
    before = edge_ref[0:1, :]
    c_mat = c_ref[...]
    for j in range(PAIRS):
        state = state_ref[:, tile(j)]
        y = y_ref[:, tile(j)] + dot_nn(c_mat, state.astype(BF16)) * spread(decay, j, low)
        total_ref[:, tile(j)] = y
        z = z_ref[:, tile(j)]
        both_ref[:, gated_tile(j)] = (y * (z * jax.nn.sigmoid(z))).astype(BF16)
        true_ref[0, :, tile(j)] = (
            sin_ref[0, :, tile(j)] + state * spread(before, j, low_row)
        ).astype(BF16)
    for i, vec_ref in enumerate((vec0_ref, vec0_ref, vec1_ref, vec1_ref)):
        both_ref[:, attn_tile(i)] = vec_ref[:, tile(i % 2)]
    edge_ref[0:1, :] = decay[CHUNK - 1 : CHUNK, :]


def mamba_correct(y, sin, c_mat, decay, state_in, gate_z, vec0, vec1):
    rows = y.shape[0]
    count = rows // CHUNK
    by_chunk = lambda width: pl.BlockSpec((CHUNK, width), lambda c: (c, 0))
    states = pl.BlockSpec((1, STATE_SIZE, MAMBA_INNER), lambda c: (c, 0, 0))
    return pl.pallas_call(
        mamba_correct_kernel,
        grid=(count,),
        in_specs=[
            by_chunk(MAMBA_INNER),
            states,
            by_chunk(LANES),
            by_chunk(LANES),
            whole((STATE_SIZE, MAMBA_INNER)),
            by_chunk(MAMBA_INNER),
            by_chunk(2 * LANES),
            by_chunk(2 * LANES),
        ],
        out_specs=[by_chunk(MAMBA_INNER), by_chunk(QUARTERS * BLOCK_TILES * LANES), states],
        out_shape=[
            jax.ShapeDtypeStruct((rows, MAMBA_INNER), F32),
            jax.ShapeDtypeStruct((rows, QUARTERS * BLOCK_TILES * LANES), BF16),
            jax.ShapeDtypeStruct((count, STATE_SIZE, MAMBA_INNER), BF16),
        ],
        scratch_shapes=[pltpu.VMEM((8, LANES), F32)],
        compiler_params=params("arbitrary"),
        cost_estimate=lasting(8.5),
        name="mamba_correct",
    )(y, sin, c_mat, decay, state_in, gate_z, vec0, vec1)


def mamba_gate_back_kernel(
    both_ref, z_ref, y_ref, c_ref, dec_ref, own_ref, dy_ref, gz_ref, gsi_ref, gsb_ref, gvec_ref, acc_ref
):
    c = pl.program_id(0)

    @pl.when(c == 0)
    def _():
        acc_ref[...] = jnp.zeros_like(acc_ref)

    low = low_half(CHUNK)
    decay = dec_ref[...]
    c_turned = c_ref[...].astype(F32).T.astype(BF16)
    for j in range(PAIRS):
        z = z_ref[:, tile(j)]
        sig = jax.nn.sigmoid(z)
        silu = z * sig
        grad = both_ref[:, gated_tile(j)]
        gz_ref[:, tile(j)] = (grad * y_ref[:, tile(j)] * (sig + silu * (1.0 - sig))).astype(BF16)
        dy = (grad * silu).astype(BF16)
        dy_ref[:, tile(j)] = dy
        scaled = (dy.astype(F32) * spread(decay, j, low)).astype(BF16)
        acc_ref[:, tile(j)] += dot_nn(c_turned, scaled)
    for i in range(QUARTERS):
        gvec_ref[:, tile(i)] = both_ref[:, attn_tile(i)].astype(BF16)

    @pl.when(c == pl.num_programs(0) - 1)
    def _():
        gsi_ref[0:STATE_SIZE, :] = acc_ref[...]
        gsb_ref[0:STATE_SIZE, :] = acc_ref[...].astype(BF16)
        gsi_ref[STATE_SIZE:, :] = own_ref[...]
        gsb_ref[STATE_SIZE:, :] = own_ref[...].astype(BF16)


def mamba_gate_back(both_grad, gate_z, total, c_mat, decay, own, tokens=()):
    rows = total.shape[0]
    by_chunk = lambda width: pl.BlockSpec((CHUNK, width), lambda c: (c, 0))
    return pl.pallas_call(
        without(mamba_gate_back_kernel, 6, len(tokens)),
        grid=(rows // CHUNK,),
        in_specs=[
            by_chunk(QUARTERS * BLOCK_TILES * LANES),
            by_chunk(MAMBA_INNER),
            by_chunk(MAMBA_INNER),
            by_chunk(LANES),
            by_chunk(LANES),
            pl.BlockSpec((16, MAMBA_INNER), lambda c: (STATE_SIZE // 16, 0)),
            *unread(tokens),
        ],
        out_specs=[
            by_chunk(MAMBA_INNER),
            by_chunk(MAMBA_INNER),
            whole((MESSAGE_ROWS, MAMBA_INNER)),
            whole((MESSAGE_ROWS, MAMBA_INNER)),
            by_chunk(QUARTERS * LANES),
        ],
        out_shape=[
            jax.ShapeDtypeStruct((rows, MAMBA_INNER), BF16),
            jax.ShapeDtypeStruct((rows, MAMBA_INNER), BF16),
            jax.ShapeDtypeStruct((MESSAGE_ROWS, MAMBA_INNER), F32),
            jax.ShapeDtypeStruct((MESSAGE_ROWS, MAMBA_INNER), BF16),
            jax.ShapeDtypeStruct((rows, QUARTERS * LANES), BF16),
        ],
        scratch_shapes=[pltpu.VMEM((STATE_SIZE, MAMBA_INNER), F32)],
        compiler_params=params("arbitrary"),
        cost_estimate=lasting(7.5),
        name="mamba_gate_back",
    )(both_grad, gate_z, total, c_mat, decay, own, *tokens)


def picks(pair):
    channel = iota((LANES, LANES), 0)
    head = iota((LANES, LANES), 1)
    return (head == 2 * pair + channel // MAMBA_HEAD_SIZE).astype(BF16)


def head_sums(product, select):
    high = product.astype(BF16)
    rest = (product - high.astype(F32)).astype(BF16)
    return dot_nn(high, select) + dot_nn(rest, select)


def mamba_back_kernel(
    sc_ref,
    edge_ref,
    mixed_ref,
    dt_ref,
    doc_ref,
    doc_row_ref,
    cw_ref,
    hp_ref,
    skip_ref,
    dy_ref,
    y_ref,
    sin_ref,
    ds_end_ref,
    gmix_ref,
    tail_ref,
    edge_grad_ref,
    gdt_ref,
    gconv_ref,
    ghead_ref,
    xs_ref,
    xa_ref,
    slope_ref,
    grad_ref,
    ds_ref,
    rows_ref,
):
    step_at = pl.program_id(0)
    count = pl.num_programs(0)
    c = count - 1 - step_at
    rows = count * CHUNK

    @pl.when(step_at == 0)
    def _():
        fill_padded(xs_ref, edge_ref, mixed_ref)
        ds_ref[...] = ds_end_ref[...]
        grad_ref[pl.ds(rows, 8), :] = jnp.zeros((8, CHANNELS), F32)
        gconv_ref[...] = jnp.zeros_like(gconv_ref)
        ghead_ref[...] = jnp.zeros_like(ghead_ref)
        rows_ref[...] = jnp.zeros_like(rows_ref)

    base = sc_ref[count]
    start = pl.multiple_of(c * CHUNK, CHUNK)
    first = base + start
    end_doc = sc_ref[c]
    doc_window = doc_ref[pl.ds(start, CHUNK + 8), :]
    doc = doc_window[0:CHUNK]
    positions_window = first + iota((CHUNK + 8, 1), 0)
    positions = positions_window[0:CHUNK]
    masks_window = lag_masks(positions_window, doc_window)
    masks = [None] + [m[0:CHUNK] for m in masks_window[1:]]
    for i in range(CHANNELS // LANES):
        summed = conv_tile(xs_ref, start, i, cw_ref, masks)
        sig = jax.nn.sigmoid(summed)
        act = summed * sig
        xa_ref[:, tile(i)] = act
        slope_ref[:, tile(i)] = sig + act * (1.0 - sig)
    raw, step, log_decay, cumul = decay_sums(dt_ref, hp_ref)
    cumul_t = cumul.T
    b_mat = xa_ref[:, tile(PAIRS)].astype(BF16)
    c_f32 = xa_ref[:, tile(PAIRS + 1)]
    c_mat = c_f32.astype(BF16)
    c_turned = c_f32.T.astype(BF16)
    key = first + iota((CHUNK, CHUNK), 0)
    query = first + iota((CHUNK, CHUNK), 1)
    visible = (key <= query) & (key >= doc_row_ref[0:1, :])
    couple = jnp.where(visible, dot_nt(b_mat, c_mat), 0.0)
    carried = (doc < first).astype(F32)
    into = jnp.exp(cumul) * carried
    last = cumul[CHUNK - 1 : CHUNK, :]
    ending = jnp.exp(last - cumul) * (positions >= end_doc).astype(F32)
    keep = jnp.exp(last) * (end_doc < first).astype(F32)
    low = low_half(CHUNK)
    low_row = low_half(1)
    grad_couple = jnp.zeros((CHUNK, CHUNK), F32)
    grad_b = jnp.zeros((CHUNK, STATE_SIZE), F32)
    grad_c = jnp.zeros((CHUNK, STATE_SIZE), F32)
    grad_cumul = jnp.zeros((CHUNK, LANES), F32)
    grad_step = jnp.zeros((CHUNK, LANES), F32)
    end_sums = jnp.zeros((8, LANES), F32)
    for j in range(PAIRS):
        select = picks(j)
        x = xa_ref[:, tile(j)]
        step_wide = spread(step, j, low)
        weighted = x * step_wide
        weighted_b = weighted.astype(BF16)
        dy = dy_ref[:, tile(j)]
        dy_f32 = dy.astype(F32)
        grad_mixing = dot_nt(split_pair(weighted_b, low), dy)
        mixing = []
        for side, h in enumerate((2 * j, 2 * j + 1)):
            gap = jnp.minimum(cumul_t[h : h + 1, :] - cumul[:, h : h + 1], 0.0)
            fade = jnp.exp(gap)
            mixing.append((couple * fade).astype(BF16))
            grad_couple += grad_mixing[side * CHUNK : (side + 1) * CHUNK] * fade
        grad_weighted = dot_nn(jnp.concatenate(mixing, axis=1), split_pair(dy, low))
        ending_wide = spread(ending, j, low)
        grad_state = ds_ref[:, tile(j)]
        grad_state_b = grad_state.astype(BF16)
        state = sin_ref[0, :, tile(j)]
        through_state = ending_wide * dot_nn(b_mat, grad_state_b)
        grad_weighted = grad_weighted + through_state
        dy_into = (dy_f32 * spread(into, j, low)).astype(BF16)
        grad_c += dot_nt(dy_into, state)
        grad_b += dot_nt((weighted * ending_wide).astype(BF16), grad_state_b)
        keep_wide = spread(keep, j, low_row)
        weighted_f32 = weighted_b.astype(F32)
        to_end = jnp.sum(weighted_f32 * through_state, axis=0, keepdims=True) + keep_wide * jnp.sum(
            grad_state * state.astype(F32), axis=0, keepdims=True
        )
        ds_ref[:, tile(j)] = keep_wide * grad_state + dot_nn(c_turned, dy_into)
        skip = skip_ref[0:1, tile(j)]
        grad_x = step_wide * grad_weighted + skip * dy_f32
        grad_ref[pl.ds(start, CHUNK), tile(j)] = grad_x * slope_ref[:, tile(j)]
        rows_ref[0:1, tile(j)] += jnp.sum(dy_f32 * x, axis=0, keepdims=True)
        in_out = dy_f32 * (y_ref[:, tile(j)] - skip * x) - weighted_f32 * grad_weighted
        grad_cumul += head_sums(in_out, select)
        grad_step += head_sums(grad_weighted * x, select)
        end_sums += head_sums(jnp.broadcast_to(to_end, (8, LANES)), select)
    grad_couple = jnp.where(visible, grad_couple, 0.0).astype(BF16)
    grad_b += dot_nn(grad_couple, c_mat)
    grad_c += dot_tn(grad_couple, b_mat)
    grad_ref[pl.ds(start, CHUNK), tile(PAIRS)] = grad_b * slope_ref[:, tile(PAIRS)]
    grad_ref[pl.ds(start, CHUNK), tile(PAIRS + 1)] = grad_c * slope_ref[:, tile(PAIRS + 1)]
    later = (iota((CHUNK, CHUNK), 0) <= iota((CHUNK, CHUNK), 1)).astype(F32)
    grad_log = dot_nn(later, grad_cumul, HIGHEST) + end_sums[0:1, :]
    grad_raw = (grad_step + grad_log * hp_ref[1:2, :]) * jax.nn.sigmoid(raw)
    gdt_ref[...] = grad_raw.astype(BF16)
    ghead_ref[0:1, :] += jnp.sum(grad_raw, axis=0, keepdims=True)
    ghead_ref[1:2, :] += jnp.sum(grad_log * log_decay, axis=0, keepdims=True)
    for i in range(CHANNELS // LANES):
        window = grad_ref[pl.ds(start, CHUNK + 8), tile(i)]
        own = window[0:CHUNK]
        padded = xs_ref[pl.ds(start, CHUNK + 8), tile(i)]
        total = cw_ref[3:4, tile(i)] * own
        gconv_ref[4:5, tile(i)] += jnp.sum(own, axis=0, keepdims=True)
        gconv_ref[3:4, tile(i)] += jnp.sum(own * padded[8 : 8 + CHUNK], axis=0, keepdims=True)
        for lag in range(1, CONV):
            masked = window * masks_window[lag]
            total = total + cw_ref[3 - lag : 4 - lag, tile(i)] * masked[lag : lag + CHUNK]
            gconv_ref[3 - lag : 4 - lag, tile(i)] += jnp.sum(
                masked[0:CHUNK] * padded[8 - lag : 8 - lag + CHUNK], axis=0, keepdims=True
            )
        gmix_ref[:, tile(i)] = total.astype(BF16)

        @pl.when(step_at == 0)
        def _():
            tail_ref[:, tile(i)] = total[CHUNK - 8 :]

        @pl.when(step_at == count - 1)
        def _():
            ahead = jnp.zeros((8, LANES), F32)
            for lag in range(1, CONV):
                head = jnp.concatenate(
                    [jnp.zeros((8, LANES), F32), window[0:8] * masks_window[lag][0:8]], axis=0
                )
                ahead = ahead + cw_ref[3 - lag : 4 - lag, tile(i)] * head[lag : lag + 8]
            edge_grad_ref[:, tile(i)] = ahead

    @pl.when(step_at == count - 1)
    def _():
        total = jnp.zeros((8, LANES), F32)
        for j in range(PAIRS):
            total += head_sums(rows_ref[:, tile(j)], picks(j))
        ghead_ref[2:3, :] = total[0:1, :]


def mamba_back(
    scalars,
    edge,
    mixed,
    dt_raw,
    doc,
    doc_row,
    conv_pack,
    head_pack,
    skip_wide,
    dy,
    y,
    sin,
    ds_end,
    tokens=(),
):
    rows = mixed.shape[0]
    count = rows // CHUNK
    by_chunk = lambda width: pl.BlockSpec((CHUNK, width), lambda i: (count - 1 - i, 0))
    return pl.pallas_call(
        without(mamba_back_kernel, 13, len(tokens)),
        grid=(count,),
        in_specs=[
            pl.BlockSpec(memory_space=pltpu.SMEM),
            whole((8, CHANNELS)),
            whole((rows, CHANNELS)),
            by_chunk(LANES),
            whole((rows + 8, 1)),
            pl.BlockSpec((8, CHUNK), lambda i: (0, count - 1 - i)),
            whole((8, CHANNELS)),
            whole((8, LANES)),
            whole((1, MAMBA_INNER)),
            by_chunk(MAMBA_INNER),
            by_chunk(MAMBA_INNER),
            pl.BlockSpec((1, STATE_SIZE, MAMBA_INNER), lambda i: (count - 1 - i, 0, 0)),
            whole((STATE_SIZE, MAMBA_INNER)),
            *unread(tokens),
        ],
        out_specs=[
            by_chunk(CHANNELS),
            whole((8, CHANNELS)),
            whole((8, CHANNELS)),
            by_chunk(LANES),
            whole((8, CHANNELS)),
            whole((8, LANES)),
        ],
        out_shape=[
            jax.ShapeDtypeStruct((rows, CHANNELS), BF16),
            jax.ShapeDtypeStruct((8, CHANNELS), F32),
            jax.ShapeDtypeStruct((8, CHANNELS), F32),
            jax.ShapeDtypeStruct((rows, LANES), BF16),
            jax.ShapeDtypeStruct((8, CHANNELS), F32),
            jax.ShapeDtypeStruct((8, LANES), F32),
        ],
        scratch_shapes=[
            pltpu.VMEM((rows + 8, CHANNELS), F32),
            pltpu.VMEM((CHUNK, CHANNELS), F32),
            pltpu.VMEM((CHUNK, CHANNELS), F32),
            pltpu.VMEM((rows + 8, CHANNELS), F32),
            pltpu.VMEM((STATE_SIZE, MAMBA_INNER), F32),
            pltpu.VMEM((8, MAMBA_INNER), F32),
        ],
        compiler_params=params("arbitrary"),
        cost_estimate=lasting(25),
        name="mamba_back",
    )(
        scalars,
        edge,
        mixed,
        dt_raw,
        doc,
        doc_row,
        conv_pack,
        head_pack,
        skip_wide,
        dy,
        y,
        sin,
        ds_end,
        *tokens,
    )


def scan_step_kernel(flag_ref, total_ref, seen_ref, got_ref, new_ref, send_ref, out_ref):
    first = flag_ref[0] == 1
    rows = slice(0, STATE_SIZE)
    rest = slice(STATE_SIZE, MESSAGE_ROWS)
    one = STATE_SIZE
    for j in range(PAIRS):
        total, seen = total_ref[:, tile(j)], seen_ref[:, tile(j)]
        got = got_ref[:, tile(j)].astype(F32)
        mine, theirs = total[one : one + 1], got[one : one + 1]
        state = jnp.where(first, mine * got[rows] + total[rows], theirs * total[rows] + got[rows])
        new_ref[rows, tile(j)] = state
        send_ref[rows, tile(j)] = state.astype(BF16)
        factor = total[rest] * got[rest]
        new_ref[rest, tile(j)] = factor
        send_ref[rest, tile(j)] = factor.astype(BF16)
        passed = seen[rows] + seen[one : one + 1] * got[rows]
        out_ref[rows, tile(j)] = jnp.where(first, passed, seen[rows])
        out_ref[rest, tile(j)] = jnp.where(first, seen[rest] * got[rest], seen[rest])


def scan_step(first, total, seen, got):
    shape = (MESSAGE_ROWS, MAMBA_INNER)
    return pl.pallas_call(
        scan_step_kernel,
        in_specs=[pl.BlockSpec(memory_space=pltpu.SMEM)] + [whole(shape)] * 3,
        out_specs=[whole(shape)] * 3,
        out_shape=[
            jax.ShapeDtypeStruct(shape, F32),
            jax.ShapeDtypeStruct(shape, BF16),
            jax.ShapeDtypeStruct(shape, F32),
        ],
        compiler_params=pltpu.CompilerParams(vmem_limit_bytes=VMEM_LIMIT),
        cost_estimate=lasting(2.5),
        name="scan_step",
    )(first.astype(jnp.int32).reshape(1), total, seen, got)


def half_roll(x):
    return pltpu.roll(x, HEAD_SIZE, 1)


def stack_low(block, rows):
    low = low_half(rows)
    parts = []
    for a in range(2):
        pair = block[:, tile(a)]
        parts.append(jnp.where(low, pair, 0.0))
        parts.append(jnp.where(low, half_roll(pair), 0.0))
    return parts


def stack_high(block, rows):
    low = low_half(rows)
    parts = []
    for a in range(2):
        pair = block[:, tile(a)]
        parts.append(jnp.where(low, 0.0, half_roll(pair)))
        parts.append(jnp.where(low, 0.0, pair))
    return parts


def tile_bounds(sc_ref, at, tiles):
    first_doc = sc_ref[at]
    last_doc = sc_ref[tiles + at]
    start = sc_ref[2 * tiles] + at * QUERY_TILE
    block_lo = first_doc // KEY_BLOCK
    block_hi = (start + QUERY_TILE - 1) // KEY_BLOCK + 1
    return start, last_doc, block_lo, block_hi


def visible_mask(block, start, doc_row):
    lanes = GROUP * QUERY_TILE
    key = block * KEY_BLOCK + iota((KEY_BLOCK, lanes), 0)
    query = start + iota((1, lanes), 1) % QUERY_TILE
    return (key <= query) & (key >= doc_row)


def attend_kernel(
    sc_ref, q_ref, kv_ref, doc_ref, vec_ref, norm_ref, lse_ref, qz_ref, max_ref, sum_ref, acc_ref
):
    at = pl.program_id(0)
    tiles = pl.num_programs(0)
    start, last_doc, block_lo, block_hi = tile_bounds(sc_ref, at, tiles)
    for g, part in enumerate(stack_low(q_ref[...].astype(F32), QUERY_TILE)):
        qz_ref[g * QUERY_TILE : (g + 1) * QUERY_TILE, :] = part.astype(BF16)
    max_ref[...] = jnp.full_like(max_ref, MASK_FILLER)
    sum_ref[...] = jnp.zeros_like(sum_ref)
    acc_ref[...] = jnp.zeros_like(acc_ref)
    doc_row = jnp.concatenate([doc_ref[0:1, :]] * GROUP, axis=1)

    def visit(block, masked):
        at_rows = sc_ref[2 * tiles + 1 + block] * KEY_BLOCK
        kv = kv_ref[pl.ds(pl.multiple_of(at_rows, KEY_BLOCK), KEY_BLOCK), :]
        scores = dot_nt(kv, qz_ref[...])
        if masked:
            scores = jnp.where(visible_mask(block, start, doc_row), scores, MASK_FILLER)
        before = max_ref[0:1, :]
        top = jnp.maximum(before, jnp.max(scores, axis=0, keepdims=True))
        prob = jnp.exp(scores - top)
        fade = jnp.exp(before - top)
        max_ref[0:1, :] = top
        sum_ref[0:1, :] = sum_ref[0:1, :] * fade + jnp.sum(prob, axis=0, keepdims=True)
        acc_ref[...] = acc_ref[...] * fade + dot_tn(kv, prob.astype(BF16))

    def one(block, carry):
        full = (block * KEY_BLOCK + KEY_BLOCK - 1 <= start) & (block * KEY_BLOCK >= last_doc)

        @pl.when(full)
        def _():
            visit(block, False)

        @pl.when(jnp.logical_not(full))
        def _():
            visit(block, True)

        return carry

    lax.fori_loop(block_lo, block_hi, one, 0)
    lse_ref[0] = jnp.broadcast_to(max_ref[0:1, :] + jnp.log(sum_ref[0:1, :]), lse_ref.shape[1:])
    scaled = acc_ref[...] / sum_ref[0:1, :]
    low = low_half(QUERY_TILE)
    for a in range(2):
        even = half_roll(scaled[:, (2 * a) * QUERY_TILE : (2 * a + 1) * QUERY_TILE].T)
        odd = scaled[:, (2 * a + 1) * QUERY_TILE : (2 * a + 2) * QUERY_TILE].T
        both = jnp.where(low, even, odd)
        norm_ref[:, tile(a)] = both
        vec_ref[:, tile(a)] = both.astype(BF16)


def attend(scalars, q, kv, doc_row, head, tokens=()):
    rows = q.shape[0]
    length = kv.shape[0]
    tiles = rows // QUERY_TILE
    lanes = GROUP * QUERY_TILE
    width = GROUP * HEAD_SIZE
    by_tile = pl.BlockSpec((QUERY_TILE, width), lambda t: (t, 0))
    return pl.pallas_call(
        without(attend_kernel, 4, len(tokens)),
        grid=(tiles,),
        in_specs=[
            pl.BlockSpec(memory_space=pltpu.SMEM),
            pl.BlockSpec((QUERY_TILE, width), lambda t: (t, head)),
            whole((length, LANES)),
            pl.BlockSpec((8, QUERY_TILE), lambda t: (0, t)),
            *unread(tokens),
        ],
        out_specs=[by_tile, by_tile, pl.BlockSpec((1, 8, lanes), lambda t: (t, 0, 0))],
        out_shape=[
            jax.ShapeDtypeStruct((rows, width), BF16),
            jax.ShapeDtypeStruct((rows, width), F32),
            jax.ShapeDtypeStruct((tiles, 8, lanes), F32),
        ],
        scratch_shapes=[
            pltpu.VMEM((lanes, LANES), BF16),
            pltpu.VMEM((8, lanes), F32),
            pltpu.VMEM((8, lanes), F32),
            pltpu.VMEM((LANES, lanes), F32),
        ],
        compiler_params=params("arbitrary"),
        cost_estimate=lasting(22),
        name="attend",
    )(scalars, q, kv, doc_row, *tokens)


def attend_back_kernel(
    sc_ref, q_ref, do_ref, norm_ref, lse_ref, kv_ref, doc_ref, dq_ref, dkv_ref, qd_ref, dkv_acc, dq_acc
):
    at = pl.program_id(0)
    tiles = pl.num_programs(0)
    lanes = GROUP * QUERY_TILE
    start, last_doc, block_lo, block_hi = tile_bounds(sc_ref, at, tiles)

    @pl.when(at == 0)
    def _():
        dkv_acc[...] = jnp.zeros_like(dkv_acc)

    grad = do_ref[...].astype(F32)
    for g, part in enumerate(stack_low(q_ref[...].astype(F32), QUERY_TILE)):
        qd_ref[g * QUERY_TILE : (g + 1) * QUERY_TILE, :] = part.astype(BF16)
    for g, part in enumerate(stack_high(grad, QUERY_TILE)):
        qd_ref[lanes + g * QUERY_TILE : lanes + (g + 1) * QUERY_TILE, :] = part.astype(BF16)
    deltas = []
    for a in range(2):
        turned = (grad[:, tile(a)] * norm_ref[:, tile(a)]).T
        deltas.append(jnp.sum(turned[0:HEAD_SIZE], axis=0, keepdims=True))
        deltas.append(jnp.sum(turned[HEAD_SIZE:], axis=0, keepdims=True))
    delta = jnp.concatenate(deltas, axis=1)
    lse = lse_ref[0, 0:1, :]
    dq_acc[...] = jnp.zeros_like(dq_acc)
    doc_row = jnp.concatenate([doc_ref[0:1, :]] * GROUP, axis=1)

    def visit(block, masked):
        first_row = sc_ref[2 * tiles + 1 + block] * KEY_BLOCK
        at_rows = pl.ds(pl.multiple_of(first_row, KEY_BLOCK), KEY_BLOCK)
        kv = kv_ref[at_rows, :]
        scores = dot_nt(kv, qd_ref[0:lanes, :])
        prob = jnp.exp(scores - lse)
        if masked:
            prob = jnp.where(visible_mask(block, start, doc_row), prob, 0.0)
        grad_prob = dot_nt(kv, qd_ref[lanes:, :])
        grad_scores = (prob * (grad_prob - delta)).astype(BF16)
        dkv_acc[at_rows, :] += dot_nn(grad_scores, qd_ref[0:lanes, :]) + dot_nn(
            prob.astype(BF16), qd_ref[lanes:, :]
        )
        dq_acc[...] += dot_tn(kv, grad_scores)

    def one(block, carry):
        full = (block * KEY_BLOCK + KEY_BLOCK - 1 <= start) & (block * KEY_BLOCK >= last_doc)

        @pl.when(full)
        def _():
            visit(block, False)

        @pl.when(jnp.logical_not(full))
        def _():
            visit(block, True)

        return carry

    lax.fori_loop(block_lo, block_hi, one, 0)
    low = low_half(QUERY_TILE)
    scale = 1.0 / math.sqrt(HEAD_SIZE)
    for a in range(2):
        even = dq_acc[:, (2 * a) * QUERY_TILE : (2 * a + 1) * QUERY_TILE].T
        odd = half_roll(dq_acc[:, (2 * a + 1) * QUERY_TILE : (2 * a + 2) * QUERY_TILE].T)
        dq_ref[:, tile(a)] = jnp.where(low, even, odd) * scale

    @pl.when(at == tiles - 1)
    def _():
        dkv_ref[...] = dkv_acc[...].astype(BF16)


def attend_back(scalars, q, grad, norm, lse, kv, doc_row, head, tokens=()):
    rows = q.shape[0]
    length = kv.shape[0]
    tiles = rows // QUERY_TILE
    lanes = GROUP * QUERY_TILE
    width = GROUP * HEAD_SIZE
    by_tile = pl.BlockSpec((QUERY_TILE, width), lambda t: (t, 0))
    by_head = pl.BlockSpec((QUERY_TILE, width), lambda t: (t, head))
    return pl.pallas_call(
        without(attend_back_kernel, 7, len(tokens)),
        grid=(tiles,),
        in_specs=[
            pl.BlockSpec(memory_space=pltpu.SMEM),
            by_head,
            by_head,
            by_tile,
            pl.BlockSpec((1, 8, lanes), lambda t: (t, 0, 0)),
            whole((length, LANES)),
            pl.BlockSpec((8, QUERY_TILE), lambda t: (0, t)),
            *unread(tokens),
        ],
        out_specs=[by_tile, whole((length, LANES))],
        out_shape=[
            jax.ShapeDtypeStruct((rows, width), F32),
            jax.ShapeDtypeStruct((length, LANES), BF16),
        ],
        scratch_shapes=[
            pltpu.VMEM((2 * lanes, LANES), BF16),
            pltpu.VMEM((length, LANES), F32),
            pltpu.VMEM((LANES, lanes), F32),
        ],
        compiler_params=params("arbitrary"),
        cost_estimate=lasting(26),
        name="attend_back",
    )(scalars, q, grad, norm, lse, kv, doc_row, *tokens)


def turn_lanes(x, cosine, sine):
    half = HEAD_SIZE // 2
    former = iota(x.shape, 1) % HEAD_SIZE < half
    other = jnp.where(former, -pltpu.roll(x, LANES - half, 1), pltpu.roll(x, half, 1))
    return x * cosine + other * sine


def rope_kernel(q_in_ref, kv_in_ref, cos_ref, sin_ref, q_ref, kv0_ref, kv1_ref):
    cosine, sine = cos_ref[...], sin_ref[...]
    scale = 1.0 / math.sqrt(HEAD_SIZE)
    for i in range(QUERY_HEADS * HEAD_SIZE // LANES):
        turned = turn_lanes(q_in_ref[:, tile(i)], cosine, sine).astype(BF16)
        q_ref[:, tile(i)] = (turned.astype(F32) * scale).astype(BF16)
    keys = turn_lanes(kv_in_ref[:, tile(0)], cosine, sine)
    values = kv_in_ref[:, tile(1)]
    low = iota(keys.shape, 1) < HEAD_SIZE
    kv0_ref[...] = jnp.where(low, keys, half_roll(values)).astype(BF16)
    kv1_ref[...] = jnp.where(low, half_roll(keys), values).astype(BF16)


def rope(q_raw, kv_raw, cosine, sine):
    rows = q_raw.shape[0]
    return pl.pallas_call(
        rope_kernel,
        out_shape=[
            jax.ShapeDtypeStruct((rows, QUERY_HEADS * HEAD_SIZE), BF16),
            jax.ShapeDtypeStruct((rows, LANES), BF16),
            jax.ShapeDtypeStruct((rows, LANES), BF16),
        ],
        compiler_params=pltpu.CompilerParams(vmem_limit_bytes=VMEM_LIMIT),
        cost_estimate=lasting(3),
        name="rope",
    )(q_raw, kv_raw, cosine, sine)


def rope_back_kernel(dq0_ref, dq1_ref, dkv0_ref, dkv1_ref, cos_ref, sin_ref, grad_ref):
    cosine, sine = cos_ref[...], -sin_ref[...]
    for head, dq_ref in enumerate((dq0_ref, dq1_ref)):
        for i in range(2):
            turned = turn_lanes(dq_ref[:, tile(i)], cosine, sine)
            grad_ref[:, tile(2 * head + i)] = turned.astype(BF16)
    first = dkv0_ref[...].astype(F32)
    second = dkv1_ref[...].astype(F32)
    low = iota(first.shape, 1) < HEAD_SIZE
    keys = jnp.where(low, first, half_roll(second))
    values = jnp.where(low, half_roll(first), second)
    grad_ref[:, tile(4)] = turn_lanes(keys, cosine, sine).astype(BF16)
    grad_ref[:, tile(5)] = values.astype(BF16)


def rope_back(dq0, dq1, dkv0, dkv1, cosine, sine):
    rows = dq0.shape[0]
    return pl.pallas_call(
        rope_back_kernel,
        out_shape=jax.ShapeDtypeStruct(
            (rows, QUERY_HEADS * HEAD_SIZE + KEY_VALUE_HEADS * LANES), BF16
        ),
        compiler_params=pltpu.CompilerParams(vmem_limit_bytes=VMEM_LIMIT),
        cost_estimate=lasting(3),
        name="rope_back",
    )(dq0, dq1, dkv0, dkv1, cosine, sine)


DEVICES = ("ctx", "fsdp")


def swap(block, axis, bit):
    count, width = lax.axis_size("ctx"), lax.axis_size("fsdp")
    partner = lambda c, f: (c ^ bit) * width + f if axis == "ctx" else c * width + (f ^ bit)
    route = [(c * width + f, partner(c, f)) for c in range(count) for f in range(width)]
    return lax.ppermute(block, DEVICES, route)


def take_rows(block, index, rows):
    return lax.dynamic_slice_in_dim(block, index * rows, rows, 0)


def after_kernel(*refs):
    pass


def after(block, *others):
    return pl.pallas_call(
        after_kernel,
        in_specs=[pl.BlockSpec(memory_space=pl.ANY)] * (1 + len(others)),
        out_specs=pl.BlockSpec(memory_space=pl.ANY),
        out_shape=jax.ShapeDtypeStruct(block.shape, block.dtype),
        input_output_aliases={0: 0},
        name="after",
    )(block, *others)


def place_kernel(parts, tokens, at_ref, *refs):
    count = 1 + max(part[0] for part in parts)
    outs = 1 + max(part[5] for part in parts)
    pieces, refs = refs[:count], refs[count + tokens :]
    out_refs, held = refs[:outs], refs[outs:-1]
    sems = refs[-1]
    come = [pltpu.make_async_copy(pieces[i], held[i], sems.at[i]) for i in range(count)]
    for copy in come:
        copy.start()
    leave = []
    for i in range(count):
        come[i].wait()
        for k, (piece, row, rows, col, cols, out) in enumerate(parts):
            if piece == i:
                here = held[i].at[pl.ds(row, rows), pl.ds(col, cols)]
                to = out_refs[out].at[pl.ds(pl.multiple_of(at_ref[k], 16), rows), :]
                leave.append(pltpu.make_async_copy(here, to, sems.at[count + k]))
                leave[-1].start()
    for copy in leave:
        copy.wait()


def place(pieces, parts, offsets, shapes, tokens=()):
    size = sum(math.prod(piece.shape) for piece in pieces) * 4
    return pl.pallas_call(
        functools.partial(place_kernel, tuple(parts), len(tokens)),
        in_specs=[pl.BlockSpec(memory_space=pltpu.SMEM)]
        + [pl.BlockSpec(memory_space=pl.ANY)] * (len(pieces) + len(tokens)),
        out_specs=[pl.BlockSpec(memory_space=pl.ANY)] * len(shapes),
        out_shape=[jax.ShapeDtypeStruct(shape, BF16) for shape in shapes],
        scratch_shapes=[pltpu.VMEM(piece.shape, BF16) for piece in pieces]
        + [pltpu.SemaphoreType.DMA((len(pieces) + len(parts),))],
        compiler_params=pltpu.CompilerParams(vmem_limit_bytes=VMEM_LIMIT),
        cost_estimate=lasting(1 + size / 3e6),
        name="place",
    )(jnp.stack(offsets).astype(jnp.int32), *pieces, *tokens)


def move(block, axis, bit, start=(), arrive=()):
    sent = after(block, *start) if start else block
    got = swap(sent, axis, bit)
    return sent, after(got, *arrive) if arrive else got


def send_x(shard, extra=0):
    side = lax.axis_index("ctx") % 2
    rows = shard.shape[0] - extra
    sent = take_rows(shard[:rows], side, rows // 2)
    return jnp.concatenate([sent, shard[rows:]], axis=0) if extra else sent


def collect(shard, near, extra=0, arrive=()):
    rank, ranks = lax.axis_index("fsdp"), lax.axis_size("fsdp")
    side = lax.axis_index("ctx") % 2
    rows, width = shard.shape[0] - extra, shard.shape[1]
    half = rows // 2
    _, far = move(near[:half] if extra else near, "ctx", 1, (), arrive)
    _, near_other = move(near, "fsdp", 1, (), arrive)
    pieces = [shard, swap(shard, "fsdp", 1), near, near_other, far, swap(far, "fsdp", 1)]
    whose = [rank, rank ^ 1, rank ^ 2, rank ^ 3, rank ^ 2, rank ^ 3]
    parts, offsets = [], []
    for k in range(6):
        size = rows if k < 2 else half
        parts.append((k, 0, size, 0, width, 0))
        offsets.append(whose[k] * rows + (0, 0, side, side, 1 - side, 1 - side)[k] * half)
        if extra and k < 4:
            parts.append((k, size, extra, 0, width, 1))
            offsets.append(whose[k] * extra)
    shapes = [(ranks * rows, width)] + ([(ranks * extra, width)] if extra else [])
    return place(pieces, parts, offsets, shapes)


def collect_whole(shard, other, near, columns, tokens=(), arrive=()):
    rank, ranks = lax.axis_index("fsdp"), lax.axis_size("fsdp")
    rows = shard.shape[0]
    pieces = [shard, other, near, move(near, "fsdp", 1, (), arrive)[1]]
    parts, offsets, shapes = [], [], {}
    for k, piece in enumerate((0, 1, 2, 3)):
        at = 0
        for width, out, shard_rows, first in columns:
            parts.append((piece, 0, rows, at, width, out))
            offsets.append((rank ^ k) * shard_rows + first)
            shapes[out] = (ranks * shard_rows, width)
            at += width
    return place(pieces, parts, offsets, [shapes[out] for out in sorted(shapes)], tokens)


def own_order(block):
    rank = lax.axis_index("fsdp")
    width = block.shape[1] // 4
    return [lax.dynamic_slice_in_dim(block, (rank ^ k) * width, width, 1) for k in (0, 2, 1, 3)]


class Reduction:
    def __init__(self, left, grad, more=None):
        self.left, self.grad, self.more = left, grad, more
        _, _, by_core, by_both = left
        sent = dot_tn(jnp.concatenate([by_core, by_both], axis=1), grad)
        if more:
            sent = sent + jnp.concatenate(more[2:], axis=0)
        self.sent, self.got = move(sent.astype(BF16), "fsdp", 1)

    def over_x(self, start=(), arrive=()):
        own, by_x, _, _ = self.left
        rows = own.shape[1]
        self.near = self.got[:rows]
        sent = dot_tn(by_x, self.grad) + self.got[rows:].astype(F32)
        if self.more:
            sent = sent + self.more[1]
        sent = sent.astype(BF16)
        self.sent, self.got = move(sent, "fsdp", 2, start, arrive)

    def halve(self, bit, start, arrive):
        side = (lax.axis_index("ctx") // bit) % 2
        half = self.own.shape[0] // 2
        self.kept = take_rows(self.own, side, half)
        sent = take_rows(self.own, 1 - side, half).astype(BF16)
        self.sent, self.got = move(sent, "ctx", bit, start, arrive)

    def add_x(self):
        self.own = dot_tn(self.left[0], self.grad) + self.near.astype(F32) + self.got.astype(F32)
        if self.more:
            self.own = self.own + self.more[0]

    def over_y(self, start=(), arrive=()):
        self.add_x()
        self.halve(1, start, arrive)

    def over_z(self, start=(), arrive=()):
        self.own = self.kept + self.got.astype(F32)
        self.halve(2, start, arrive)

    def rest(self, start=(), arrive=()):
        self.own = (self.kept + self.got.astype(F32)).astype(BF16)
        bit = 4
        while bit < lax.axis_size("ctx"):
            self.sent, self.got = move(self.own, "ctx", bit, start, arrive)
            self.own = (self.own.astype(F32) + self.got.astype(F32)).astype(BF16)
            bit *= 2

    def join(self, bit, start=()):
        side = (lax.axis_index("ctx") // bit) % 2
        self.sent, other = move(self.own, "ctx", bit, start)
        self.own = jnp.concatenate(
            [jnp.where(side == 0, self.own, other), jnp.where(side == 0, other, self.own)], axis=0
        )

    def result(self, z_start=(), y_start=()):
        self.join(2, z_start)
        self.join(1, y_start)
        return self.own.astype(F32)


def ctx_bits():
    bits = [1]
    while 2 * bits[-1] < lax.axis_size("ctx"):
        bits.append(2 * bits[-1])
    return bits


def spread_order():
    apart = jnp.arange(lax.axis_size("ctx"), dtype=jnp.int32) ^ lax.axis_index("ctx")
    where = jnp.zeros_like(apart)
    for k, bit in enumerate(reversed(ctx_bits())):
        where += ((apart // bit) % 2) << k
    return where


class Spread:
    def __init__(self, block):
        self.block, self.bits = block, ctx_bits()

    def step(self, arrive=()):
        _, got = move(self.block, "ctx", self.bits.pop(), (), arrive)
        self.block = jnp.concatenate([self.block, got], axis=0)

    def finish(self, arrive=()):
        while self.bits:
            self.step(arrive)
        return self.block


class BlockSums:
    def __init__(self, blocks):
        self.blocks, self.bits = blocks, ctx_bits()

    def step(self, start=(), arrive=()):
        half = self.blocks.shape[0] // 2
        bit = self.bits.pop(0)
        self.sent, got = move(self.blocks[half:], "ctx", bit, start, arrive)
        self.blocks = (self.blocks[:half].astype(F32) + got.astype(F32)).astype(BF16)

    def finish(self, start=()):
        while self.bits:
            self.step(start)
        return self.blocks


def stretches_of(shapes, rows):
    found, at = [], 0
    for index, (height, width) in enumerate(shapes):
        for first in range(0, height, rows):
            found.append((index, first, at))
            at += width
    return found, at


def split_kernel(count, side_ref, *refs):
    owns, (kept_ref, sent_ref) = refs[:count], refs[count:]
    half = kept_ref.shape[0]
    found, _ = stretches_of([own.shape for own in owns], 2 * half)
    mine = pl.multiple_of(side_ref[0] * half, half)
    theirs = pl.multiple_of((1 - side_ref[0]) * half, half)
    for index, first, at in found:
        own = owns[index]
        columns = slice(at, at + own.shape[1])
        kept_ref[:, columns] = own[pl.ds(first + mine, half), :]
        sent_ref[:, columns] = own[pl.ds(first + theirs, half), :]


def split_pack(side, owns):
    rows = min(own.shape[0] for own in owns)
    _, width = stretches_of([own.shape for own in owns], rows)
    shape = (rows // 2, width)
    return pl.pallas_call(
        functools.partial(split_kernel, len(owns)),
        in_specs=[pl.BlockSpec(memory_space=pltpu.SMEM)] + [whole(own.shape) for own in owns],
        out_specs=[whole(shape)] * 2,
        out_shape=[jax.ShapeDtypeStruct(shape, BF16)] * 2,
        compiler_params=pltpu.CompilerParams(vmem_limit_bytes=VMEM_LIMIT),
        cost_estimate=lasting(3),
        name="split",
    )(side.reshape(1), *owns)


def fold_kernel(side_ref, kept_ref, got_ref, new_ref, sent_ref):
    half = new_ref.shape[0]
    mine = pl.ds(pl.multiple_of(side_ref[0] * half, half), half)
    theirs = pl.ds(pl.multiple_of((1 - side_ref[0]) * half, half), half)
    new_ref[...] = (kept_ref[mine, :].astype(F32) + got_ref[mine, :].astype(F32)).astype(BF16)
    sent_ref[...] = (kept_ref[theirs, :].astype(F32) + got_ref[theirs, :].astype(F32)).astype(BF16)


def fold_pack(side, kept, got):
    shape = (kept.shape[0] // 2, kept.shape[1])
    return pl.pallas_call(
        fold_kernel,
        in_specs=[pl.BlockSpec(memory_space=pltpu.SMEM)] + [whole(kept.shape)] * 2,
        out_specs=[whole(shape)] * 2,
        out_shape=[jax.ShapeDtypeStruct(shape, BF16)] * 2,
        compiler_params=pltpu.CompilerParams(vmem_limit_bytes=VMEM_LIMIT),
        cost_estimate=lasting(2),
        name="fold",
    )(side.reshape(1), kept, got)


def join_kernel(side_ref, own_ref, got_ref, out_ref):
    half = own_ref.shape[0]
    out_ref[pl.ds(pl.multiple_of(side_ref[0] * half, half), half), :] = own_ref[...]
    out_ref[pl.ds(pl.multiple_of((1 - side_ref[0]) * half, half), half), :] = got_ref[...]


def join_pack(side, own, got):
    shape = (2 * own.shape[0], own.shape[1])
    return pl.pallas_call(
        join_kernel,
        in_specs=[pl.BlockSpec(memory_space=pltpu.SMEM)] + [whole(own.shape)] * 2,
        out_specs=whole(shape),
        out_shape=jax.ShapeDtypeStruct(shape, BF16),
        compiler_params=pltpu.CompilerParams(vmem_limit_bytes=VMEM_LIMIT),
        cost_estimate=lasting(2),
        name="join",
    )(side.reshape(1), own, got)


def unpack_kernel(parts, side_ref, own_ref, got_ref, *out_refs):
    half = own_ref.shape[0]
    mine = pl.multiple_of(side_ref[0] * half, half)
    theirs = pl.multiple_of((1 - side_ref[0]) * half, half)
    for out, first, at, skip, width in parts:
        columns = slice(at, at + width)
        to = slice(skip, skip + width)
        out_refs[out][pl.ds(first + mine, half), to] = own_ref[:, columns].astype(F32)
        out_refs[out][pl.ds(first + theirs, half), to] = got_ref[:, columns].astype(F32)


def unpack(side, own, got, shapes):
    rows = 2 * own.shape[0]
    found, _ = stretches_of(shapes, rows)
    parts = [(index, first, at, 0, shapes[index][1]) for index, first, at in found]
    return pl.pallas_call(
        functools.partial(unpack_kernel, parts),
        in_specs=[pl.BlockSpec(memory_space=pltpu.SMEM)] + [whole(own.shape)] * 2,
        out_specs=[whole(shape) for shape in shapes],
        out_shape=[jax.ShapeDtypeStruct(shape, F32) for shape in shapes],
        compiler_params=pltpu.CompilerParams(vmem_limit_bytes=VMEM_LIMIT),
        cost_estimate=lasting(4),
        name="unpack",
    )(side.reshape(1), own, got)


class Pack:
    def __init__(self, owns):
        self.shapes = [own.shape for own in owns]
        self.owns = owns

    def side(self, bit):
        return (lax.axis_index("ctx") // bit) % 2

    def over_y(self, start=(), arrive=()):
        self.kept, sent = split_pack(self.side(1), self.owns)
        self.sent, self.got = move(sent, "ctx", 1, start, arrive)

    def over_z(self, start=(), arrive=()):
        self.kept, sent = fold_pack(self.side(2), self.kept, self.got)
        self.sent, self.got = move(sent, "ctx", 2, start, arrive)

    def rest(self, start=(), arrive=()):
        self.own = (self.kept.astype(F32) + self.got.astype(F32)).astype(BF16)
        for bit in ctx_bits()[2:]:
            self.sent, self.got = move(self.own, "ctx", bit, start, arrive)
            self.own = (self.own.astype(F32) + self.got.astype(F32)).astype(BF16)

    def back_z(self, start=(), arrive=()):
        self.sent, got = move(self.own, "ctx", 2, start, arrive)
        self.own = join_pack(self.side(2), self.own, got)

    def back_y(self, start=(), arrive=()):
        self.sent, got = move(self.own, "ctx", 1, start, arrive)
        return unpack(self.side(1), self.own, got, self.shapes)


def shift_along(block, axis, distance):
    devices = range(lax.axis_size(axis))
    route = [(i - distance, i) for i in devices if i - distance in devices]
    return lax.ppermute(block, axis, route)


def segment_starts(positions, starts):
    reached = starts[None, :] <= positions[:, None]
    return jnp.max(jnp.where(reached, starts[None, :], -1), axis=1)


class Scan:
    def __init__(self, own, send, upwards):
        shape = (MESSAGE_ROWS, MAMBA_INNER)
        self.own, self.send, self.upwards = own, send, upwards
        factor_row = lax.broadcasted_iota(jnp.int32, shape, 0) >= STATE_SIZE
        self.seen = factor_row.astype(F32)
        self.bits = ctx_bits()

    def step(self, arrive=()):
        bit = self.bits.pop(0)
        above = (lax.axis_index("ctx") // bit) % 2 == 1
        _, got = move(self.send, "ctx", bit, (), arrive)
        first = above if self.upwards else jnp.logical_not(above)
        self.own, self.send, self.seen = scan_step(first, self.own, self.seen, got)
        return self.send

    def finish(self, arrive=()):
        while self.bits:
            self.step(arrive)
        return self.seen


def outer_sum(left, right):
    return dot_tn(left, right)


def time_steps(left, right):
    return dot_nt(left, right)


def local(
    tokens,
    cotangent,
    doc_starts,
    gain_mix,
    w_z,
    w_xbc,
    w_dt,
    conv_w,
    conv_b,
    dt_bias,
    a_log,
    skip_factor,
    w_mo,
    w_q,
    key_value_weight,
    w_o,
    gain_ffn,
    w_gate,
    w_up,
    w_down,
):
    xbc_dt = jnp.pad(
        jnp.concatenate([w_xbc, w_dt], axis=1), ((0, 0), (0, LANES - MAMBA_HEADS))
    )
    small = jnp.concatenate(
        [v.reshape(-1) for v in (gain_mix, conv_w, conv_b, dt_bias, a_log, skip_factor, gain_ffn)]
    )
    wide = w_q.shape[1] + key_value_weight.shape[1]
    small_rows = 16
    small = jnp.pad(small, (0, small_rows * wide - small.shape[0])).reshape(small_rows, wide)
    shard_qkv = jnp.concatenate([jnp.concatenate([w_q, key_value_weight], axis=1), small], axis=0)
    near_qkv = swap(send_x(shard_qkv, small_rows), "fsdp", 2)
    near_xbc = swap(send_x(xbc_dt), "fsdp", 2)
    side_by_side = lambda w, rows: [w[i : i + rows] for i in range(0, w.shape[0], rows)]
    rows_in = w_z.shape[0]
    shard_omo = jnp.concatenate([w_o, w_mo], axis=0)
    shard_zo = jnp.concatenate([w_z] + side_by_side(shard_omo, rows_in), axis=1)
    shard_gate_up = jnp.concatenate([w_gate, w_up], axis=1)
    sent_zo = after(shard_zo, near_qkv)
    near_zo = swap(sent_zo, "fsdp", 2)
    sent_gate_up = after(shard_gate_up, near_xbc)
    near_gate_up = swap(sent_gate_up, "fsdp", 2)
    sent_down = after(w_down, near_zo)
    near_down = swap(sent_down, "fsdp", 2)
    full_qkv, small_all = collect(shard_qkv, near_qkv, small_rows)
    model = w_down.shape[1]

    def stretches(out, shard_rows):
        return [(model, out, shard_rows, first) for first in range(0, shard_rows, rows_in)]

    ranks = lax.axis_size("fsdp")
    small_all = small_all.reshape(ranks, -1).astype(F32)
    at = [0]

    def unpack(rows, width):
        part = small_all[:, at[0] : at[0] + rows * width].reshape(-1, rows, width)
        at[0] += rows * width
        return part.transpose(1, 0, 2).reshape(rows, -1)

    full_gain_mix = unpack(1, gain_mix.shape[0])[0]
    full_conv_w = unpack(CONV, conv_b.shape[0])
    full_conv_b = unpack(1, conv_b.shape[0])[0]
    full_dt_bias = unpack(1, dt_bias.shape[0])[0]
    full_a_log = unpack(1, dt_bias.shape[0])[0]
    full_skip = unpack(1, dt_bias.shape[0])[0]
    full_gain_ffn = unpack(1, gain_ffn.shape[0])[0]
    o_rows = w_o.shape[0]
    wide_in = xbc_dt.shape[1]
    ctx_rank = lax.axis_index("ctx")
    inputs = tokens[0].astype(F32)
    rows = inputs.shape[0]
    starts = doc_starts[0]
    base = ctx_rank * rows
    positions = base + jnp.arange(rows, dtype=jnp.int32)
    doc = segment_starts(positions, starts)
    doc_col = jnp.pad(doc, (0, 8))[:, None]
    doc_row = jnp.broadcast_to(doc[None, :], (8, rows))
    scalars = jnp.concatenate([doc[CHUNK - 1 :: CHUNK], base[None]])
    attn_scalars = jnp.concatenate(
        [doc[::QUERY_TILE], doc[QUERY_TILE - 1 :: QUERY_TILE], base[None], spread_order()]
    )
    half = HEAD_SIZE // 2
    freqs = ROPE_BASE ** (
        -2.0 * (jnp.arange(LANES, dtype=jnp.int32) % half).astype(F32) / HEAD_SIZE
    )
    angles = positions.astype(F32)[:, None] * freqs[None, :]
    cosine, sine = jnp.cos(angles), jnp.sin(angles)
    conv_pack = jnp.pad(
        jnp.concatenate([full_conv_w, full_conv_b[None]], axis=0), ((0, 3), (0, 0))
    )
    pad_heads = lambda v: jnp.pad(v, (0, LANES - MAMBA_HEADS))[None]
    head_pack = jnp.concatenate(
        [pad_heads(full_dt_bias), pad_heads(-jnp.exp(full_a_log)), jnp.zeros((6, LANES), F32)], axis=0
    )
    skip_wide = jnp.repeat(full_skip, MAMBA_HEAD_SIZE)[None]

    scale_one = lax.rsqrt(jnp.mean(inputs * inputs, axis=-1, keepdims=True) + EPSILON)
    normed = (inputs * scale_one * full_gain_mix[None, :]).astype(BF16)
    q_width = QUERY_HEADS * HEAD_SIZE
    qkv_raw = dot_nn(normed, full_qkv)
    query, kv_first, kv_second = rope(
        qkv_raw[:, :q_width], qkv_raw[:, q_width:], cosine, sine
    )
    spreads = [Spread(kv) for kv in (kv_first, kv_second)]
    full_xbc = collect(xbc_dt, near_xbc, 0, [query])[0]
    for spread_kv in spreads:
        spread_kv.step()
        spread_kv.step([full_xbc])
    mixed_in = dot_nn(normed, full_xbc[:, :CHANNELS]).astype(BF16)
    dt_raw = dot_nn(normed, full_xbc[:, CHANNELS:])
    edge = shift_along(mixed_in[rows - 8 :], "ctx", 1).astype(F32)
    y_local, state_local, message, own_state, decay, c_mat = mamba_forward(
        scalars, edge, mixed_in, dt_raw, doc_col[:rows], conv_pack, head_pack, skip_wide
    )
    kv_all = [spread_kv.finish([message]) for spread_kv in spreads]
    scan = Scan(own_state, message, True)
    tokens = [message, sent_gate_up, sent_down]
    attended = [attend(attn_scalars, query, kv_all[0], doc_row, 0, tokens)]
    first_done = attended[0][0]
    other_zo, other_gate_up, other_down = [
        move(shard, "fsdp", 1, (), [first_done])[1] for shard in (shard_zo, shard_gate_up, w_down)
    ]
    tokens = [scan.step([first_done]), first_done, other_zo, other_gate_up, other_down]
    attended.append(attend(attn_scalars, query, kv_all[1], doc_row, 1, tokens))
    second_done = attended[1][0]
    scan.step([second_done])
    full_z, full_omo = collect_whole(
        shard_zo,
        other_zo,
        near_zo,
        [(w_z.shape[1], 0, rows_in, 0)] + stretches(1, shard_omo.shape[0]),
        [second_done],
        [first_done],
    )
    gate_z = dot_nn(normed, full_z)
    full_gate_up = collect_whole(
        shard_gate_up,
        other_gate_up,
        after(near_gate_up, second_done),
        [(2 * w_gate.shape[1], 0, rows_in, 0)],
        [second_done],
        [second_done],
    )[0]
    state_in = scan.finish([gate_z, full_gate_up])
    full_down = collect_whole(
        w_down,
        other_down,
        after(near_down, second_done),
        [(model, 0, w_down.shape[0], 0)],
    )[0]
    y_total, both, state_true = mamba_correct(
        y_local, state_local, c_mat, decay, state_in, gate_z, attended[0][0], attended[1][0]
    )
    hidden = inputs + dot_nn(both, full_omo)
    gain_two = full_gain_ffn
    scale_two = lax.rsqrt(jnp.mean(hidden * hidden, axis=-1, keepdims=True) + EPSILON)
    normed_ffn = (hidden * scale_two * gain_two[None, :]).astype(BF16)
    gate_up = dot_nn(normed_ffn, full_gate_up)
    ff = gate_up.shape[1] // 2
    gate, upper = gate_up[:, :ff], gate_up[:, ff:]
    sig_gate = jax.nn.sigmoid(gate)
    silu_gate = gate * sig_gate
    activ = (silu_gate * upper).astype(BF16)
    result = hidden + dot_nn(activ, full_down)

    grad_out = cotangent[0]
    down = Reduction(own_order(activ), grad_out)
    grad_act = time_steps(grad_out, full_down)
    grad_gate = (grad_act * upper * sig_gate * (1.0 + gate * (1.0 - sig_gate))).astype(BF16)
    grad_up = (grad_act * silu_gate).astype(BF16)
    grad_gate_up = jnp.concatenate([grad_gate, grad_up], axis=1)
    gate_up_sum = Reduction(own_order(normed_ffn), grad_gate_up)
    down.over_x()
    grad_n2 = time_steps(grad_gate_up, full_gate_up)
    scaled_two = grad_n2 * gain_two[None, :]
    grad_hidden = (
        grad_out.astype(F32)
        + scale_two * scaled_two
        - hidden * scale_two**3 * jnp.mean(scaled_two * hidden, axis=-1, keepdims=True)
    )
    grad_hid_b = grad_hidden.astype(BF16)
    gate_up_sum.over_x()
    both_grad = time_steps(grad_hid_b, full_omo)
    grad_y, grad_z, own_grad, grad_message, grad_attn = mamba_gate_back(
        both_grad, gate_z, y_total, c_mat, decay, own_state, [down.sent, gate_up_sum.sent]
    )
    omo = Reduction(own_order(both), grad_hid_b)
    left_mix = own_order(normed)
    z_sum = Reduction(left_mix, grad_z)
    scan = Scan(own_grad, grad_message, False)
    backs = []

    def back(j, tokens):
        backs.append(
            attend_back(
                attn_scalars,
                query,
                grad_attn,
                attended[j][1],
                attended[j][2],
                kv_all[j],
                doc_row,
                j,
                tokens,
            )
        )

    grad_n1_z = time_steps(grad_z, full_z)
    first_send = scan.step()
    back(0, [first_send, omo.sent, z_sum.sent, grad_n1_z])
    first_done = backs[0][0]
    for part in (down, gate_up_sum, omo, z_sum):
        part.got = after(part.got, first_done)
    second_send = scan.step([first_done])
    down.add_x()
    gate_up_sum.add_x()
    ffn = Pack([gate_up_sum.own.astype(BF16), down.own.astype(BF16)])
    ffn.over_y()
    omo.over_x()
    z_sum.over_x()
    kv_sums = [BlockSums(backs[0][1])]
    back(1, [second_send, ffn.sent, omo.sent, z_sum.sent, first_done])
    second_done = backs[1][0]
    for part in (ffn, omo, z_sum):
        part.got = after(part.got, second_done)
    kv_sums[0].step((), [second_done])
    state_grad = scan.finish([second_done])
    ffn.over_z()
    omo.add_x()
    z_sum.add_x()
    mixer = Pack([z_sum.own.astype(BF16), omo.own.astype(BF16)])
    mixer.over_y()
    kv_sums.append(BlockSums(backs[1][1]))
    grad_mixed, tail, edge_grad, grad_dt, grad_conv, grad_heads = mamba_back(
        scalars,
        edge,
        mixed_in,
        dt_raw,
        doc_col,
        doc_row,
        conv_pack,
        head_pack,
        skip_wide,
        grad_y,
        y_total,
        state_true,
        state_grad,
        [ffn.sent, mixer.sent, kv_sums[0].blocks],
    )
    behind = shift_along(edge_grad, "ctx", -1)
    grad_mixed = grad_mixed.at[rows - 8 :].set((tail + behind).astype(BF16))
    third_done = grad_dt
    for part in (ffn, mixer):
        part.got = after(part.got, third_done)
    kv_sums[1].step((), [third_done])
    kv_both = BlockSums(jnp.concatenate([part.blocks for part in kv_sums], axis=1))
    kv_both.bits = kv_sums[0].bits
    grad_xbc = jnp.concatenate([grad_mixed, grad_dt], axis=1)
    fsdp_rank = lax.axis_index("fsdp")
    conv_width, heads_width = conv_b.shape[0], dt_bias.shape[0]
    small_width = -(-(conv_width * (CONV + 1) + heads_width * 3) // rows_in)
    small_at = CHANNELS + MAMBA_HEADS
    blocks = [
        g.reshape(g.shape[0], ranks, -1).transpose(1, 0, 2).reshape(ranks, -1)
        for g in (grad_conv[: CONV + 1], grad_heads[:3, :MAMBA_HEADS])
    ]
    small_grad = jnp.concatenate(blocks, axis=1)
    small_count = small_grad.shape[1]
    small_grad = jnp.pad(small_grad, ((0, 0), (0, small_width * rows_in - small_count)))
    small_grad = jnp.pad(
        small_grad.reshape(ranks, rows_in, small_width),
        ((0, 0), (0, 0), (small_at, wide_in - small_at - small_width)),
    )
    more = [lax.dynamic_index_in_dim(small_grad, fsdp_rank ^ k, 0, False) for k in (0, 2, 1, 3)]
    xbc_sum = Reduction(left_mix, grad_xbc, more)
    xbc_sum.over_x()
    x_left = [xbc_sum.sent]
    kv_both.step((), x_left)
    ffn.rest((), x_left)
    grad_kv = kv_both.finish()
    grad_qkv = rope_back(
        backs[0][0], backs[1][0], grad_kv[:, :LANES], grad_kv[:, LANES:], cosine, sine
    )
    qkv_sum = Reduction(left_mix, grad_qkv)
    qkv_sum.over_x()
    xbc_sum.add_x()
    qkv_sum.add_x()
    last_own = jnp.concatenate([xbc_sum.own, qkv_sum.own], axis=1).astype(BF16)
    ffn.back_z()
    mixer.over_z(x_left)
    mixer.rest()
    mixer.back_z()
    grad_w_gate_up, grad_w_down = ffn.back_y()
    grad_w_z, grad_w_omo = mixer.back_y()
    last_total = lax.psum(last_own, "ctx").astype(F32)
    grad_w_xbc, grad_w_qkv = last_total[:, :wide_in], last_total[:, wide_in:]
    small_own = grad_w_xbc[:, small_at : small_at + small_width].reshape(-1)[:small_count]
    conv_own = small_own[: conv_width * (CONV + 1)].reshape(CONV + 1, conv_width)
    heads_own = small_own[conv_width * (CONV + 1) :].reshape(3, heads_width)
    grad_n1 = (
        grad_n1_z
        + time_steps(grad_xbc, full_xbc)
        + time_steps(grad_qkv, full_qkv)
    )
    scaled_one = grad_n1 * full_gain_mix[None, :]
    grad_tokens = (
        grad_hidden
        + scale_one * scaled_one
        - inputs * scale_one**3 * jnp.mean(scaled_one * inputs, axis=-1, keepdims=True)
    )
    row_sums = lambda grad, weight: jnp.sum(grad * weight.astype(F32), axis=1)
    grad_gain_ffn = row_sums(
        grad_w_gate_up, jnp.concatenate([w_gate, w_up], axis=1)
    ) / gain_ffn.astype(F32)
    grad_gain_mix = (
        row_sums(grad_w_z, w_z)
        + row_sums(grad_w_xbc, xbc_dt)
        + row_sums(grad_w_qkv, jnp.concatenate([w_q, key_value_weight], axis=1))
    ) / gain_mix.astype(F32)
    totals = (
        grad_gain_mix,
        grad_w_z,
        grad_w_xbc[:, :CHANNELS],
        grad_w_xbc[:, CHANNELS : CHANNELS + MAMBA_HEADS],
        conv_own[:CONV],
        conv_own[CONV],
        heads_own[0],
        heads_own[1],
        heads_own[2],
        grad_w_omo[o_rows:],
        grad_w_qkv[:, :q_width],
        grad_w_qkv[:, q_width:],
        grad_w_omo[:o_rows],
        grad_gain_ffn,
        grad_w_gate_up[:, :ff],
        grad_w_gate_up[:, ff:],
        grad_w_down,
    )
    return (result.astype(BF16)[None], grad_tokens[None]) + totals


def solution(mesh):
    in_specs = (
        P("fsdp", "ctx", None),
        P("fsdp", "ctx", None),
        P("fsdp", None),
        P("fsdp"),
        P("fsdp", None),
        P("fsdp", None),
        P("fsdp", None),
        P(None, "fsdp"),
        P("fsdp"),
        P("fsdp"),
        P("fsdp"),
        P("fsdp"),
        P("fsdp", None),
        P("fsdp", None),
        P("fsdp", None),
        P("fsdp", None),
        P("fsdp"),
        P("fsdp", None),
        P("fsdp", None),
        P("fsdp", None),
    )
    out_specs = (
        P("fsdp", "ctx", None),
        P("fsdp", "ctx", None),
        P("fsdp"),
        P("fsdp", None),
        P("fsdp", None),
        P("fsdp", None),
        P(None, "fsdp"),
        P("fsdp"),
        P("fsdp"),
        P("fsdp"),
        P("fsdp"),
        P("fsdp", None),
        P("fsdp", None),
        P("fsdp", None),
        P("fsdp", None),
        P("fsdp"),
        P("fsdp", None),
        P("fsdp", None),
        P("fsdp", None),
    )
    return jax.shard_map(local, mesh=mesh, in_specs=in_specs, out_specs=out_specs, check_vma=False)
```

```python
import functools
import math

import jax
import jax.numpy as jnp
from jax import lax
from jax.experimental import pallas as pl
from jax.experimental.pallas import tpu as pltpu
from jax.sharding import PartitionSpec as P

MAMBA_HEADS = 24
MAMBA_HEAD_SIZE = 64
STATE_SIZE = 128
CONV = 4
QUERY_HEADS = 8
KEY_VALUE_HEADS = 2
HEAD_SIZE = 64
MAMBA_INNER = MAMBA_HEADS * MAMBA_HEAD_SIZE
CHANNELS = MAMBA_INNER + 2 * STATE_SIZE
LANES = 128
PAIRS = MAMBA_INNER // LANES
CHUNK = 128
KEY_BLOCK = 512
QUERY_TILE = 256
GROUP = QUERY_HEADS // KEY_VALUE_HEADS
MESSAGE_ROWS = STATE_SIZE + 16
VMEM_LIMIT = 56 * 1024 * 1024

EPSILON = 1e-06
ROPE_BASE = 10000.0
MASK_FILLER = -1e30
HIGHEST = lax.Precision.HIGHEST
F32 = jnp.float32
BF16 = jnp.bfloat16


def dot_nn(a, b, precision=None):
    return lax.dot_general(
        a, b, (((1,), (0,)), ((), ())), precision=precision, preferred_element_type=F32
    )


def dot_nt(a, b):
    return lax.dot_general(a, b, (((1,), (1,)), ((), ())), preferred_element_type=F32)


def dot_tn(a, b):
    return lax.dot_general(a, b, (((0,), (0,)), ((), ())), preferred_element_type=F32)


def iota(shape, dim):
    return lax.broadcasted_iota(jnp.int32, shape, dim)


def params(*semantics):
    return pltpu.CompilerParams(dimension_semantics=semantics, vmem_limit_bytes=VMEM_LIMIT)


def lasting(microseconds):
    return pl.CostEstimate(flops=int(microseconds * 1.15e9), bytes_accessed=0, transcendentals=0)


def without(kernel, at, count):
    def body(*refs):
        kernel(*refs[:at], *refs[at + count :])

    return body


def unread(arrays):
    return [pl.BlockSpec(memory_space=pl.ANY)] * len(arrays)


def whole(shape):
    return pl.BlockSpec(shape, lambda *_: (0,) * len(shape))


def low_half(rows):
    return iota((rows, LANES), 1) < MAMBA_HEAD_SIZE


def spread(values, pair, low):
    a = values[:, 2 * pair : 2 * pair + 1]
    b = values[:, 2 * pair + 1 : 2 * pair + 2]
    return jnp.where(low, a, b)


def tile(i):
    return slice(i * LANES, (i + 1) * LANES)


def split_pair(x, low):
    zero = jnp.zeros_like(x)
    return jnp.concatenate([jnp.where(low, x, zero), jnp.where(low, zero, x)], axis=0)


def fill_padded(xs_ref, edge_ref, mixed_ref):
    xs_ref[0:8, :] = edge_ref[...]
    xs_ref[8:, :] = mixed_ref[...].astype(F32)


def lag_masks(positions, doc):
    return [None] + [(positions - lag >= doc).astype(F32) for lag in range(1, CONV)]


def conv_tile(xs_ref, start, i, cw_ref, masks):
    window = xs_ref[pl.ds(start, CHUNK + 8), tile(i)]
    summed = cw_ref[4:5, tile(i)] + cw_ref[3:4, tile(i)] * window[8 : 8 + CHUNK]
    for lag in range(1, CONV):
        shifted = window[8 - lag : 8 - lag + CHUNK]
        summed = summed + cw_ref[3 - lag : 4 - lag, tile(i)] * (shifted * masks[lag])
    return summed


def softplus(v):
    return jnp.maximum(v, 0.0) + jnp.log1p(jnp.exp(-jnp.abs(v)))


def decay_sums(dt_ref, hp_ref):
    raw = dt_ref[...] + hp_ref[0:1, :]
    step = softplus(raw)
    log_decay = step * hp_ref[1:2, :]
    order = iota((CHUNK, CHUNK), 0) >= iota((CHUNK, CHUNK), 1)
    cumul = dot_nn(order.astype(F32), log_decay, HIGHEST)
    return raw, step, log_decay, cumul


def mamba_forward_kernel(
    sc_ref,
    edge_ref,
    mixed_ref,
    dt_ref,
    doc_ref,
    cw_ref,
    hp_ref,
    skip_ref,
    y_ref,
    sin_ref,
    msg_ref,
    own_ref,
    dec_ref,
    c_ref,
    xs_ref,
    xa_ref,
    state_ref,
    carry_ref,
):
    c = pl.program_id(0)
    count = pl.num_programs(0)

    @pl.when(c == 0)
    def _():
        fill_padded(xs_ref, edge_ref, mixed_ref)
        state_ref[...] = jnp.zeros_like(state_ref)
        carry_ref[...] = jnp.zeros_like(carry_ref)

    base = sc_ref[count]
    start = pl.multiple_of(c * CHUNK, CHUNK)
    first = base + start
    end_doc = sc_ref[c]
    doc = doc_ref[...]
    positions = first + iota((CHUNK, 1), 0)
    masks = lag_masks(positions, doc)
    for i in range(CHANNELS // LANES):
        summed = conv_tile(xs_ref, start, i, cw_ref, masks)
        xa_ref[:, tile(i)] = summed * jax.nn.sigmoid(summed)
    _, step, log_decay, cumul = decay_sums(dt_ref, hp_ref)
    cumul_t = cumul.T
    b_mat = xa_ref[:, tile(PAIRS)]
    c_mat = xa_ref[:, tile(PAIRS + 1)].astype(BF16)
    c_ref[...] = c_mat
    couple = dot_nt(c_mat, b_mat.astype(BF16))
    b_turned = b_mat.T.astype(BF16)
    col = first + iota((CHUNK, CHUNK), 1)
    row = first + iota((CHUNK, CHUNK), 0)
    couple = jnp.where((col <= row) & (col >= doc), couple, 0.0)
    carried = (doc < first).astype(F32)
    into = jnp.exp(cumul) * carried
    last = cumul[CHUNK - 1 : CHUNK, :]
    ending = jnp.exp(last - cumul) * (positions >= end_doc).astype(F32)
    keep = jnp.exp(last) * (end_doc < first).astype(F32)
    dec_ref[...] = jnp.where(doc < base, jnp.exp(cumul + carry_ref[0:1, :]), 0.0)
    low = low_half(CHUNK)
    low_row = low_half(1)
    for j in range(PAIRS):
        x = xa_ref[:, tile(j)]
        weighted = x * spread(step, j, low)
        mixing = []
        for h in (2 * j, 2 * j + 1):
            gap = jnp.minimum(cumul[:, h : h + 1] - cumul_t[h : h + 1, :], 0.0)
            mixing.append((couple * jnp.exp(gap)).astype(BF16))
        y = dot_nn(jnp.concatenate(mixing, axis=1), split_pair(weighted.astype(BF16), low))
        state = state_ref[:, tile(j)]
        sin_ref[0, :, tile(j)] = state
        y = y + dot_nn(c_mat, state.astype(BF16)) * spread(into, j, low)
        y_ref[:, tile(j)] = y + skip_ref[0:1, tile(j)] * x
        fresh = dot_nn(b_turned, (weighted * spread(ending, j, low)).astype(BF16))
        state_ref[:, tile(j)] = fresh + state * spread(keep, j, low_row)
    carry_ref[...] = carry_ref[...] + last

    @pl.when(c == count - 1)
    def _():
        msg_ref[0:STATE_SIZE, :] = state_ref[...].astype(BF16)
        own_ref[0:STATE_SIZE, :] = state_ref[...]
        through = jnp.exp(carry_ref[...]) * (end_doc < base).astype(F32)
        low8 = low_half(8)
        for j in range(PAIRS):
            wide = spread(through, j, low8)
            wide = jnp.concatenate([wide, wide], axis=0)
            msg_ref[STATE_SIZE:, tile(j)] = wide.astype(BF16)
            own_ref[STATE_SIZE:, tile(j)] = wide


def mamba_forward(scalars, edge, mixed, dt_raw, doc, conv_pack, head_pack, skip_wide):
    rows = mixed.shape[0]
    count = rows // CHUNK
    by_chunk = lambda width: pl.BlockSpec((CHUNK, width), lambda c: (c, 0))
    return pl.pallas_call(
        mamba_forward_kernel,
        grid=(count,),
        in_specs=[
            pl.BlockSpec(memory_space=pltpu.SMEM),
            whole((8, CHANNELS)),
            whole((rows, CHANNELS)),
            by_chunk(LANES),
            by_chunk(1),
            whole((8, CHANNELS)),
            whole((8, LANES)),
            whole((1, MAMBA_INNER)),
        ],
        out_specs=[
            by_chunk(MAMBA_INNER),
            pl.BlockSpec((1, STATE_SIZE, MAMBA_INNER), lambda c: (c, 0, 0)),
            whole((MESSAGE_ROWS, MAMBA_INNER)),
            whole((MESSAGE_ROWS, MAMBA_INNER)),
            by_chunk(LANES),
            by_chunk(LANES),
        ],
        out_shape=[
            jax.ShapeDtypeStruct((rows, MAMBA_INNER), F32),
            jax.ShapeDtypeStruct((count, STATE_SIZE, MAMBA_INNER), F32),
            jax.ShapeDtypeStruct((MESSAGE_ROWS, MAMBA_INNER), BF16),
            jax.ShapeDtypeStruct((MESSAGE_ROWS, MAMBA_INNER), F32),
            jax.ShapeDtypeStruct((rows, LANES), F32),
            jax.ShapeDtypeStruct((rows, LANES), BF16),
        ],
        scratch_shapes=[
            pltpu.VMEM((rows + 8, CHANNELS), F32),
            pltpu.VMEM((CHUNK, CHANNELS), F32),
            pltpu.VMEM((STATE_SIZE, MAMBA_INNER), F32),
            pltpu.VMEM((8, LANES), F32),
        ],
        compiler_params=params("arbitrary"),
        cost_estimate=lasting(13),
        name="mamba_forward",
    )(scalars, edge, mixed, dt_raw, doc, conv_pack, head_pack, skip_wide)


QUARTERS = 4
BLOCK_TILES = 1 + PAIRS // QUARTERS


def attn_tile(i):
    return tile(i * BLOCK_TILES)


def gated_tile(j):
    per = PAIRS // QUARTERS
    return tile(j // per * BLOCK_TILES + 1 + j % per)


def mamba_correct_kernel(
    y_ref, sin_ref, c_ref, dec_ref, state_ref, z_ref, vec0_ref, vec1_ref, total_ref, both_ref, true_ref, edge_ref
):
    c = pl.program_id(0)

    @pl.when(c == 0)
    def _():
        edge_ref[...] = jnp.ones_like(edge_ref)

    low = low_half(CHUNK)
    low_row = low_half(1)
    decay = dec_ref[...]
    before = edge_ref[0:1, :]
    c_mat = c_ref[...]
    for j in range(PAIRS):
        state = state_ref[:, tile(j)]
        y = y_ref[:, tile(j)] + dot_nn(c_mat, state.astype(BF16)) * spread(decay, j, low)
        total_ref[:, tile(j)] = y
        z = z_ref[:, tile(j)]
        both_ref[:, gated_tile(j)] = (y * (z * jax.nn.sigmoid(z))).astype(BF16)
        true_ref[0, :, tile(j)] = (
            sin_ref[0, :, tile(j)] + state * spread(before, j, low_row)
        ).astype(BF16)
    for i, vec_ref in enumerate((vec0_ref, vec0_ref, vec1_ref, vec1_ref)):
        both_ref[:, attn_tile(i)] = vec_ref[:, tile(i % 2)]
    edge_ref[0:1, :] = decay[CHUNK - 1 : CHUNK, :]


def mamba_correct(y, sin, c_mat, decay, state_in, gate_z, vec0, vec1):
    rows = y.shape[0]
    count = rows // CHUNK
    by_chunk = lambda width: pl.BlockSpec((CHUNK, width), lambda c: (c, 0))
    states = pl.BlockSpec((1, STATE_SIZE, MAMBA_INNER), lambda c: (c, 0, 0))
    return pl.pallas_call(
        mamba_correct_kernel,
        grid=(count,),
        in_specs=[
            by_chunk(MAMBA_INNER),
            states,
            by_chunk(LANES),
            by_chunk(LANES),
            whole((STATE_SIZE, MAMBA_INNER)),
            by_chunk(MAMBA_INNER),
            by_chunk(2 * LANES),
            by_chunk(2 * LANES),
        ],
        out_specs=[by_chunk(MAMBA_INNER), by_chunk(QUARTERS * BLOCK_TILES * LANES), states],
        out_shape=[
            jax.ShapeDtypeStruct((rows, MAMBA_INNER), F32),
            jax.ShapeDtypeStruct((rows, QUARTERS * BLOCK_TILES * LANES), BF16),
            jax.ShapeDtypeStruct((count, STATE_SIZE, MAMBA_INNER), BF16),
        ],
        scratch_shapes=[pltpu.VMEM((8, LANES), F32)],
        compiler_params=params("arbitrary"),
        cost_estimate=lasting(8.5),
        name="mamba_correct",
    )(y, sin, c_mat, decay, state_in, gate_z, vec0, vec1)


def mamba_gate_back_kernel(
    both_ref, z_ref, y_ref, c_ref, dec_ref, own_ref, dy_ref, gz_ref, gsi_ref, gsb_ref, gvec_ref, acc_ref
):
    c = pl.program_id(0)

    @pl.when(c == 0)
    def _():
        acc_ref[...] = jnp.zeros_like(acc_ref)

    low = low_half(CHUNK)
    decay = dec_ref[...]
    c_turned = c_ref[...].astype(F32).T.astype(BF16)
    for j in range(PAIRS):
        z = z_ref[:, tile(j)]
        sig = jax.nn.sigmoid(z)
        silu = z * sig
        grad = both_ref[:, gated_tile(j)]
        gz_ref[:, tile(j)] = (grad * y_ref[:, tile(j)] * (sig + silu * (1.0 - sig))).astype(BF16)
        dy = (grad * silu).astype(BF16)
        dy_ref[:, tile(j)] = dy
        scaled = (dy.astype(F32) * spread(decay, j, low)).astype(BF16)
        acc_ref[:, tile(j)] += dot_nn(c_turned, scaled)
    for i in range(QUARTERS):
        gvec_ref[:, tile(i)] = both_ref[:, attn_tile(i)].astype(BF16)

    @pl.when(c == pl.num_programs(0) - 1)
    def _():
        gsi_ref[0:STATE_SIZE, :] = acc_ref[...]
        gsb_ref[0:STATE_SIZE, :] = acc_ref[...].astype(BF16)
        gsi_ref[STATE_SIZE:, :] = own_ref[...]
        gsb_ref[STATE_SIZE:, :] = own_ref[...].astype(BF16)


def mamba_gate_back(both_grad, gate_z, total, c_mat, decay, own, tokens=()):
    rows = total.shape[0]
    by_chunk = lambda width: pl.BlockSpec((CHUNK, width), lambda c: (c, 0))
    return pl.pallas_call(
        without(mamba_gate_back_kernel, 6, len(tokens)),
        grid=(rows // CHUNK,),
        in_specs=[
            by_chunk(QUARTERS * BLOCK_TILES * LANES),
            by_chunk(MAMBA_INNER),
            by_chunk(MAMBA_INNER),
            by_chunk(LANES),
            by_chunk(LANES),
            pl.BlockSpec((16, MAMBA_INNER), lambda c: (STATE_SIZE // 16, 0)),
            *unread(tokens),
        ],
        out_specs=[
            by_chunk(MAMBA_INNER),
            by_chunk(MAMBA_INNER),
            whole((MESSAGE_ROWS, MAMBA_INNER)),
            whole((MESSAGE_ROWS, MAMBA_INNER)),
            by_chunk(QUARTERS * LANES),
        ],
        out_shape=[
            jax.ShapeDtypeStruct((rows, MAMBA_INNER), BF16),
            jax.ShapeDtypeStruct((rows, MAMBA_INNER), BF16),
            jax.ShapeDtypeStruct((MESSAGE_ROWS, MAMBA_INNER), F32),
            jax.ShapeDtypeStruct((MESSAGE_ROWS, MAMBA_INNER), BF16),
            jax.ShapeDtypeStruct((rows, QUARTERS * LANES), BF16),
        ],
        scratch_shapes=[pltpu.VMEM((STATE_SIZE, MAMBA_INNER), F32)],
        compiler_params=params("arbitrary"),
        cost_estimate=lasting(7.5),
        name="mamba_gate_back",
    )(both_grad, gate_z, total, c_mat, decay, own, *tokens)


def picks(pair):
    channel = iota((LANES, LANES), 0)
    head = iota((LANES, LANES), 1)
    return (head == 2 * pair + channel // MAMBA_HEAD_SIZE).astype(BF16)


def head_sums(product, select):
    high = product.astype(BF16)
    rest = (product - high.astype(F32)).astype(BF16)
    return dot_nn(high, select) + dot_nn(rest, select)


def mamba_back_kernel(
    sc_ref,
    edge_ref,
    mixed_ref,
    dt_ref,
    doc_ref,
    doc_row_ref,
    cw_ref,
    hp_ref,
    skip_ref,
    dy_ref,
    y_ref,
    sin_ref,
    ds_end_ref,
    gmix_ref,
    tail_ref,
    edge_grad_ref,
    gdt_ref,
    gconv_ref,
    ghead_ref,
    xs_ref,
    xa_ref,
    slope_ref,
    grad_ref,
    ds_ref,
    rows_ref,
):
    step_at = pl.program_id(0)
    count = pl.num_programs(0)
    c = count - 1 - step_at
    rows = count * CHUNK

    @pl.when(step_at == 0)
    def _():
        fill_padded(xs_ref, edge_ref, mixed_ref)
        ds_ref[...] = ds_end_ref[...]
        grad_ref[pl.ds(rows, 8), :] = jnp.zeros((8, CHANNELS), F32)
        gconv_ref[...] = jnp.zeros_like(gconv_ref)
        ghead_ref[...] = jnp.zeros_like(ghead_ref)
        rows_ref[...] = jnp.zeros_like(rows_ref)

    base = sc_ref[count]
    start = pl.multiple_of(c * CHUNK, CHUNK)
    first = base + start
    end_doc = sc_ref[c]
    doc_window = doc_ref[pl.ds(start, CHUNK + 8), :]
    doc = doc_window[0:CHUNK]
    positions_window = first + iota((CHUNK + 8, 1), 0)
    positions = positions_window[0:CHUNK]
    masks_window = lag_masks(positions_window, doc_window)
    masks = [None] + [m[0:CHUNK] for m in masks_window[1:]]
    for i in range(CHANNELS // LANES):
        summed = conv_tile(xs_ref, start, i, cw_ref, masks)
        sig = jax.nn.sigmoid(summed)
        act = summed * sig
        xa_ref[:, tile(i)] = act
        slope_ref[:, tile(i)] = sig + act * (1.0 - sig)
    raw, step, log_decay, cumul = decay_sums(dt_ref, hp_ref)
    cumul_t = cumul.T
    b_mat = xa_ref[:, tile(PAIRS)].astype(BF16)
    c_f32 = xa_ref[:, tile(PAIRS + 1)]
    c_mat = c_f32.astype(BF16)
    c_turned = c_f32.T.astype(BF16)
    key = first + iota((CHUNK, CHUNK), 0)
    query = first + iota((CHUNK, CHUNK), 1)
    visible = (key <= query) & (key >= doc_row_ref[0:1, :])
    couple = jnp.where(visible, dot_nt(b_mat, c_mat), 0.0)
    carried = (doc < first).astype(F32)
    into = jnp.exp(cumul) * carried
    last = cumul[CHUNK - 1 : CHUNK, :]
    ending = jnp.exp(last - cumul) * (positions >= end_doc).astype(F32)
    keep = jnp.exp(last) * (end_doc < first).astype(F32)
    low = low_half(CHUNK)
    low_row = low_half(1)
    grad_couple = jnp.zeros((CHUNK, CHUNK), F32)
    grad_b = jnp.zeros((CHUNK, STATE_SIZE), F32)
    grad_c = jnp.zeros((CHUNK, STATE_SIZE), F32)
    grad_cumul = jnp.zeros((CHUNK, LANES), F32)
    grad_step = jnp.zeros((CHUNK, LANES), F32)
    end_sums = jnp.zeros((8, LANES), F32)
    for j in range(PAIRS):
        select = picks(j)
        x = xa_ref[:, tile(j)]
        step_wide = spread(step, j, low)
        weighted = x * step_wide
        weighted_b = weighted.astype(BF16)
        dy = dy_ref[:, tile(j)]
        dy_f32 = dy.astype(F32)
        grad_mixing = dot_nt(split_pair(weighted_b, low), dy)
        mixing = []
        for side, h in enumerate((2 * j, 2 * j + 1)):
            gap = jnp.minimum(cumul_t[h : h + 1, :] - cumul[:, h : h + 1], 0.0)
            fade = jnp.exp(gap)
            mixing.append((couple * fade).astype(BF16))
            grad_couple += grad_mixing[side * CHUNK : (side + 1) * CHUNK] * fade
        grad_weighted = dot_nn(jnp.concatenate(mixing, axis=1), split_pair(dy, low))
        ending_wide = spread(ending, j, low)
        grad_state = ds_ref[:, tile(j)]
        grad_state_b = grad_state.astype(BF16)
        state = sin_ref[0, :, tile(j)]
        through_state = ending_wide * dot_nn(b_mat, grad_state_b)
        grad_weighted = grad_weighted + through_state
        dy_into = (dy_f32 * spread(into, j, low)).astype(BF16)
        grad_c += dot_nt(dy_into, state)
        grad_b += dot_nt((weighted * ending_wide).astype(BF16), grad_state_b)
        keep_wide = spread(keep, j, low_row)
        weighted_f32 = weighted_b.astype(F32)
        to_end = jnp.sum(weighted_f32 * through_state, axis=0, keepdims=True) + keep_wide * jnp.sum(
            grad_state * state.astype(F32), axis=0, keepdims=True
        )
        ds_ref[:, tile(j)] = keep_wide * grad_state + dot_nn(c_turned, dy_into)
        skip = skip_ref[0:1, tile(j)]
        grad_x = step_wide * grad_weighted + skip * dy_f32
        grad_ref[pl.ds(start, CHUNK), tile(j)] = grad_x * slope_ref[:, tile(j)]
        rows_ref[0:1, tile(j)] += jnp.sum(dy_f32 * x, axis=0, keepdims=True)
        in_out = dy_f32 * (y_ref[:, tile(j)] - skip * x) - weighted_f32 * grad_weighted
        grad_cumul += head_sums(in_out, select)
        grad_step += head_sums(grad_weighted * x, select)
        end_sums += head_sums(jnp.broadcast_to(to_end, (8, LANES)), select)
    grad_couple = jnp.where(visible, grad_couple, 0.0).astype(BF16)
    grad_b += dot_nn(grad_couple, c_mat)
    grad_c += dot_tn(grad_couple, b_mat)
    grad_ref[pl.ds(start, CHUNK), tile(PAIRS)] = grad_b * slope_ref[:, tile(PAIRS)]
    grad_ref[pl.ds(start, CHUNK), tile(PAIRS + 1)] = grad_c * slope_ref[:, tile(PAIRS + 1)]
    later = (iota((CHUNK, CHUNK), 0) <= iota((CHUNK, CHUNK), 1)).astype(F32)
    grad_log = dot_nn(later, grad_cumul, HIGHEST) + end_sums[0:1, :]
    grad_raw = (grad_step + grad_log * hp_ref[1:2, :]) * jax.nn.sigmoid(raw)
    gdt_ref[...] = grad_raw.astype(BF16)
    ghead_ref[0:1, :] += jnp.sum(grad_raw, axis=0, keepdims=True)
    ghead_ref[1:2, :] += jnp.sum(grad_log * log_decay, axis=0, keepdims=True)
    for i in range(CHANNELS // LANES):
        window = grad_ref[pl.ds(start, CHUNK + 8), tile(i)]
        own = window[0:CHUNK]
        padded = xs_ref[pl.ds(start, CHUNK + 8), tile(i)]
        total = cw_ref[3:4, tile(i)] * own
        gconv_ref[4:5, tile(i)] += jnp.sum(own, axis=0, keepdims=True)
        gconv_ref[3:4, tile(i)] += jnp.sum(own * padded[8 : 8 + CHUNK], axis=0, keepdims=True)
        for lag in range(1, CONV):
            masked = window * masks_window[lag]
            total = total + cw_ref[3 - lag : 4 - lag, tile(i)] * masked[lag : lag + CHUNK]
            gconv_ref[3 - lag : 4 - lag, tile(i)] += jnp.sum(
                masked[0:CHUNK] * padded[8 - lag : 8 - lag + CHUNK], axis=0, keepdims=True
            )
        gmix_ref[:, tile(i)] = total.astype(BF16)

        @pl.when(step_at == 0)
        def _():
            tail_ref[:, tile(i)] = total[CHUNK - 8 :]

        @pl.when(step_at == count - 1)
        def _():
            ahead = jnp.zeros((8, LANES), F32)
            for lag in range(1, CONV):
                head = jnp.concatenate(
                    [jnp.zeros((8, LANES), F32), window[0:8] * masks_window[lag][0:8]], axis=0
                )
                ahead = ahead + cw_ref[3 - lag : 4 - lag, tile(i)] * head[lag : lag + 8]
            edge_grad_ref[:, tile(i)] = ahead

    @pl.when(step_at == count - 1)
    def _():
        total = jnp.zeros((8, LANES), F32)
        for j in range(PAIRS):
            total += head_sums(rows_ref[:, tile(j)], picks(j))
        ghead_ref[2:3, :] = total[0:1, :]


def mamba_back(
    scalars,
    edge,
    mixed,
    dt_raw,
    doc,
    doc_row,
    conv_pack,
    head_pack,
    skip_wide,
    dy,
    y,
    sin,
    ds_end,
    tokens=(),
):
    rows = mixed.shape[0]
    count = rows // CHUNK
    by_chunk = lambda width: pl.BlockSpec((CHUNK, width), lambda i: (count - 1 - i, 0))
    return pl.pallas_call(
        without(mamba_back_kernel, 13, len(tokens)),
        grid=(count,),
        in_specs=[
            pl.BlockSpec(memory_space=pltpu.SMEM),
            whole((8, CHANNELS)),
            whole((rows, CHANNELS)),
            by_chunk(LANES),
            whole((rows + 8, 1)),
            pl.BlockSpec((8, CHUNK), lambda i: (0, count - 1 - i)),
            whole((8, CHANNELS)),
            whole((8, LANES)),
            whole((1, MAMBA_INNER)),
            by_chunk(MAMBA_INNER),
            by_chunk(MAMBA_INNER),
            pl.BlockSpec((1, STATE_SIZE, MAMBA_INNER), lambda i: (count - 1 - i, 0, 0)),
            whole((STATE_SIZE, MAMBA_INNER)),
            *unread(tokens),
        ],
        out_specs=[
            by_chunk(CHANNELS),
            whole((8, CHANNELS)),
            whole((8, CHANNELS)),
            by_chunk(LANES),
            whole((8, CHANNELS)),
            whole((8, LANES)),
        ],
        out_shape=[
            jax.ShapeDtypeStruct((rows, CHANNELS), BF16),
            jax.ShapeDtypeStruct((8, CHANNELS), F32),
            jax.ShapeDtypeStruct((8, CHANNELS), F32),
            jax.ShapeDtypeStruct((rows, LANES), BF16),
            jax.ShapeDtypeStruct((8, CHANNELS), F32),
            jax.ShapeDtypeStruct((8, LANES), F32),
        ],
        scratch_shapes=[
            pltpu.VMEM((rows + 8, CHANNELS), F32),
            pltpu.VMEM((CHUNK, CHANNELS), F32),
            pltpu.VMEM((CHUNK, CHANNELS), F32),
            pltpu.VMEM((rows + 8, CHANNELS), F32),
            pltpu.VMEM((STATE_SIZE, MAMBA_INNER), F32),
            pltpu.VMEM((8, MAMBA_INNER), F32),
        ],
        compiler_params=params("arbitrary"),
        cost_estimate=lasting(25),
        name="mamba_back",
    )(
        scalars,
        edge,
        mixed,
        dt_raw,
        doc,
        doc_row,
        conv_pack,
        head_pack,
        skip_wide,
        dy,
        y,
        sin,
        ds_end,
        *tokens,
    )


def scan_step_kernel(begins, ends, flag_ref, *refs):
    total_ref, refs = refs[0], refs[1:]
    seen_ref, refs = (None, refs) if begins else (refs[0], refs[1:])
    got_ref, out_ref = refs[0], refs[-1]
    first = flag_ref[0] == 1
    rows = slice(0, STATE_SIZE)
    rest = slice(STATE_SIZE, MESSAGE_ROWS)
    one = STATE_SIZE
    for j in range(PAIRS):
        got = got_ref[:, tile(j)].astype(F32)
        if begins:
            out_ref[rows, tile(j)] = jnp.where(first, got[rows], 0.0)
            out_ref[rest, tile(j)] = jnp.where(first, got[rest], 1.0)
        else:
            seen = seen_ref[:, tile(j)]
            passed = seen[rows] + seen[one : one + 1] * got[rows]
            out_ref[rows, tile(j)] = jnp.where(first, passed, seen[rows])
            out_ref[rest, tile(j)] = jnp.where(first, seen[rest] * got[rest], seen[rest])
        if not ends:
            new_ref, send_ref = refs[1:3]
            total = total_ref[:, tile(j)]
            mine, theirs = total[one : one + 1], got[one : one + 1]
            state = jnp.where(first, mine * got[rows] + total[rows], theirs * total[rows] + got[rows])
            new_ref[rows, tile(j)] = state
            send_ref[rows, tile(j)] = state.astype(BF16)
            factor = total[rest] * got[rest]
            new_ref[rest, tile(j)] = factor
            send_ref[rest, tile(j)] = factor.astype(BF16)


def scan_step(first, total, seen, got, ends):
    shape = (MESSAGE_ROWS, MAMBA_INNER)
    ins = [total, got] if seen is None else [total, seen, got]
    outs = [F32] if ends else [F32, BF16, F32]
    specs = [whole(shape)] * len(ins)
    if ends:
        specs[0] = pl.BlockSpec(memory_space=pl.ANY)
    found = pl.pallas_call(
        functools.partial(scan_step_kernel, seen is None, ends),
        in_specs=[pl.BlockSpec(memory_space=pltpu.SMEM)] + specs,
        out_specs=[whole(shape)] * len(outs),
        out_shape=[jax.ShapeDtypeStruct(shape, kind) for kind in outs],
        compiler_params=pltpu.CompilerParams(vmem_limit_bytes=VMEM_LIMIT),
        cost_estimate=lasting(2.5),
        name="scan_step",
    )(first.astype(jnp.int32).reshape(1), *ins)
    return (None, None, found[0]) if ends else found


def half_roll(x):
    return pltpu.roll(x, HEAD_SIZE, 1)


def stack_low(block, rows):
    low = low_half(rows)
    parts = []
    for a in range(2):
        pair = block[:, tile(a)]
        parts.append(jnp.where(low, pair, 0.0))
        parts.append(jnp.where(low, half_roll(pair), 0.0))
    return parts


def stack_high(block, rows):
    low = low_half(rows)
    parts = []
    for a in range(2):
        pair = block[:, tile(a)]
        parts.append(jnp.where(low, 0.0, half_roll(pair)))
        parts.append(jnp.where(low, 0.0, pair))
    return parts


def tile_bounds(sc_ref, at, tiles):
    first_doc = sc_ref[at]
    last_doc = sc_ref[tiles + at]
    start = sc_ref[2 * tiles] + at * QUERY_TILE
    block_lo = first_doc // KEY_BLOCK
    block_hi = (start + QUERY_TILE - 1) // KEY_BLOCK + 1
    return start, last_doc, block_lo, block_hi


def visible_mask(block, start, doc_row):
    lanes = GROUP * QUERY_TILE
    key = block * KEY_BLOCK + iota((KEY_BLOCK, lanes), 0)
    query = start + iota((1, lanes), 1) % QUERY_TILE
    return (key <= query) & (key >= doc_row)


def attend_kernel(
    sc_ref, q_ref, kv_ref, doc_ref, vec_ref, norm_ref, lse_ref, qz_ref, max_ref, acc_ref
):
    at = pl.program_id(0)
    tiles = pl.num_programs(0)
    start, last_doc, block_lo, block_hi = tile_bounds(sc_ref, at, tiles)
    for g, part in enumerate(stack_low(q_ref[...].astype(F32), QUERY_TILE)):
        qz_ref[g * QUERY_TILE : (g + 1) * QUERY_TILE, :] = part.astype(BF16)
    max_ref[...] = jnp.full_like(max_ref, MASK_FILLER)
    acc_ref[...] = jnp.zeros_like(acc_ref)
    doc_row = jnp.concatenate([doc_ref[0:1, :]] * GROUP, axis=1)

    def visit(block, masked):
        at_rows = sc_ref[2 * tiles + 1 + block] * KEY_BLOCK
        kv = kv_ref[pl.ds(pl.multiple_of(at_rows, KEY_BLOCK), KEY_BLOCK), :]
        values = jnp.where(low_half(KEY_BLOCK), jnp.ones_like(kv), kv)
        scores = dot_nt(kv, qz_ref[...])
        if masked:
            scores = jnp.where(visible_mask(block, start, doc_row), scores, MASK_FILLER)
        before = max_ref[0:1, :]
        top = jnp.maximum(before, jnp.max(scores, axis=0, keepdims=True))
        prob = jnp.exp(scores - top)
        fade = jnp.exp(before - top)
        max_ref[0:1, :] = top
        acc_ref[...] = acc_ref[...] * fade + dot_tn(values, prob.astype(BF16))

    def one(block, carry):
        full = (block * KEY_BLOCK + KEY_BLOCK - 1 <= start) & (block * KEY_BLOCK >= last_doc)

        @pl.when(full)
        def _():
            visit(block, False)

        @pl.when(jnp.logical_not(full))
        def _():
            visit(block, True)

        return carry

    lax.fori_loop(block_lo, block_hi, one, 0)
    total = acc_ref[0:1, :]
    lse_ref[0] = jnp.broadcast_to(max_ref[0:1, :] + jnp.log(total), lse_ref.shape[1:])
    scaled = acc_ref[...] / total
    low = low_half(QUERY_TILE)
    for a in range(2):
        even = half_roll(scaled[:, (2 * a) * QUERY_TILE : (2 * a + 1) * QUERY_TILE].T)
        odd = scaled[:, (2 * a + 1) * QUERY_TILE : (2 * a + 2) * QUERY_TILE].T
        both = jnp.where(low, even, odd)
        norm_ref[:, tile(a)] = both
        vec_ref[:, tile(a)] = both.astype(BF16)


def carrying(kernel, ins, outs, parts, pieces):
    def body(*refs):
        own_ins, refs = refs[:ins], refs[ins:]
        at_ref, piece_refs, refs = refs[0], refs[1 : 1 + pieces], refs[1 + pieces :]
        own_outs, refs = refs[:outs], refs[outs:]
        places = 1 + max(part[5] for part in parts)
        place_refs, refs = refs[:places], refs[places:]
        own_scratch, held, sems = refs[: -pieces - 1], refs[-pieces - 1 : -1], refs[-1]
        step, last = pl.program_id(0), pl.num_programs(0) - 1
        come, leave = place_copies(parts, at_ref, piece_refs, place_refs, held, sems)

        @pl.when(step == 0)
        def _():
            for copy in come:
                copy.start()

        kernel(*own_ins, *own_outs, *own_scratch)

        @pl.when(step == 0)
        def _():
            for copy in come:
                copy.wait()
            for _, copy in leave:
                copy.start()

        @pl.when(step == last)
        def _():
            for _, copy in leave:
                copy.wait()

    return body


def place_copies(parts, at_ref, pieces, out_refs, held, sems):
    come = [
        pltpu.make_async_copy(piece, here, sems.at[i])
        for i, (piece, here) in enumerate(zip(pieces, held))
    ]
    leave = []
    for k, (piece, row, rows, col, cols, out) in enumerate(parts):
        here = held[piece].at[pl.ds(row, rows), pl.ds(col, cols)]
        to = out_refs[out].at[pl.ds(pl.multiple_of(at_ref[k], 16), rows), :]
        leave.append((piece, pltpu.make_async_copy(here, to, sems.at[len(pieces) + k])))
    return come, leave


def attend(scalars, q, kv, doc_row, head, tokens=(), carried=None):
    rows = q.shape[0]
    length = kv.shape[0]
    tiles = rows // QUERY_TILE
    lanes = GROUP * QUERY_TILE
    width = GROUP * HEAD_SIZE
    by_tile = pl.BlockSpec((QUERY_TILE, width), lambda t: (t, 0))
    kernel = attend_kernel
    more_in, more_out, more_shape, more_scratch, more = [], [], [], [], []
    if carried:
        pieces, parts, offsets, shapes = carried
        kernel = carrying(kernel, 4, 3, parts, len(pieces))
        more_in = [pl.BlockSpec(memory_space=pltpu.SMEM)] + unread(pieces)
        more_out = unread(shapes)
        more_shape = [jax.ShapeDtypeStruct(shape, BF16) for shape in shapes]
        more_scratch = [pltpu.VMEM(piece.shape, BF16) for piece in pieces]
        more_scratch.append(pltpu.SemaphoreType.DMA((len(pieces) + len(parts),)))
        more = [jnp.stack(offsets).astype(jnp.int32), *pieces]
    return pl.pallas_call(
        without(kernel, 4 + len(more_in), len(tokens)),
        grid=(tiles,),
        in_specs=[
            pl.BlockSpec(memory_space=pltpu.SMEM),
            pl.BlockSpec((QUERY_TILE, width), lambda t: (t, head)),
            whole((length, LANES)),
            pl.BlockSpec((8, QUERY_TILE), lambda t: (0, t)),
            *more_in,
            *unread(tokens),
        ],
        out_specs=[by_tile, by_tile, pl.BlockSpec((1, 8, lanes), lambda t: (t, 0, 0)), *more_out],
        out_shape=[
            jax.ShapeDtypeStruct((rows, width), BF16),
            jax.ShapeDtypeStruct((rows, width), F32),
            jax.ShapeDtypeStruct((tiles, 8, lanes), F32),
            *more_shape,
        ],
        scratch_shapes=[
            pltpu.VMEM((lanes, LANES), BF16),
            pltpu.VMEM((8, lanes), F32),
            pltpu.VMEM((LANES, lanes), F32),
            *more_scratch,
        ],
        compiler_params=params("arbitrary"),
        cost_estimate=lasting(18),
        name="attend",
    )(scalars, q, kv, doc_row, *more, *tokens)


def attend_back_kernel(
    sc_ref, q_ref, do_ref, norm_ref, lse_ref, kv_ref, doc_ref, dq_ref, dkv_ref, qd_ref, dkv_acc, dq_acc
):
    at = pl.program_id(0)
    tiles = pl.num_programs(0)
    lanes = GROUP * QUERY_TILE
    start, last_doc, block_lo, block_hi = tile_bounds(sc_ref, at, tiles)

    @pl.when(at == 0)
    def _():
        dkv_acc[...] = jnp.zeros_like(dkv_acc)

    grad = do_ref[...].astype(F32)
    for g, part in enumerate(stack_low(q_ref[...].astype(F32), QUERY_TILE)):
        qd_ref[g * QUERY_TILE : (g + 1) * QUERY_TILE, :] = part.astype(BF16)
    for g, part in enumerate(stack_high(grad, QUERY_TILE)):
        qd_ref[lanes + g * QUERY_TILE : lanes + (g + 1) * QUERY_TILE, :] = part.astype(BF16)
    deltas = []
    for a in range(2):
        turned = (grad[:, tile(a)] * norm_ref[:, tile(a)]).T
        deltas.append(jnp.sum(turned[0:HEAD_SIZE], axis=0, keepdims=True))
        deltas.append(jnp.sum(turned[HEAD_SIZE:], axis=0, keepdims=True))
    delta = jnp.concatenate(deltas, axis=1)
    lse = lse_ref[0, 0:1, :]
    dq_acc[...] = jnp.zeros_like(dq_acc)
    doc_row = jnp.concatenate([doc_ref[0:1, :]] * GROUP, axis=1)

    def visit(block, masked):
        first_row = sc_ref[2 * tiles + 1 + block] * KEY_BLOCK
        at_rows = pl.ds(pl.multiple_of(first_row, KEY_BLOCK), KEY_BLOCK)
        kv = kv_ref[at_rows, :]
        scores = dot_nt(kv, qd_ref[0:lanes, :])
        prob = jnp.exp(scores - lse)
        if masked:
            prob = jnp.where(visible_mask(block, start, doc_row), prob, 0.0)
        grad_prob = dot_nt(kv, qd_ref[lanes:, :])
        grad_scores = (prob * (grad_prob - delta)).astype(BF16)
        dkv_acc[at_rows, :] += dot_nn(grad_scores, qd_ref[0:lanes, :]) + dot_nn(
            prob.astype(BF16), qd_ref[lanes:, :]
        )
        dq_acc[...] += dot_tn(kv, grad_scores)

    def one(block, carry):
        full = (block * KEY_BLOCK + KEY_BLOCK - 1 <= start) & (block * KEY_BLOCK >= last_doc)

        @pl.when(full)
        def _():
            visit(block, False)

        @pl.when(jnp.logical_not(full))
        def _():
            visit(block, True)

        return carry

    lax.fori_loop(block_lo, block_hi, one, 0)
    low = low_half(QUERY_TILE)
    scale = 1.0 / math.sqrt(HEAD_SIZE)
    for a in range(2):
        even = dq_acc[:, (2 * a) * QUERY_TILE : (2 * a + 1) * QUERY_TILE].T
        odd = half_roll(dq_acc[:, (2 * a + 1) * QUERY_TILE : (2 * a + 2) * QUERY_TILE].T)
        dq_ref[:, tile(a)] = jnp.where(low, even, odd) * scale

    @pl.when(at == tiles - 1)
    def _():
        dkv_ref[...] = dkv_acc[...].astype(BF16)


def attend_back(scalars, q, grad, norm, lse, kv, doc_row, head, tokens=()):
    rows = q.shape[0]
    length = kv.shape[0]
    tiles = rows // QUERY_TILE
    lanes = GROUP * QUERY_TILE
    width = GROUP * HEAD_SIZE
    by_tile = pl.BlockSpec((QUERY_TILE, width), lambda t: (t, 0))
    by_head = pl.BlockSpec((QUERY_TILE, width), lambda t: (t, head))
    return pl.pallas_call(
        without(attend_back_kernel, 7, len(tokens)),
        grid=(tiles,),
        in_specs=[
            pl.BlockSpec(memory_space=pltpu.SMEM),
            by_head,
            by_head,
            by_tile,
            pl.BlockSpec((1, 8, lanes), lambda t: (t, 0, 0)),
            whole((length, LANES)),
            pl.BlockSpec((8, QUERY_TILE), lambda t: (0, t)),
            *unread(tokens),
        ],
        out_specs=[by_tile, whole((length, LANES))],
        out_shape=[
            jax.ShapeDtypeStruct((rows, width), F32),
            jax.ShapeDtypeStruct((length, LANES), BF16),
        ],
        scratch_shapes=[
            pltpu.VMEM((2 * lanes, LANES), BF16),
            pltpu.VMEM((length, LANES), F32),
            pltpu.VMEM((LANES, lanes), F32),
        ],
        compiler_params=params("arbitrary"),
        cost_estimate=lasting(26),
        name="attend_back",
    )(scalars, q, grad, norm, lse, kv, doc_row, *tokens)


def turn_lanes(x, cosine, sine):
    half = HEAD_SIZE // 2
    former = iota(x.shape, 1) % HEAD_SIZE < half
    other = jnp.where(former, -pltpu.roll(x, LANES - half, 1), pltpu.roll(x, half, 1))
    return x * cosine + other * sine


def rope_kernel(q_in_ref, kv_in_ref, cos_ref, sin_ref, q_ref, kv0_ref, kv1_ref):
    cosine, sine = cos_ref[...], sin_ref[...]
    scale = 1.0 / math.sqrt(HEAD_SIZE)
    for i in range(QUERY_HEADS * HEAD_SIZE // LANES):
        turned = turn_lanes(q_in_ref[:, tile(i)], cosine, sine).astype(BF16)
        q_ref[:, tile(i)] = (turned.astype(F32) * scale).astype(BF16)
    keys = turn_lanes(kv_in_ref[:, tile(0)], cosine, sine)
    values = kv_in_ref[:, tile(1)]
    low = iota(keys.shape, 1) < HEAD_SIZE
    kv0_ref[...] = jnp.where(low, keys, half_roll(values)).astype(BF16)
    kv1_ref[...] = jnp.where(low, half_roll(keys), values).astype(BF16)


def rope(q_raw, kv_raw, cosine, sine):
    rows = q_raw.shape[0]
    return pl.pallas_call(
        rope_kernel,
        out_shape=[
            jax.ShapeDtypeStruct((rows, QUERY_HEADS * HEAD_SIZE), BF16),
            jax.ShapeDtypeStruct((rows, LANES), BF16),
            jax.ShapeDtypeStruct((rows, LANES), BF16),
        ],
        compiler_params=pltpu.CompilerParams(vmem_limit_bytes=VMEM_LIMIT),
        cost_estimate=lasting(3),
        name="rope",
    )(q_raw, kv_raw, cosine, sine)


def rope_back_kernel(dq0_ref, dq1_ref, dkv0_ref, dkv1_ref, cos_ref, sin_ref, grad_ref):
    cosine, sine = cos_ref[...], -sin_ref[...]
    for head, dq_ref in enumerate((dq0_ref, dq1_ref)):
        for i in range(2):
            turned = turn_lanes(dq_ref[:, tile(i)], cosine, sine)
            grad_ref[:, tile(2 * head + i)] = turned.astype(BF16)
    first = dkv0_ref[...].astype(F32)
    second = dkv1_ref[...].astype(F32)
    low = iota(first.shape, 1) < HEAD_SIZE
    keys = jnp.where(low, first, half_roll(second))
    values = jnp.where(low, half_roll(first), second)
    grad_ref[:, tile(4)] = turn_lanes(keys, cosine, sine).astype(BF16)
    grad_ref[:, tile(5)] = values.astype(BF16)


def rope_back(dq0, dq1, dkv0, dkv1, cosine, sine):
    rows = dq0.shape[0]
    return pl.pallas_call(
        rope_back_kernel,
        out_shape=jax.ShapeDtypeStruct(
            (rows, QUERY_HEADS * HEAD_SIZE + KEY_VALUE_HEADS * LANES), BF16
        ),
        compiler_params=pltpu.CompilerParams(vmem_limit_bytes=VMEM_LIMIT),
        cost_estimate=lasting(3),
        name="rope_back",
    )(dq0, dq1, dkv0, dkv1, cosine, sine)


DEVICES = ("ctx", "fsdp")


def swap(block, axis, bit):
    count, width = lax.axis_size("ctx"), lax.axis_size("fsdp")
    partner = lambda c, f: (c ^ bit) * width + f if axis == "ctx" else c * width + (f ^ bit)
    route = [(c * width + f, partner(c, f)) for c in range(count) for f in range(width)]
    return lax.ppermute(block, DEVICES, route)


def take_rows(block, index, rows):
    return lax.dynamic_slice_in_dim(block, index * rows, rows, 0)


def after_kernel(*refs):
    pass


def after(block, *others):
    return pl.pallas_call(
        after_kernel,
        in_specs=[pl.BlockSpec(memory_space=pl.ANY)] * (1 + len(others)),
        out_specs=pl.BlockSpec(memory_space=pl.ANY),
        out_shape=jax.ShapeDtypeStruct(block.shape, block.dtype),
        input_output_aliases={0: 0},
        name="after",
    )(block, *others)


def place_kernel(parts, tokens, at_ref, *refs):
    count = 1 + max(part[0] for part in parts)
    outs = 1 + max(part[5] for part in parts)
    pieces, refs = refs[:count], refs[count + tokens :]
    out_refs, held, sems = refs[:outs], refs[outs:-1], refs[-1]
    come, leave = place_copies(parts, at_ref, pieces, out_refs, held, sems)
    for copy in come:
        copy.start()
    for i in range(count):
        come[i].wait()
        for piece, copy in leave:
            if piece == i:
                copy.start()
    for _, copy in leave:
        copy.wait()


def place(pieces, parts, offsets, shapes, tokens=()):
    size = sum(math.prod(piece.shape) for piece in pieces) * 4
    return pl.pallas_call(
        functools.partial(place_kernel, tuple(parts), len(tokens)),
        in_specs=[pl.BlockSpec(memory_space=pltpu.SMEM)]
        + [pl.BlockSpec(memory_space=pl.ANY)] * (len(pieces) + len(tokens)),
        out_specs=[pl.BlockSpec(memory_space=pl.ANY)] * len(shapes),
        out_shape=[jax.ShapeDtypeStruct(shape, BF16) for shape in shapes],
        scratch_shapes=[pltpu.VMEM(piece.shape, BF16) for piece in pieces]
        + [pltpu.SemaphoreType.DMA((len(pieces) + len(parts),))],
        compiler_params=pltpu.CompilerParams(vmem_limit_bytes=VMEM_LIMIT),
        cost_estimate=lasting(1 + size / 3e6),
        name="place",
    )(jnp.stack(offsets).astype(jnp.int32), *pieces, *tokens)


def move(block, axis, bit, start=(), arrive=()):
    sent = after(block, *start) if start else block
    got = swap(sent, axis, bit)
    return sent, after(got, *arrive) if arrive else got


def whole_parts(shard, other, near, columns, arrive=(), extra=0):
    rank, ranks = lax.axis_index("fsdp"), lax.axis_size("fsdp")
    rows = shard.shape[0] - extra
    pieces = [shard, other, near, move(near, "fsdp", 1, (), arrive)[1]]
    parts, offsets, shapes = [], [], {}
    for k in range(4):
        at = 0
        for width, out, shard_rows, first in columns:
            parts.append((k, 0, rows, at, width, out))
            offsets.append((rank ^ k) * shard_rows + first)
            shapes[out] = (ranks * shard_rows, width)
            at += width
        if extra:
            out = 1 + max(column[1] for column in columns)
            parts.append((k, rows, extra, 0, at, out))
            offsets.append((rank ^ k) * extra)
            shapes[out] = (ranks * extra, at)
    return pieces, parts, offsets, [shapes[out] for out in sorted(shapes)]


def product_kernel(blocks, adds, halves, at_ref, *refs):
    left_refs, refs = refs[:blocks], refs[blocks:]
    grad_ref, refs = refs[0], refs[1:]
    add_refs, refs = refs[:adds], refs[adds:]
    rows = left_refs[0].shape[1]
    turned_ref = refs[-2]

    @pl.when(pl.program_id(0) == 0)
    def _():
        for i, left_ref in enumerate(left_refs):
            turned = left_ref[...].astype(F32).T.astype(BF16)
            turned_ref[i * rows : (i + 1) * rows, :] = turned

    total = dot_nn(turned_ref[...], grad_ref[...])
    for add_ref in add_refs:
        total = total + add_ref[...].astype(F32)
    if not halves:
        refs[0][...] = total.astype(BF16)
        return
    kept_ref, sent_ref, total_ref = refs[0], refs[1], refs[-1]
    total_ref[...] = total
    half = rows // 2
    side = at_ref[blocks]
    for i in range(blocks):
        to = slice(i * half, (i + 1) * half)
        mine = pl.multiple_of(i * rows + side * half, half)
        theirs = pl.multiple_of(i * rows + (1 - side) * half, half)
        kept_ref[to, :] = total_ref[pl.ds(mine, half), :].astype(BF16)
        sent_ref[to, :] = total_ref[pl.ds(theirs, half), :].astype(BF16)


def product(left, which, grad, adds=(), halves=False, tokens=()):
    tokens_count = len(tokens)
    depth, width = grad.shape
    rows = left.shape[1] // lax.axis_size("fsdp")
    height = rows * len(which)
    span = max(w for w in range(LANES, min(width, 2049), LANES) if width % w == 0)
    span = span if 5 * span >= 2 * width else width
    rank, side = lax.axis_index("fsdp"), lax.axis_index("ctx") % 2
    at = jnp.stack([rank ^ k for k in which] + [side]).astype(jnp.int32)
    block_of = lambda i: pl.BlockSpec((depth, rows), lambda t, at: (0, at[i]))
    add_of = lambda block: pl.BlockSpec((height, span), lambda t, at: (block, t))
    outs = 2 if halves else 1
    shape = (height // outs, width)
    found = pl.pallas_call(
        without(
            functools.partial(product_kernel, len(which), len(adds), halves),
            2 + len(which) + len(adds),
            tokens_count,
        ),
        grid_spec=pltpu.PrefetchScalarGridSpec(
            num_scalar_prefetch=1,
            grid=(width // span,),
            in_specs=[block_of(i) for i in range(len(which))]
            + [pl.BlockSpec((depth, span), lambda t, at: (0, t))]
            + [add_of(block) for _, block in adds]
            + unread(tokens),
            out_specs=[pl.BlockSpec((height // outs, span), lambda t, at: (0, t))] * outs,
            scratch_shapes=[
                pltpu.VMEM((height, depth), BF16),
                pltpu.VMEM((height, span), F32),
            ],
        ),
        out_shape=[jax.ShapeDtypeStruct(shape, BF16)] * outs,
        compiler_params=params("arbitrary"),
        cost_estimate=lasting(1 + height * width * 3e-6),
        name="product",
    )(at, *([left] * len(which)), grad, *[array for array, _ in adds], *tokens)
    return found if halves else found[0]


class Reduction:
    def __init__(self, left, grad, more=None):
        self.left, self.grad = left, grad
        self.more = more or [[], [], []]
        sent = product(left, (1, 3), grad, self.more[2])
        self.sent, self.got = move(sent, "fsdp", 1)

    def hold(self, *tokens):
        self.got = after(self.got, *tokens)

    def over_x(self, start=(), arrive=(), tokens=()):
        self.near = self.got
        sent = product(self.left, (2,), self.grad, [(self.got, 1)] + self.more[1], False, tokens)
        self.sent, self.got = move(sent, "fsdp", 2, start, arrive)

    def then_over_y(self, start=(), arrive=(), tokens=()):
        adds = [(self.near, 0), (self.got, 0)] + self.more[0]
        self.kept, sent = product(self.left, (0,), self.grad, adds, True, tokens)
        self.sent, self.got = move(sent, "ctx", 1, start, arrive)

    def first_over_y(self, start=(), arrive=(), tokens=()):
        self.kept, sent = product(self.left, (0, 2), self.grad, [(self.got, 0)], True, tokens)
        self.sent, self.got = move(sent, "ctx", 1, start, arrive)

    def then_over_x(self, start=(), arrive=()):
        total = (self.kept.astype(F32) + self.got.astype(F32)).astype(BF16)
        half = total.shape[0] // 2
        self.kept = total[:half]
        self.sent, self.got = move(total[half:], "fsdp", 2, start, arrive)


def ctx_bits():
    bits = [1]
    while 2 * bits[-1] < lax.axis_size("ctx"):
        bits.append(2 * bits[-1])
    return bits


def spread_order():
    apart = jnp.arange(lax.axis_size("ctx"), dtype=jnp.int32) ^ lax.axis_index("ctx")
    where = jnp.zeros_like(apart)
    for k, bit in enumerate(reversed(ctx_bits())):
        where += ((apart // bit) % 2) << k
    return where


class Spread:
    def __init__(self, block):
        self.block, self.bits = block, ctx_bits()

    def step(self, arrive=()):
        _, got = move(self.block, "ctx", self.bits.pop(), (), arrive)
        self.block = jnp.concatenate([self.block, got], axis=0)

    def finish(self, arrive=()):
        while self.bits:
            self.step(arrive)
        return self.block


class BlockSums:
    def __init__(self, blocks):
        self.blocks, self.bits = blocks, ctx_bits()

    def step(self, start=(), arrive=()):
        half = self.blocks.shape[0] // 2
        bit = self.bits.pop(0)
        self.sent, got = move(self.blocks[half:], "ctx", bit, start, arrive)
        self.blocks = (self.blocks[:half].astype(F32) + got.astype(F32)).astype(BF16)

    def finish(self, start=()):
        while self.bits:
            self.step(start)
        return self.blocks


def stretches_of(shapes, rows):
    found, at = [], 0
    for index, (height, width) in enumerate(shapes):
        for first in range(0, height, rows):
            found.append((index, first, at))
            at += width
    return found, at


def fold_kernel(count, side_ref, *refs):
    new_ref, sent_ref = refs[2 * count :]
    half = new_ref.shape[0]
    mine = pl.multiple_of(side_ref[0] * half, half)
    theirs = pl.multiple_of((1 - side_ref[0]) * half, half)
    at = 0
    for i in range(count):
        kept_ref, got_ref = refs[2 * i], refs[2 * i + 1]
        height, width = kept_ref.shape
        for first in range(0, height, 2 * half):
            columns = slice(at, at + width)
            for row, out_ref in ((mine, new_ref), (theirs, sent_ref)):
                rows = pl.ds(first + row, half)
                total = kept_ref[rows, :].astype(F32) + got_ref[rows, :].astype(F32)
                out_ref[:, columns] = total.astype(BF16)
            at += width


def fold_pack(side, pairs):
    arrays = [array for pair in pairs for array in pair]
    rows = min(array.shape[0] for array in arrays)
    _, width = stretches_of([kept.shape for kept, _ in pairs], rows)
    shape = (rows // 2, width)
    return pl.pallas_call(
        functools.partial(fold_kernel, len(pairs)),
        in_specs=[pl.BlockSpec(memory_space=pltpu.SMEM)] + [whole(array.shape) for array in arrays],
        out_specs=[whole(shape)] * 2,
        out_shape=[jax.ShapeDtypeStruct(shape, BF16)] * 2,
        compiler_params=pltpu.CompilerParams(vmem_limit_bytes=VMEM_LIMIT),
        cost_estimate=lasting(2),
        name="fold",
    )(side.reshape(1), *arrays)


def join_kernel(side_ref, own_ref, got_ref, out_ref):
    half = own_ref.shape[0]
    out_ref[pl.ds(pl.multiple_of(side_ref[0] * half, half), half), :] = own_ref[...]
    out_ref[pl.ds(pl.multiple_of((1 - side_ref[0]) * half, half), half), :] = got_ref[...]


def join_pack(side, own, got):
    shape = (2 * own.shape[0], own.shape[1])
    return pl.pallas_call(
        join_kernel,
        in_specs=[pl.BlockSpec(memory_space=pltpu.SMEM)] + [whole(own.shape)] * 2,
        out_specs=whole(shape),
        out_shape=jax.ShapeDtypeStruct(shape, BF16),
        compiler_params=pltpu.CompilerParams(vmem_limit_bytes=VMEM_LIMIT),
        cost_estimate=lasting(2),
        name="join",
    )(side.reshape(1), own, got)


def unpack_kernel(parts, outs, side_ref, own_ref, got_ref, *out_refs):
    rows = own_ref.shape[0]
    for side in range(2):

        @pl.when(side_ref[0] == side)
        def _():
            for array, height, first, at in parts:
                for half, ref in ((side, own_ref), (1 - side, got_ref)):
                    row = half * (height // 2) + first
                    for out_ref, (source, top, end, left, right) in zip(out_refs, outs):
                        if source == array and top <= row < end:
                            to = slice(row - top, row - top + rows)
                            out_ref[to, :] = ref[:, at + left : at + right].astype(F32)


def unpack(side, own, got, shapes, outs):
    found, _ = stretches_of([(height // 2, width) for height, width in shapes], own.shape[0])
    parts = [(index, shapes[index][0], first, at) for index, first, at in found]
    out_shapes = [(end - top, right - left) for _, top, end, left, right in outs]
    return pl.pallas_call(
        functools.partial(unpack_kernel, parts, outs),
        in_specs=[pl.BlockSpec(memory_space=pltpu.SMEM)] + [whole(own.shape)] * 2,
        out_specs=[whole(shape) for shape in out_shapes],
        out_shape=[jax.ShapeDtypeStruct(shape, F32) for shape in out_shapes],
        compiler_params=pltpu.CompilerParams(vmem_limit_bytes=VMEM_LIMIT),
        cost_estimate=lasting(4),
        name="unpack",
    )(side.reshape(1), own, got)


class Pack:
    def __init__(self, pairs):
        self.pairs = pairs
        self.shapes = [(2 * kept.shape[0], kept.shape[1]) for kept, _ in pairs]

    def hold(self, *tokens):
        self.got = after(self.got, *tokens)

    def side(self, bit):
        return (lax.axis_index("ctx") // bit) % 2

    def over_z(self, start=(), arrive=()):
        self.kept, sent = fold_pack(self.side(2), self.pairs)
        self.sent, self.got = move(sent, "ctx", 2, start, arrive)

    def rest(self, start=(), arrive=()):
        self.own = (self.kept.astype(F32) + self.got.astype(F32)).astype(BF16)
        self.kept = None
        for bit in ctx_bits()[2:]:
            self.total()
            self.sent, self.got = move(self.own, "ctx", bit, start, arrive)
            self.kept = self.own

    def total(self):
        if self.kept is not None:
            self.own = (self.kept.astype(F32) + self.got.astype(F32)).astype(BF16)
            self.kept = None

    def back_z(self, start=(), arrive=()):
        self.total()
        self.sent, got = move(self.own, "ctx", 2, start, arrive)
        self.own = join_pack(self.side(2), self.own, got)

    def back_y(self, outs, start=(), arrive=()):
        self.sent, got = move(self.own, "ctx", 1, start, arrive)
        return unpack(self.side(1), self.own, got, self.shapes, outs)


def shift_along(block, axis, distance):
    devices = range(lax.axis_size(axis))
    route = [(i - distance, i) for i in devices if i - distance in devices]
    return lax.ppermute(block, axis, route)


def segment_starts(positions, starts):
    reached = starts[None, :] <= positions[:, None]
    return jnp.max(jnp.where(reached, starts[None, :], -1), axis=1)


class Scan:
    def __init__(self, own, send, upwards):
        self.own, self.send, self.upwards = own, send, upwards
        self.seen = None
        self.bits = ctx_bits()

    def step(self, arrive=()):
        bit = self.bits.pop(0)
        above = (lax.axis_index("ctx") // bit) % 2 == 1
        _, got = move(self.send, "ctx", bit, (), arrive)
        first = above if self.upwards else jnp.logical_not(above)
        self.own, self.send, self.seen = scan_step(
            first, self.own, self.seen, got, not self.bits
        )
        return self.send

    def finish(self, arrive=()):
        while self.bits:
            self.step(arrive)
        return self.seen


def outer_sum(left, right):
    return dot_tn(left, right)


def time_steps(left, right):
    return dot_nt(left, right)


def local(
    tokens,
    cotangent,
    doc_starts,
    gain_mix,
    w_z,
    w_xbc,
    w_dt,
    conv_w,
    conv_b,
    dt_bias,
    a_log,
    skip_factor,
    w_mo,
    w_q,
    key_value_weight,
    w_o,
    gain_ffn,
    w_gate,
    w_up,
    w_down,
):
    xbc_dt = jnp.pad(
        jnp.concatenate([w_xbc, w_dt], axis=1), ((0, 0), (0, LANES - MAMBA_HEADS))
    )
    small = jnp.concatenate(
        [v.reshape(-1) for v in (gain_mix, conv_w, conv_b, dt_bias, a_log, skip_factor, gain_ffn)]
    )
    wide = w_q.shape[1] + key_value_weight.shape[1]
    small_rows = 16
    small = jnp.pad(small, (0, small_rows * wide - small.shape[0])).reshape(small_rows, wide)
    shard_qkv = jnp.concatenate([jnp.concatenate([w_q, key_value_weight], axis=1), small], axis=0)
    near_qkv = swap(shard_qkv, "fsdp", 2)
    near_xbc = swap(xbc_dt, "fsdp", 2)
    side_by_side = lambda w, rows: [w[i : i + rows] for i in range(0, w.shape[0], rows)]
    rows_in = w_z.shape[0]
    shard_omo = jnp.concatenate([w_o, w_mo], axis=0)
    shard_zo = jnp.concatenate([w_z] + side_by_side(shard_omo, rows_in), axis=1)
    shard_ffn = jnp.concatenate([w_gate, w_up] + side_by_side(w_down, rows_in), axis=1)
    shard_zo = after(shard_zo, near_qkv)
    near_zo = swap(shard_zo, "fsdp", 2)
    shard_ffn = after(shard_ffn, near_qkv)
    near_ffn = swap(shard_ffn, "fsdp", 2)
    other_xbc, other_zo, other_ffn = [
        swap(shard, "fsdp", 1) for shard in (xbc_dt, shard_zo, shard_ffn)
    ]
    full_qkv, small_all = place(
        *whole_parts(
            shard_qkv,
            swap(shard_qkv, "fsdp", 1),
            near_qkv,
            [(shard_qkv.shape[1], 0, rows_in, 0)],
            (),
            small_rows,
        )
    )
    model = w_down.shape[1]

    def stretches(out, shard_rows):
        return [(model, out, shard_rows, first) for first in range(0, shard_rows, rows_in)]

    ranks = lax.axis_size("fsdp")
    small_all = small_all.reshape(ranks, -1).astype(F32)
    at = [0]

    def unpack(rows, width):
        part = small_all[:, at[0] : at[0] + rows * width].reshape(-1, rows, width)
        at[0] += rows * width
        return part.transpose(1, 0, 2).reshape(rows, -1)

    full_gain_mix = unpack(1, gain_mix.shape[0])[0]
    full_conv_w = unpack(CONV, conv_b.shape[0])
    full_conv_b = unpack(1, conv_b.shape[0])[0]
    full_dt_bias = unpack(1, dt_bias.shape[0])[0]
    full_a_log = unpack(1, dt_bias.shape[0])[0]
    full_skip = unpack(1, dt_bias.shape[0])[0]
    full_gain_ffn = unpack(1, gain_ffn.shape[0])[0]
    o_rows = w_o.shape[0]
    wide_in = xbc_dt.shape[1]
    ctx_rank = lax.axis_index("ctx")
    inputs = tokens[0].astype(F32)
    rows = inputs.shape[0]
    starts = doc_starts[0]
    base = ctx_rank * rows
    positions = base + jnp.arange(rows, dtype=jnp.int32)
    doc = segment_starts(positions, starts)
    doc_col = jnp.pad(doc, (0, 8))[:, None]
    doc_row = jnp.broadcast_to(doc[None, :], (8, rows))
    scalars = jnp.concatenate([doc[CHUNK - 1 :: CHUNK], base[None]])
    attn_scalars = jnp.concatenate(
        [doc[::QUERY_TILE], doc[QUERY_TILE - 1 :: QUERY_TILE], base[None], spread_order()]
    )
    half = HEAD_SIZE // 2
    freqs = ROPE_BASE ** (
        -2.0 * (jnp.arange(LANES, dtype=jnp.int32) % half).astype(F32) / HEAD_SIZE
    )
    angles = positions.astype(F32)[:, None] * freqs[None, :]
    cosine, sine = jnp.cos(angles), jnp.sin(angles)
    conv_pack = jnp.pad(
        jnp.concatenate([full_conv_w, full_conv_b[None]], axis=0), ((0, 3), (0, 0))
    )
    pad_heads = lambda v: jnp.pad(v, (0, LANES - MAMBA_HEADS))[None]
    head_pack = jnp.concatenate(
        [pad_heads(full_dt_bias), pad_heads(-jnp.exp(full_a_log)), jnp.zeros((6, LANES), F32)], axis=0
    )
    skip_wide = jnp.repeat(full_skip, MAMBA_HEAD_SIZE)[None]

    scale_one = lax.rsqrt(jnp.mean(inputs * inputs, axis=-1, keepdims=True) + EPSILON)
    normed = (inputs * scale_one * full_gain_mix[None, :]).astype(BF16)
    q_width = QUERY_HEADS * HEAD_SIZE
    qkv_raw = dot_nn(normed, full_qkv)
    query, kv_first, kv_second = rope(
        qkv_raw[:, :q_width], qkv_raw[:, q_width:], cosine, sine
    )
    spreads = [Spread(kv) for kv in (kv_first, kv_second)]
    full_xbc = place(
        *whole_parts(
            xbc_dt,
            other_xbc,
            after(near_xbc, query),
            [(xbc_dt.shape[1], 0, rows_in, 0)],
        ),
        [other_zo, other_ffn],
    )[0]
    for spread_kv in spreads:
        spread_kv.step()
        spread_kv.block = after(spread_kv.block, full_xbc)
        spread_kv.step()
    mixed_in = dot_nn(normed, full_xbc[:, :CHANNELS]).astype(BF16)
    dt_raw = dot_nn(normed, full_xbc[:, CHANNELS:])
    edge = shift_along(mixed_in[rows - 8 :], "ctx", 1).astype(F32)
    y_local, state_local, message, own_state, decay, c_mat = mamba_forward(
        scalars, edge, mixed_in, dt_raw, doc_col[:rows], conv_pack, head_pack, skip_wide
    )
    kv_all = [spreads[0].finish([message])]
    scan = Scan(own_state, message, True)
    tokens = [message]
    attended = [attend(attn_scalars, query, kv_all[0], doc_row, 0, tokens)]
    first_done = attended[0][0]
    kv_all.append(spreads[1].finish([first_done]))
    carried = whole_parts(
        shard_zo,
        other_zo,
        after(near_zo, message),
        [(w_z.shape[1], 0, rows_in, 0)] + stretches(1, shard_omo.shape[0]),
    )
    tokens = [scan.step([first_done]), first_done]
    *second, full_z, full_omo = attend(
        attn_scalars, query, kv_all[1], doc_row, 1, tokens, carried
    )
    attended.append(second)
    second_done = attended[1][0]
    scan.step([second_done])
    gate_z = dot_nn(normed, full_z)
    state_in = scan.finish([gate_z])
    full_gate_up, full_down = place(
        *whole_parts(
            shard_ffn,
            other_ffn,
            after(near_ffn, state_in),
            [(2 * w_gate.shape[1], 0, rows_in, 0)] + stretches(1, w_down.shape[0]),
        )
    )
    y_total, both, state_true = mamba_correct(
        y_local, state_local, c_mat, decay, state_in, gate_z, attended[0][0], attended[1][0]
    )
    hidden = inputs + dot_nn(both, full_omo)
    gain_two = full_gain_ffn
    scale_two = lax.rsqrt(jnp.mean(hidden * hidden, axis=-1, keepdims=True) + EPSILON)
    normed_ffn = (hidden * scale_two * gain_two[None, :]).astype(BF16)
    gate_up = dot_nn(normed_ffn, full_gate_up)
    ff = gate_up.shape[1] // 2
    gate, upper = gate_up[:, :ff], gate_up[:, ff:]
    sig_gate = jax.nn.sigmoid(gate)
    silu_gate = gate * sig_gate
    activ = (silu_gate * upper).astype(BF16)
    result = hidden + dot_nn(activ, full_down)

    grad_out = cotangent[0]
    down = Reduction(activ, grad_out)
    grad_act = time_steps(grad_out, full_down)
    grad_gate = (grad_act * upper * sig_gate * (1.0 + gate * (1.0 - sig_gate))).astype(BF16)
    grad_up = (grad_act * silu_gate).astype(BF16)
    grad_gate_up = jnp.concatenate([grad_gate, grad_up], axis=1)
    gate_up_sum = Reduction(normed_ffn, grad_gate_up)
    grad_n2 = time_steps(grad_gate_up, full_gate_up)
    scaled_two = grad_n2 * gain_two[None, :]
    grad_hidden = (
        grad_out.astype(F32)
        + scale_two * scaled_two
        - hidden * scale_two**3 * jnp.mean(scaled_two * hidden, axis=-1, keepdims=True)
    )
    gate_up_sum.over_x()
    down.first_over_y(tokens=[gate_up_sum.sent])
    grad_hid_b = after(grad_hidden.astype(BF16), gate_up_sum.sent, down.sent)
    both_grad = time_steps(grad_hid_b, full_omo)
    grad_y, grad_z, own_grad, grad_message, grad_attn = mamba_gate_back(
        both_grad, gate_z, y_total, c_mat, decay, own_state
    )
    omo = Reduction(both, grad_hid_b)
    z_sum = Reduction(normed, grad_z)
    scan = Scan(own_grad, grad_message, False)
    backs = []

    def back(j, tokens):
        backs.append(
            attend_back(
                attn_scalars,
                query,
                grad_attn,
                attended[j][1],
                attended[j][2],
                kv_all[j],
                doc_row,
                j,
                tokens,
            )
        )

    down.hold(grad_attn)
    down.then_over_x()
    backs = []

    def back(j, tokens):
        backs.append(
            attend_back(
                attn_scalars,
                query,
                grad_attn,
                attended[j][1],
                attended[j][2],
                kv_all[j],
                doc_row,
                j,
                tokens,
            )
        )

    scan.step()
    gate_up_sum.hold(scan.send)
    gate_up_sum.then_over_y()
    omo.first_over_y(tokens=[gate_up_sum.sent])
    z_sum.over_x()
    grad_n1_z = time_steps(grad_z, full_z)
    scan.step([gate_up_sum.sent])
    gate_up_sum.hold(scan.send)
    down.hold(scan.send)
    ffn = Pack([(gate_up_sum.kept, gate_up_sum.got), (down.kept, down.got)])
    ffn.over_z()
    back(0, [scan.send, ffn.sent, omo.sent, z_sum.sent, grad_n1_z])
    first_done = backs[0][0]
    for part in (ffn, omo, z_sum):
        part.hold(first_done)
    state_grad = scan.finish([first_done])
    ffn.rest()
    omo.then_over_x()
    z_sum.then_over_y()
    first_kv = BlockSums(backs[0][1])
    first_kv.sent = first_kv.blocks[first_kv.blocks.shape[0] // 2 :]
    grad_mixed, tail, edge_grad, grad_dt, grad_conv, grad_heads = mamba_back(
        scalars,
        edge,
        mixed_in,
        dt_raw,
        doc_col,
        doc_row,
        conv_pack,
        head_pack,
        skip_wide,
        grad_y,
        y_total,
        state_true,
        state_grad,
        [ffn.sent, z_sum.sent, omo.sent, first_kv.sent, first_done],
    )
    third_done = grad_dt
    for part in (ffn, omo, z_sum):
        part.hold(third_done)
    first_kv.step((), [third_done])
    mixer = Pack([(z_sum.kept, z_sum.got), (omo.kept, omo.got)])
    mixer.over_z()
    behind = shift_along(edge_grad, "ctx", -1)
    grad_mixed = grad_mixed.at[rows - 8 :].set((tail + behind).astype(BF16))
    grad_xbc = jnp.concatenate([grad_mixed, grad_dt], axis=1)
    fsdp_rank = lax.axis_index("fsdp")
    conv_width, heads_width = conv_b.shape[0], dt_bias.shape[0]
    small_width = -(-(conv_width * (CONV + 1) + heads_width * 3) // rows_in)
    small_at = CHANNELS + MAMBA_HEADS
    blocks = [
        g.reshape(g.shape[0], ranks, -1).transpose(1, 0, 2).reshape(ranks, -1)
        for g in (grad_conv[: CONV + 1], grad_heads[:3, :MAMBA_HEADS])
    ]
    small_grad = jnp.concatenate(blocks, axis=1)
    small_count = small_grad.shape[1]
    small_grad = jnp.pad(small_grad, ((0, 0), (0, small_width * rows_in - small_count)))
    small_grad = jnp.pad(
        small_grad.reshape(ranks, rows_in, small_width),
        ((0, 0), (0, 0), (small_at, wide_in - small_at - small_width)),
    )
    block_of = lambda k: lax.dynamic_index_in_dim(small_grad, fsdp_rank ^ k, 0, False)
    more = [
        [(block_of(0), 0)],
        [(block_of(2), 0)],
        [(jnp.concatenate([block_of(1), block_of(3)], axis=0), 0)],
    ]
    xbc_sum = Reduction(normed, grad_xbc, more)
    grad_n1_xbc = time_steps(grad_xbc, full_xbc)
    xbc_sum.over_x()
    ffn.back_z((), [xbc_sum.sent])
    back(1, [xbc_sum.sent, mixer.sent, ffn.own, first_kv.blocks, grad_n1_xbc, third_done])
    second_done = backs[1][0]
    ff = w_gate.shape[1]
    grad_w_gate, grad_w_up, grad_w_down = ffn.back_y(
        [
            (0, 0, rows_in, 0, ff),
            (0, 0, rows_in, ff, 2 * ff),
            (1, 0, w_down.shape[0], 0, model),
        ],
        (),
        [second_done],
    )
    xbc_sum.hold(second_done)
    mixer.hold(second_done)
    first_kv.step((), [second_done])
    second_kv = BlockSums(backs[1][1])
    second_kv.step((), [grad_w_down])
    y_in = [second_kv.blocks]
    xbc_sum.then_over_y()
    y_left = [xbc_sum.sent]
    xbc = Pack([(xbc_sum.kept, after(xbc_sum.got, *y_in))])
    second_kv.step(y_left)
    z_in = [second_kv.blocks]
    first_kv.step((), y_in)
    grad_kv0, grad_kv1 = first_kv.finish(), second_kv.finish()
    grad_qkv = rope_back(backs[0][0], backs[1][0], grad_kv0, grad_kv1, cosine, sine)
    qkv_sum = Reduction(normed, grad_qkv)
    core_left = [qkv_sum.sent]
    xbc.over_z((), core_left)
    mixer.rest((), core_left)
    qkv_sum.over_x()
    x_left = [qkv_sum.sent]
    qkv_sum.then_over_y()
    y_left = [qkv_sum.sent]
    xbc.rest((), y_left)
    mixer.back_z((), y_left)
    qkv = Pack([(qkv_sum.kept, after(qkv_sum.got, mixer.own))])
    qkv.over_z()
    z_left = [qkv.sent]
    xbc.back_z((), z_left)
    omo_rows = shard_omo.shape[0]
    mixer_outs = [
        (0, 0, rows_in, 0, w_z.shape[1]),
        (1, 0, o_rows, 0, model),
        (1, o_rows, omo_rows, 0, model),
    ]
    qkv.rest()
    qkv.back_z()
    join_left = [qkv.own]
    grad_w_q, grad_w_kv = qkv.back_y(
        [(0, 0, rows_in, 0, q_width), (0, 0, rows_in, q_width, qkv_raw.shape[1])]
    )
    grad_w_z, grad_w_o, grad_w_mo = mixer.back_y(mixer_outs, (), join_left)
    grad_w_xbc, grad_w_dt = xbc.back_y(
        [(0, 0, rows_in, 0, CHANNELS), (0, 0, rows_in, CHANNELS, wide_in)], (), join_left
    )
    small_own = grad_w_dt[:, small_at - CHANNELS : small_at - CHANNELS + small_width].reshape(-1)[:small_count]
    conv_own = small_own[: conv_width * (CONV + 1)].reshape(CONV + 1, conv_width)
    heads_own = small_own[conv_width * (CONV + 1) :].reshape(3, heads_width)
    grad_n1 = (
        grad_n1_z
        + grad_n1_xbc
        + time_steps(after(grad_qkv, *x_left), full_qkv)
    )
    scaled_one = grad_n1 * full_gain_mix[None, :]
    grad_tokens = (
        grad_hidden
        + scale_one * scaled_one
        - inputs * scale_one**3 * jnp.mean(scaled_one * inputs, axis=-1, keepdims=True)
    )
    row_sums = lambda grad, weight: jnp.sum(grad * weight.astype(F32), axis=1)
    grad_gain_ffn = (
        row_sums(grad_w_gate, w_gate) + row_sums(grad_w_up, w_up)
    ) / gain_ffn.astype(F32)
    grad_gain_mix = (
        row_sums(grad_w_z, w_z)
        + row_sums(grad_w_xbc, w_xbc)
        + row_sums(grad_w_dt[:, :MAMBA_HEADS], w_dt)
        + row_sums(grad_w_q, w_q)
        + row_sums(grad_w_kv, key_value_weight)
    ) / gain_mix.astype(F32)
    totals = (
        grad_gain_mix,
        grad_w_z,
        grad_w_xbc,
        grad_w_dt[:, :MAMBA_HEADS],
        conv_own[:CONV],
        conv_own[CONV],
        heads_own[0],
        heads_own[1],
        heads_own[2],
        grad_w_mo,
        grad_w_q,
        grad_w_kv,
        grad_w_o,
        grad_gain_ffn,
        grad_w_gate,
        grad_w_up,
        grad_w_down,
    )
    return (result.astype(BF16)[None], grad_tokens[None]) + totals


def solution(mesh):
    in_specs = (
        P("fsdp", "ctx", None),
        P("fsdp", "ctx", None),
        P("fsdp", None),
        P("fsdp"),
        P("fsdp", None),
        P("fsdp", None),
        P("fsdp", None),
        P(None, "fsdp"),
        P("fsdp"),
        P("fsdp"),
        P("fsdp"),
        P("fsdp"),
        P("fsdp", None),
        P("fsdp", None),
        P("fsdp", None),
        P("fsdp", None),
        P("fsdp"),
        P("fsdp", None),
        P("fsdp", None),
        P("fsdp", None),
    )
    out_specs = (
        P("fsdp", "ctx", None),
        P("fsdp", "ctx", None),
        P("fsdp"),
        P("fsdp", None),
        P("fsdp", None),
        P("fsdp", None),
        P(None, "fsdp"),
        P("fsdp"),
        P("fsdp"),
        P("fsdp"),
        P("fsdp"),
        P("fsdp", None),
        P("fsdp", None),
        P("fsdp", None),
        P("fsdp", None),
        P("fsdp"),
        P("fsdp", None),
        P("fsdp", None),
        P("fsdp", None),
    )
    return jax.shard_map(local, mesh=mesh, in_specs=in_specs, out_specs=out_specs, check_vma=False)
```

```python
import functools
import math

import jax
import jax.numpy as jnp
from jax import lax
from jax.experimental import pallas as pl
from jax.experimental.pallas import tpu as pltpu
from jax.sharding import PartitionSpec as P

MAMBA_HEADS = 24
MAMBA_HEAD_SIZE = 64
STATE_SIZE = 128
CONV = 4
QUERY_HEADS = 8
KEY_VALUE_HEADS = 2
HEAD_SIZE = 64
MAMBA_INNER = MAMBA_HEADS * MAMBA_HEAD_SIZE
CHANNELS = MAMBA_INNER + 2 * STATE_SIZE
LANES = 128
PAIRS = MAMBA_INNER // LANES
CHUNK = 128
KEY_BLOCK = 512
QUERY_TILE = 256
GROUP = QUERY_HEADS // KEY_VALUE_HEADS
MESSAGE_ROWS = STATE_SIZE + 16
VMEM_LIMIT = 56 * 1024 * 1024

EPSILON = 1e-06
ROPE_BASE = 10000.0
MASK_FILLER = -1e30
HIGHEST = lax.Precision.HIGHEST
F32 = jnp.float32
BF16 = jnp.bfloat16


def dot_nn(a, b, precision=None):
    return lax.dot_general(
        a, b, (((1,), (0,)), ((), ())), precision=precision, preferred_element_type=F32
    )


def dot_nt(a, b):
    return lax.dot_general(a, b, (((1,), (1,)), ((), ())), preferred_element_type=F32)


def dot_tn(a, b):
    return lax.dot_general(a, b, (((0,), (0,)), ((), ())), preferred_element_type=F32)


def iota(shape, dim):
    return lax.broadcasted_iota(jnp.int32, shape, dim)


def params(*semantics):
    return pltpu.CompilerParams(dimension_semantics=semantics, vmem_limit_bytes=VMEM_LIMIT)


def lasting(microseconds):
    return pl.CostEstimate(flops=int(microseconds * 1.15e9), bytes_accessed=0, transcendentals=0)


def without(kernel, at, count):
    def body(*refs):
        kernel(*refs[:at], *refs[at + count :])

    return body


def unread(arrays):
    return [pl.BlockSpec(memory_space=pl.ANY)] * len(arrays)


def whole(shape):
    return pl.BlockSpec(shape, lambda *_: (0,) * len(shape))


def low_half(rows):
    return iota((rows, LANES), 1) < MAMBA_HEAD_SIZE


def spread(values, pair, low):
    a = values[:, 2 * pair : 2 * pair + 1]
    b = values[:, 2 * pair + 1 : 2 * pair + 2]
    return jnp.where(low, a, b)


def tile(i):
    return slice(i * LANES, (i + 1) * LANES)


def split_pair(x, low):
    zero = jnp.zeros_like(x)
    return jnp.concatenate([jnp.where(low, x, zero), jnp.where(low, zero, x)], axis=0)


def fill_padded(xs_ref, edge_ref, mixed_ref):
    xs_ref[0:8, :] = edge_ref[...]
    xs_ref[8:, :] = mixed_ref[...].astype(F32)


def lag_masks(positions, doc):
    return [None] + [(positions - lag >= doc).astype(F32) for lag in range(1, CONV)]


def conv_tile(xs_ref, start, i, cw_ref, masks):
    window = xs_ref[pl.ds(start, CHUNK + 8), tile(i)]
    summed = cw_ref[4:5, tile(i)] + cw_ref[3:4, tile(i)] * window[8 : 8 + CHUNK]
    for lag in range(1, CONV):
        shifted = window[8 - lag : 8 - lag + CHUNK]
        summed = summed + cw_ref[3 - lag : 4 - lag, tile(i)] * (shifted * masks[lag])
    return summed


def softplus(v):
    return jnp.maximum(v, 0.0) + jnp.log1p(jnp.exp(-jnp.abs(v)))


def decay_sums(dt_ref, hp_ref):
    raw = dt_ref[...] + hp_ref[0:1, :]
    step = softplus(raw)
    log_decay = step * hp_ref[1:2, :]
    order = iota((CHUNK, CHUNK), 0) >= iota((CHUNK, CHUNK), 1)
    cumul = dot_nn(order.astype(F32), log_decay, HIGHEST)
    return raw, step, log_decay, cumul


def mamba_forward_kernel(
    sc_ref,
    edge_ref,
    mixed_ref,
    dt_ref,
    doc_ref,
    cw_ref,
    hp_ref,
    skip_ref,
    y_ref,
    sin_ref,
    msg_ref,
    own_ref,
    dec_ref,
    c_ref,
    xs_ref,
    xa_ref,
    state_ref,
    carry_ref,
):
    c = pl.program_id(0)
    count = pl.num_programs(0)

    @pl.when(c == 0)
    def _():
        fill_padded(xs_ref, edge_ref, mixed_ref)
        state_ref[...] = jnp.zeros_like(state_ref)
        carry_ref[...] = jnp.zeros_like(carry_ref)

    base = sc_ref[count]
    start = pl.multiple_of(c * CHUNK, CHUNK)
    first = base + start
    end_doc = sc_ref[c]
    doc = doc_ref[...]
    positions = first + iota((CHUNK, 1), 0)
    masks = lag_masks(positions, doc)
    for i in range(CHANNELS // LANES):
        summed = conv_tile(xs_ref, start, i, cw_ref, masks)
        xa_ref[:, tile(i)] = summed * jax.nn.sigmoid(summed)
    _, step, log_decay, cumul = decay_sums(dt_ref, hp_ref)
    cumul_t = cumul.T
    b_mat = xa_ref[:, tile(PAIRS)]
    c_mat = xa_ref[:, tile(PAIRS + 1)].astype(BF16)
    c_ref[...] = c_mat
    couple = dot_nt(c_mat, b_mat.astype(BF16))
    b_turned = b_mat.T.astype(BF16)
    col = first + iota((CHUNK, CHUNK), 1)
    row = first + iota((CHUNK, CHUNK), 0)
    couple = jnp.where((col <= row) & (col >= doc), couple, 0.0)
    carried = (doc < first).astype(F32)
    into = jnp.exp(cumul) * carried
    last = cumul[CHUNK - 1 : CHUNK, :]
    ending = jnp.exp(last - cumul) * (positions >= end_doc).astype(F32)
    keep = jnp.exp(last) * (end_doc < first).astype(F32)
    dec_ref[...] = jnp.where(doc < base, jnp.exp(cumul + carry_ref[0:1, :]), 0.0)
    low = low_half(CHUNK)
    low_row = low_half(1)
    for j in range(PAIRS):
        x = xa_ref[:, tile(j)]
        weighted = x * spread(step, j, low)
        mixing = []
        for h in (2 * j, 2 * j + 1):
            gap = jnp.minimum(cumul[:, h : h + 1] - cumul_t[h : h + 1, :], 0.0)
            mixing.append((couple * jnp.exp(gap)).astype(BF16))
        y = dot_nn(jnp.concatenate(mixing, axis=1), split_pair(weighted.astype(BF16), low))
        state = state_ref[:, tile(j)]
        sin_ref[0, :, tile(j)] = state
        y = y + dot_nn(c_mat, state.astype(BF16)) * spread(into, j, low)
        y_ref[:, tile(j)] = y + skip_ref[0:1, tile(j)] * x
        fresh = dot_nn(b_turned, (weighted * spread(ending, j, low)).astype(BF16))
        state_ref[:, tile(j)] = fresh + state * spread(keep, j, low_row)
    carry_ref[...] = carry_ref[...] + last

    @pl.when(c == count - 1)
    def _():
        msg_ref[0:STATE_SIZE, :] = state_ref[...].astype(BF16)
        own_ref[0:STATE_SIZE, :] = state_ref[...]
        through = jnp.exp(carry_ref[...]) * (end_doc < base).astype(F32)
        low8 = low_half(8)
        for j in range(PAIRS):
            wide = spread(through, j, low8)
            wide = jnp.concatenate([wide, wide], axis=0)
            msg_ref[STATE_SIZE:, tile(j)] = wide.astype(BF16)
            own_ref[STATE_SIZE:, tile(j)] = wide


def mamba_forward(
    scalars, edge, mixed, dt_raw, doc, conv_pack, head_pack, skip_wide, tokens=()
):
    rows = mixed.shape[0]
    count = rows // CHUNK
    by_chunk = lambda width: pl.BlockSpec((CHUNK, width), lambda c: (c, 0))
    return pl.pallas_call(
        without(mamba_forward_kernel, 8, len(tokens)),
        grid=(count,),
        in_specs=[
            pl.BlockSpec(memory_space=pltpu.SMEM),
            whole((8, CHANNELS)),
            whole((rows, CHANNELS)),
            by_chunk(LANES),
            by_chunk(1),
            whole((8, CHANNELS)),
            whole((8, LANES)),
            whole((1, MAMBA_INNER)),
            *unread(tokens),
        ],
        out_specs=[
            by_chunk(MAMBA_INNER),
            pl.BlockSpec((1, STATE_SIZE, MAMBA_INNER), lambda c: (c, 0, 0)),
            whole((MESSAGE_ROWS, MAMBA_INNER)),
            whole((MESSAGE_ROWS, MAMBA_INNER)),
            by_chunk(LANES),
            by_chunk(LANES),
        ],
        out_shape=[
            jax.ShapeDtypeStruct((rows, MAMBA_INNER), F32),
            jax.ShapeDtypeStruct((count, STATE_SIZE, MAMBA_INNER), F32),
            jax.ShapeDtypeStruct((MESSAGE_ROWS, MAMBA_INNER), BF16),
            jax.ShapeDtypeStruct((MESSAGE_ROWS, MAMBA_INNER), F32),
            jax.ShapeDtypeStruct((rows, LANES), F32),
            jax.ShapeDtypeStruct((rows, LANES), BF16),
        ],
        scratch_shapes=[
            pltpu.VMEM((rows + 8, CHANNELS), F32),
            pltpu.VMEM((CHUNK, CHANNELS), F32),
            pltpu.VMEM((STATE_SIZE, MAMBA_INNER), F32),
            pltpu.VMEM((8, LANES), F32),
        ],
        compiler_params=params("arbitrary"),
        cost_estimate=lasting(13),
        name="mamba_forward",
    )(scalars, edge, mixed, dt_raw, doc, conv_pack, head_pack, skip_wide, *tokens)


QUARTERS = 4
BLOCK_TILES = 1 + PAIRS // QUARTERS


def attn_tile(i):
    return tile(i * BLOCK_TILES)


def gated_tile(j):
    per = PAIRS // QUARTERS
    return tile(j // per * BLOCK_TILES + 1 + j % per)


def mamba_correct_kernel(
    y_ref, sin_ref, c_ref, dec_ref, state_ref, z_ref, vec0_ref, vec1_ref, total_ref, both_ref, true_ref, edge_ref
):
    c = pl.program_id(0)

    @pl.when(c == 0)
    def _():
        edge_ref[...] = jnp.ones_like(edge_ref)

    low = low_half(CHUNK)
    low_row = low_half(1)
    decay = dec_ref[...]
    before = edge_ref[0:1, :]
    c_mat = c_ref[...]
    for j in range(PAIRS):
        state = state_ref[:, tile(j)]
        y = y_ref[:, tile(j)] + dot_nn(c_mat, state.astype(BF16)) * spread(decay, j, low)
        total_ref[:, tile(j)] = y
        z = z_ref[:, tile(j)]
        both_ref[:, gated_tile(j)] = (y * (z * jax.nn.sigmoid(z))).astype(BF16)
        true_ref[0, :, tile(j)] = (
            sin_ref[0, :, tile(j)] + state * spread(before, j, low_row)
        ).astype(BF16)
    for i, vec_ref in enumerate((vec0_ref, vec0_ref, vec1_ref, vec1_ref)):
        both_ref[:, attn_tile(i)] = vec_ref[:, tile(i % 2)]
    edge_ref[0:1, :] = decay[CHUNK - 1 : CHUNK, :]


def mamba_correct(y, sin, c_mat, decay, state_in, gate_z, vec0, vec1):
    rows = y.shape[0]
    count = rows // CHUNK
    by_chunk = lambda width: pl.BlockSpec((CHUNK, width), lambda c: (c, 0))
    states = pl.BlockSpec((1, STATE_SIZE, MAMBA_INNER), lambda c: (c, 0, 0))
    return pl.pallas_call(
        mamba_correct_kernel,
        grid=(count,),
        in_specs=[
            by_chunk(MAMBA_INNER),
            states,
            by_chunk(LANES),
            by_chunk(LANES),
            whole((STATE_SIZE, MAMBA_INNER)),
            by_chunk(MAMBA_INNER),
            by_chunk(2 * LANES),
            by_chunk(2 * LANES),
        ],
        out_specs=[by_chunk(MAMBA_INNER), by_chunk(QUARTERS * BLOCK_TILES * LANES), states],
        out_shape=[
            jax.ShapeDtypeStruct((rows, MAMBA_INNER), F32),
            jax.ShapeDtypeStruct((rows, QUARTERS * BLOCK_TILES * LANES), BF16),
            jax.ShapeDtypeStruct((count, STATE_SIZE, MAMBA_INNER), BF16),
        ],
        scratch_shapes=[pltpu.VMEM((8, LANES), F32)],
        compiler_params=params("arbitrary"),
        cost_estimate=lasting(8.5),
        name="mamba_correct",
    )(y, sin, c_mat, decay, state_in, gate_z, vec0, vec1)


def mamba_gate_back_kernel(
    both_ref, z_ref, y_ref, c_ref, dec_ref, own_ref, dy_ref, gz_ref, gsi_ref, gsb_ref, gvec_ref, acc_ref
):
    c = pl.program_id(0)

    @pl.when(c == 0)
    def _():
        acc_ref[...] = jnp.zeros_like(acc_ref)

    low = low_half(CHUNK)
    decay = dec_ref[...]
    c_turned = c_ref[...].astype(F32).T.astype(BF16)
    for j in range(PAIRS):
        z = z_ref[:, tile(j)]
        sig = jax.nn.sigmoid(z)
        silu = z * sig
        grad = both_ref[:, gated_tile(j)].astype(F32)
        gz_ref[:, tile(j)] = (grad * y_ref[:, tile(j)] * (sig + silu * (1.0 - sig))).astype(BF16)
        dy = (grad * silu).astype(BF16)
        dy_ref[:, tile(j)] = dy
        scaled = (dy.astype(F32) * spread(decay, j, low)).astype(BF16)
        acc_ref[:, tile(j)] += dot_nn(c_turned, scaled)
    for i in range(QUARTERS):
        gvec_ref[:, tile(i)] = both_ref[:, attn_tile(i)]

    @pl.when(c == pl.num_programs(0) - 1)
    def _():
        gsi_ref[0:STATE_SIZE, :] = acc_ref[...]
        gsb_ref[0:STATE_SIZE, :] = acc_ref[...].astype(BF16)
        gsi_ref[STATE_SIZE:, :] = own_ref[...]
        gsb_ref[STATE_SIZE:, :] = own_ref[...].astype(BF16)


def mamba_gate_back(both_grad, gate_z, total, c_mat, decay, own, tokens=()):
    rows = total.shape[0]
    by_chunk = lambda width: pl.BlockSpec((CHUNK, width), lambda c: (c, 0))
    return pl.pallas_call(
        without(mamba_gate_back_kernel, 6, len(tokens)),
        grid=(rows // CHUNK,),
        in_specs=[
            by_chunk(QUARTERS * BLOCK_TILES * LANES),
            by_chunk(MAMBA_INNER),
            by_chunk(MAMBA_INNER),
            by_chunk(LANES),
            by_chunk(LANES),
            pl.BlockSpec((16, MAMBA_INNER), lambda c: (STATE_SIZE // 16, 0)),
            *unread(tokens),
        ],
        out_specs=[
            by_chunk(MAMBA_INNER),
            by_chunk(MAMBA_INNER),
            whole((MESSAGE_ROWS, MAMBA_INNER)),
            whole((MESSAGE_ROWS, MAMBA_INNER)),
            by_chunk(QUARTERS * LANES),
        ],
        out_shape=[
            jax.ShapeDtypeStruct((rows, MAMBA_INNER), BF16),
            jax.ShapeDtypeStruct((rows, MAMBA_INNER), BF16),
            jax.ShapeDtypeStruct((MESSAGE_ROWS, MAMBA_INNER), F32),
            jax.ShapeDtypeStruct((MESSAGE_ROWS, MAMBA_INNER), BF16),
            jax.ShapeDtypeStruct((rows, QUARTERS * LANES), BF16),
        ],
        scratch_shapes=[pltpu.VMEM((STATE_SIZE, MAMBA_INNER), F32)],
        compiler_params=params("arbitrary"),
        cost_estimate=lasting(7.5),
        name="mamba_gate_back",
    )(both_grad, gate_z, total, c_mat, decay, own, *tokens)


def picks(pair):
    channel = iota((LANES, LANES), 0)
    head = iota((LANES, LANES), 1)
    return (head == 2 * pair + channel // MAMBA_HEAD_SIZE).astype(BF16)


def head_sums(product, select):
    high = product.astype(BF16)
    rest = (product - high.astype(F32)).astype(BF16)
    return dot_nn(high, select) + dot_nn(rest, select)


def mamba_back_kernel(
    sc_ref,
    edge_ref,
    mixed_ref,
    dt_ref,
    doc_ref,
    doc_row_ref,
    cw_ref,
    hp_ref,
    skip_ref,
    dy_ref,
    y_ref,
    sin_ref,
    ds_end_ref,
    gmix_ref,
    tail_ref,
    edge_grad_ref,
    gconv_ref,
    ghead_ref,
    xs_ref,
    xa_ref,
    slope_ref,
    grad_ref,
    ds_ref,
    rows_ref,
):
    step_at = pl.program_id(0)
    count = pl.num_programs(0)
    c = count - 1 - step_at
    rows = count * CHUNK

    @pl.when(step_at == 0)
    def _():
        fill_padded(xs_ref, edge_ref, mixed_ref)
        ds_ref[...] = ds_end_ref[...]
        grad_ref[pl.ds(rows, 8), :] = jnp.zeros((8, CHANNELS), F32)
        gconv_ref[...] = jnp.zeros_like(gconv_ref)
        ghead_ref[...] = jnp.zeros_like(ghead_ref)
        rows_ref[...] = jnp.zeros_like(rows_ref)

    base = sc_ref[count]
    start = pl.multiple_of(c * CHUNK, CHUNK)
    first = base + start
    end_doc = sc_ref[c]
    doc_window = doc_ref[pl.ds(start, CHUNK + 8), :]
    doc = doc_window[0:CHUNK]
    positions_window = first + iota((CHUNK + 8, 1), 0)
    positions = positions_window[0:CHUNK]
    masks_window = lag_masks(positions_window, doc_window)
    masks = [None] + [m[0:CHUNK] for m in masks_window[1:]]
    for i in range(CHANNELS // LANES):
        summed = conv_tile(xs_ref, start, i, cw_ref, masks)
        sig = jax.nn.sigmoid(summed)
        act = summed * sig
        xa_ref[:, tile(i)] = act
        slope_ref[:, tile(i)] = sig + act * (1.0 - sig)
    raw, step, log_decay, cumul = decay_sums(dt_ref, hp_ref)
    cumul_t = cumul.T
    b_mat = xa_ref[:, tile(PAIRS)].astype(BF16)
    c_f32 = xa_ref[:, tile(PAIRS + 1)]
    c_mat = c_f32.astype(BF16)
    c_turned = c_f32.T.astype(BF16)
    key = first + iota((CHUNK, CHUNK), 0)
    query = first + iota((CHUNK, CHUNK), 1)
    visible = (key <= query) & (key >= doc_row_ref[0:1, :])
    couple = jnp.where(visible, dot_nt(b_mat, c_mat), 0.0)
    carried = (doc < first).astype(F32)
    into = jnp.exp(cumul) * carried
    last = cumul[CHUNK - 1 : CHUNK, :]
    ending = jnp.exp(last - cumul) * (positions >= end_doc).astype(F32)
    keep = jnp.exp(last) * (end_doc < first).astype(F32)
    low = low_half(CHUNK)
    low_row = low_half(1)
    grad_couple = jnp.zeros((CHUNK, CHUNK), F32)
    grad_b = jnp.zeros((CHUNK, STATE_SIZE), F32)
    grad_c = jnp.zeros((CHUNK, STATE_SIZE), F32)
    grad_cumul = jnp.zeros((CHUNK, LANES), F32)
    grad_step = jnp.zeros((CHUNK, LANES), F32)
    end_sums = jnp.zeros((8, LANES), F32)
    for j in range(PAIRS):
        select = picks(j)
        x = xa_ref[:, tile(j)]
        step_wide = spread(step, j, low)
        weighted = x * step_wide
        weighted_b = weighted.astype(BF16)
        dy = dy_ref[:, tile(j)]
        dy_f32 = dy.astype(F32)
        grad_mixing = dot_nt(split_pair(weighted_b, low), dy)
        mixing = []
        for side, h in enumerate((2 * j, 2 * j + 1)):
            gap = jnp.minimum(cumul_t[h : h + 1, :] - cumul[:, h : h + 1], 0.0)
            fade = jnp.exp(gap)
            mixing.append((couple * fade).astype(BF16))
            grad_couple += grad_mixing[side * CHUNK : (side + 1) * CHUNK] * fade
        grad_weighted = dot_nn(jnp.concatenate(mixing, axis=1), split_pair(dy, low))
        ending_wide = spread(ending, j, low)
        grad_state = ds_ref[:, tile(j)]
        grad_state_b = grad_state.astype(BF16)
        state = sin_ref[0, :, tile(j)]
        through_state = ending_wide * dot_nn(b_mat, grad_state_b)
        grad_weighted = grad_weighted + through_state
        dy_into = (dy_f32 * spread(into, j, low)).astype(BF16)
        grad_c += dot_nt(dy_into, state)
        grad_b += dot_nt((weighted * ending_wide).astype(BF16), grad_state_b)
        keep_wide = spread(keep, j, low_row)
        weighted_f32 = weighted_b.astype(F32)
        to_end = jnp.sum(weighted_f32 * through_state, axis=0, keepdims=True) + keep_wide * jnp.sum(
            grad_state * state.astype(F32), axis=0, keepdims=True
        )
        ds_ref[:, tile(j)] = keep_wide * grad_state + dot_nn(c_turned, dy_into)
        skip = skip_ref[0:1, tile(j)]
        grad_x = step_wide * grad_weighted + skip * dy_f32
        grad_ref[pl.ds(start, CHUNK), tile(j)] = grad_x * slope_ref[:, tile(j)]
        rows_ref[0:1, tile(j)] += jnp.sum(dy_f32 * x, axis=0, keepdims=True)
        in_out = dy_f32 * (y_ref[:, tile(j)] - skip * x) - weighted_f32 * grad_weighted
        grad_cumul += head_sums(in_out, select)
        grad_step += head_sums(grad_weighted * x, select)
        end_sums += head_sums(jnp.broadcast_to(to_end, (8, LANES)), select)
    grad_couple = jnp.where(visible, grad_couple, 0.0).astype(BF16)
    grad_b += dot_nn(grad_couple, c_mat)
    grad_c += dot_tn(grad_couple, b_mat)
    grad_ref[pl.ds(start, CHUNK), tile(PAIRS)] = grad_b * slope_ref[:, tile(PAIRS)]
    grad_ref[pl.ds(start, CHUNK), tile(PAIRS + 1)] = grad_c * slope_ref[:, tile(PAIRS + 1)]
    later = (iota((CHUNK, CHUNK), 0) <= iota((CHUNK, CHUNK), 1)).astype(F32)
    grad_log = dot_nn(later, grad_cumul, HIGHEST) + end_sums[0:1, :]
    grad_raw = (grad_step + grad_log * hp_ref[1:2, :]) * jax.nn.sigmoid(raw)
    gmix_ref[:, tile(CHANNELS // LANES)] = grad_raw.astype(BF16)
    ghead_ref[0:1, :] += jnp.sum(grad_raw, axis=0, keepdims=True)
    ghead_ref[1:2, :] += jnp.sum(grad_log * log_decay, axis=0, keepdims=True)
    for i in range(CHANNELS // LANES):
        window = grad_ref[pl.ds(start, CHUNK + 8), tile(i)]
        own = window[0:CHUNK]
        padded = xs_ref[pl.ds(start, CHUNK + 8), tile(i)]
        total = cw_ref[3:4, tile(i)] * own
        gconv_ref[4:5, tile(i)] += jnp.sum(own, axis=0, keepdims=True)
        gconv_ref[3:4, tile(i)] += jnp.sum(own * padded[8 : 8 + CHUNK], axis=0, keepdims=True)
        for lag in range(1, CONV):
            masked = window * masks_window[lag]
            total = total + cw_ref[3 - lag : 4 - lag, tile(i)] * masked[lag : lag + CHUNK]
            gconv_ref[3 - lag : 4 - lag, tile(i)] += jnp.sum(
                masked[0:CHUNK] * padded[8 - lag : 8 - lag + CHUNK], axis=0, keepdims=True
            )
        gmix_ref[:, tile(i)] = total.astype(BF16)

        @pl.when(step_at == 0)
        def _():
            tail_ref[:, tile(i)] = total[CHUNK - 8 :]

        @pl.when(step_at == count - 1)
        def _():
            ahead = jnp.zeros((8, LANES), F32)
            for lag in range(1, CONV):
                head = jnp.concatenate(
                    [jnp.zeros((8, LANES), F32), window[0:8] * masks_window[lag][0:8]], axis=0
                )
                ahead = ahead + cw_ref[3 - lag : 4 - lag, tile(i)] * head[lag : lag + 8]
            edge_grad_ref[:, tile(i)] = ahead

    @pl.when(step_at == count - 1)
    def _():
        total = jnp.zeros((8, LANES), F32)
        for j in range(PAIRS):
            total += head_sums(rows_ref[:, tile(j)], picks(j))
        ghead_ref[2:3, :] = total[0:1, :]


def mamba_back(
    scalars,
    edge,
    mixed,
    dt_raw,
    doc,
    doc_row,
    conv_pack,
    head_pack,
    skip_wide,
    dy,
    y,
    sin,
    ds_end,
    tokens=(),
):
    rows = mixed.shape[0]
    count = rows // CHUNK
    by_chunk = lambda width: pl.BlockSpec((CHUNK, width), lambda i: (count - 1 - i, 0))
    return pl.pallas_call(
        without(mamba_back_kernel, 13, len(tokens)),
        grid=(count,),
        in_specs=[
            pl.BlockSpec(memory_space=pltpu.SMEM),
            whole((8, CHANNELS)),
            whole((rows, CHANNELS)),
            by_chunk(LANES),
            whole((rows + 8, 1)),
            pl.BlockSpec((8, CHUNK), lambda i: (0, count - 1 - i)),
            whole((8, CHANNELS)),
            whole((8, LANES)),
            whole((1, MAMBA_INNER)),
            by_chunk(MAMBA_INNER),
            by_chunk(MAMBA_INNER),
            pl.BlockSpec((1, STATE_SIZE, MAMBA_INNER), lambda i: (count - 1 - i, 0, 0)),
            whole((STATE_SIZE, MAMBA_INNER)),
            *unread(tokens),
        ],
        out_specs=[
            by_chunk(CHANNELS + LANES),
            whole((8, CHANNELS)),
            whole((8, CHANNELS)),
            whole((8, CHANNELS)),
            whole((8, LANES)),
        ],
        out_shape=[
            jax.ShapeDtypeStruct((rows, CHANNELS + LANES), BF16),
            jax.ShapeDtypeStruct((8, CHANNELS), F32),
            jax.ShapeDtypeStruct((8, CHANNELS), F32),
            jax.ShapeDtypeStruct((8, CHANNELS), F32),
            jax.ShapeDtypeStruct((8, LANES), F32),
        ],
        scratch_shapes=[
            pltpu.VMEM((rows + 8, CHANNELS), F32),
            pltpu.VMEM((CHUNK, CHANNELS), F32),
            pltpu.VMEM((CHUNK, CHANNELS), F32),
            pltpu.VMEM((rows + 8, CHANNELS), F32),
            pltpu.VMEM((STATE_SIZE, MAMBA_INNER), F32),
            pltpu.VMEM((8, MAMBA_INNER), F32),
        ],
        compiler_params=params("arbitrary"),
        cost_estimate=lasting(25),
        name="mamba_back",
    )(
        scalars,
        edge,
        mixed,
        dt_raw,
        doc,
        doc_row,
        conv_pack,
        head_pack,
        skip_wide,
        dy,
        y,
        sin,
        ds_end,
        *tokens,
    )


def scan_step_kernel(begins, ends, flag_ref, *refs):
    total_ref, refs = refs[0], refs[1:]
    seen_ref, refs = (None, refs) if begins else (refs[0], refs[1:])
    got_ref, out_ref = refs[0], refs[-1]
    first = flag_ref[0] == 1
    rows = slice(0, STATE_SIZE)
    rest = slice(STATE_SIZE, MESSAGE_ROWS)
    one = STATE_SIZE
    for j in range(PAIRS):
        got = got_ref[:, tile(j)].astype(F32)
        if begins:
            out_ref[rows, tile(j)] = jnp.where(first, got[rows], 0.0)
            out_ref[rest, tile(j)] = jnp.where(first, got[rest], 1.0)
        else:
            seen = seen_ref[:, tile(j)]
            passed = seen[rows] + seen[one : one + 1] * got[rows]
            out_ref[rows, tile(j)] = jnp.where(first, passed, seen[rows])
            out_ref[rest, tile(j)] = jnp.where(first, seen[rest] * got[rest], seen[rest])
        if not ends:
            new_ref, send_ref = refs[1:3]
            total = total_ref[:, tile(j)]
            mine, theirs = total[one : one + 1], got[one : one + 1]
            state = jnp.where(first, mine * got[rows] + total[rows], theirs * total[rows] + got[rows])
            new_ref[rows, tile(j)] = state
            send_ref[rows, tile(j)] = state.astype(BF16)
            factor = total[rest] * got[rest]
            new_ref[rest, tile(j)] = factor
            send_ref[rest, tile(j)] = factor.astype(BF16)


def scan_step(first, total, seen, got, ends):
    shape = (MESSAGE_ROWS, MAMBA_INNER)
    ins = [total, got] if seen is None else [total, seen, got]
    outs = [F32] if ends else [F32, BF16, F32]
    specs = [whole(shape)] * len(ins)
    if ends:
        specs[0] = pl.BlockSpec(memory_space=pl.ANY)
    found = pl.pallas_call(
        functools.partial(scan_step_kernel, seen is None, ends),
        in_specs=[pl.BlockSpec(memory_space=pltpu.SMEM)] + specs,
        out_specs=[whole(shape)] * len(outs),
        out_shape=[jax.ShapeDtypeStruct(shape, kind) for kind in outs],
        compiler_params=pltpu.CompilerParams(vmem_limit_bytes=VMEM_LIMIT),
        cost_estimate=lasting(2.5),
        name="scan_step",
    )(first.astype(jnp.int32).reshape(1), *ins)
    return (None, None, found[0]) if ends else found


def half_roll(x):
    return pltpu.roll(x, HEAD_SIZE, 1)


def stack_low(block, rows):
    low = low_half(rows)
    parts = []
    for a in range(2):
        pair = block[:, tile(a)]
        parts.append(jnp.where(low, pair, 0.0))
        parts.append(jnp.where(low, half_roll(pair), 0.0))
    return parts


def stack_high(block, rows):
    low = low_half(rows)
    parts = []
    for a in range(2):
        pair = block[:, tile(a)]
        parts.append(jnp.where(low, 0.0, half_roll(pair)))
        parts.append(jnp.where(low, 0.0, pair))
    return parts


def tile_bounds(sc_ref, at, tiles):
    first_doc = sc_ref[at]
    last_doc = sc_ref[tiles + at]
    start = sc_ref[2 * tiles] + at * QUERY_TILE
    block_lo = first_doc // KEY_BLOCK
    block_hi = (start + QUERY_TILE - 1) // KEY_BLOCK + 1
    return start, last_doc, block_lo, block_hi


def visible_mask(block, start, doc_row):
    lanes = GROUP * QUERY_TILE
    key = block * KEY_BLOCK + iota((KEY_BLOCK, lanes), 0)
    query = start + iota((1, lanes), 1) % QUERY_TILE
    return (key <= query) & (key >= doc_row)


def attend_kernel(
    sc_ref, q_ref, kv_ref, doc_ref, vec_ref, norm_ref, lse_ref, qz_ref, max_ref, acc_ref
):
    at = pl.program_id(0)
    tiles = pl.num_programs(0)
    start, last_doc, block_lo, block_hi = tile_bounds(sc_ref, at, tiles)
    for g, part in enumerate(stack_low(q_ref[...].astype(F32), QUERY_TILE)):
        qz_ref[g * QUERY_TILE : (g + 1) * QUERY_TILE, :] = part.astype(BF16)
    max_ref[...] = jnp.full_like(max_ref, MASK_FILLER)
    acc_ref[...] = jnp.zeros_like(acc_ref)
    doc_row = jnp.concatenate([doc_ref[0:1, :]] * GROUP, axis=1)

    def visit(block, masked):
        at_rows = sc_ref[2 * tiles + 1 + block] * KEY_BLOCK
        kv = kv_ref[pl.ds(pl.multiple_of(at_rows, KEY_BLOCK), KEY_BLOCK), :]
        values = jnp.where(low_half(KEY_BLOCK), jnp.ones_like(kv), kv)
        scores = dot_nt(kv, qz_ref[...])
        if masked:
            scores = jnp.where(visible_mask(block, start, doc_row), scores, MASK_FILLER)
        before = max_ref[0:1, :]
        top = jnp.maximum(before, jnp.max(scores, axis=0, keepdims=True))
        prob = jnp.exp(scores - top)
        fade = jnp.exp(before - top)
        max_ref[0:1, :] = top
        acc_ref[...] = acc_ref[...] * fade + dot_tn(values, prob.astype(BF16))

    def one(block, carry):
        full = (block * KEY_BLOCK + KEY_BLOCK - 1 <= start) & (block * KEY_BLOCK >= last_doc)

        @pl.when(full)
        def _():
            visit(block, False)

        @pl.when(jnp.logical_not(full))
        def _():
            visit(block, True)

        return carry

    lax.fori_loop(block_lo, block_hi, one, 0)
    total = acc_ref[0:1, :]
    lse_ref[0] = jnp.broadcast_to(max_ref[0:1, :] + jnp.log(total), lse_ref.shape[1:])
    scaled = acc_ref[...] / total
    low = low_half(QUERY_TILE)
    for a in range(2):
        even = half_roll(scaled[:, (2 * a) * QUERY_TILE : (2 * a + 1) * QUERY_TILE].T)
        odd = scaled[:, (2 * a + 1) * QUERY_TILE : (2 * a + 2) * QUERY_TILE].T
        both = jnp.where(low, even, odd)
        norm_ref[:, tile(a)] = both
        vec_ref[:, tile(a)] = both.astype(BF16)


def carrying(kernel, ins, outs, parts, pieces):
    def body(*refs):
        own_ins, refs = refs[:ins], refs[ins:]
        at_ref, piece_refs, refs = refs[0], refs[1 : 1 + pieces], refs[1 + pieces :]
        own_outs, refs = refs[:outs], refs[outs:]
        places = 1 + max(part[5] for part in parts)
        place_refs, refs = refs[:places], refs[places:]
        own_scratch, held, sems = refs[: -pieces - 1], refs[-pieces - 1 : -1], refs[-1]
        step, last = pl.program_id(0), pl.num_programs(0) - 1
        come, leave = place_copies(parts, at_ref, piece_refs, place_refs, held, sems)

        @pl.when(step == 0)
        def _():
            for copy in come:
                copy.start()

        kernel(*own_ins, *own_outs, *own_scratch)

        @pl.when(step == 0)
        def _():
            for copy in come:
                copy.wait()
            for _, copy in leave:
                copy.start()

        @pl.when(step == last)
        def _():
            for _, copy in leave:
                copy.wait()

    return body


def place_copies(parts, at_ref, pieces, out_refs, held, sems):
    come = [
        pltpu.make_async_copy(piece, here, sems.at[i])
        for i, (piece, here) in enumerate(zip(pieces, held))
    ]
    leave = []
    for k, (piece, row, rows, col, cols, out) in enumerate(parts):
        here = held[piece].at[pl.ds(row, rows), pl.ds(col, cols)]
        to = out_refs[out].at[pl.ds(pl.multiple_of(at_ref[k], 16), rows), :]
        leave.append((piece, pltpu.make_async_copy(here, to, sems.at[len(pieces) + k])))
    return come, leave


def attend(scalars, q, kv, doc_row, head, tokens=(), carried=None):
    rows = q.shape[0]
    length = kv.shape[0]
    tiles = rows // QUERY_TILE
    lanes = GROUP * QUERY_TILE
    width = GROUP * HEAD_SIZE
    by_tile = pl.BlockSpec((QUERY_TILE, width), lambda t: (t, 0))
    kernel = attend_kernel
    more_in, more_out, more_shape, more_scratch, more = [], [], [], [], []
    if carried:
        pieces, parts, offsets, shapes = carried
        kernel = carrying(kernel, 4, 3, parts, len(pieces))
        more_in = [pl.BlockSpec(memory_space=pltpu.SMEM)] + unread(pieces)
        more_out = unread(shapes)
        more_shape = [jax.ShapeDtypeStruct(shape, BF16) for shape in shapes]
        more_scratch = [pltpu.VMEM(piece.shape, BF16) for piece in pieces]
        more_scratch.append(pltpu.SemaphoreType.DMA((len(pieces) + len(parts),)))
        more = [jnp.stack(offsets).astype(jnp.int32), *pieces]
    return pl.pallas_call(
        without(kernel, 4 + len(more_in), len(tokens)),
        grid=(tiles,),
        in_specs=[
            pl.BlockSpec(memory_space=pltpu.SMEM),
            pl.BlockSpec((QUERY_TILE, width), lambda t: (t, head)),
            whole((length, LANES)),
            pl.BlockSpec((8, QUERY_TILE), lambda t: (0, t)),
            *more_in,
            *unread(tokens),
        ],
        out_specs=[by_tile, by_tile, pl.BlockSpec((1, 8, lanes), lambda t: (t, 0, 0)), *more_out],
        out_shape=[
            jax.ShapeDtypeStruct((rows, width), BF16),
            jax.ShapeDtypeStruct((rows, width), F32),
            jax.ShapeDtypeStruct((tiles, 8, lanes), F32),
            *more_shape,
        ],
        scratch_shapes=[
            pltpu.VMEM((lanes, LANES), BF16),
            pltpu.VMEM((8, lanes), F32),
            pltpu.VMEM((LANES, lanes), F32),
            *more_scratch,
        ],
        compiler_params=params("arbitrary"),
        cost_estimate=lasting(18),
        name="attend",
    )(scalars, q, kv, doc_row, *more, *tokens)


def attend_back_kernel(
    sc_ref, q_ref, do_ref, norm_ref, lse_ref, kv_ref, doc_ref, dq_ref, dkv_ref, qd_ref, dkv_acc, dq_acc
):
    at = pl.program_id(0)
    tiles = pl.num_programs(0)
    lanes = GROUP * QUERY_TILE
    start, last_doc, block_lo, block_hi = tile_bounds(sc_ref, at, tiles)

    @pl.when(at == 0)
    def _():
        dkv_acc[...] = jnp.zeros_like(dkv_acc)

    grad = do_ref[...].astype(F32)
    for g, part in enumerate(stack_low(q_ref[...].astype(F32), QUERY_TILE)):
        qd_ref[g * QUERY_TILE : (g + 1) * QUERY_TILE, :] = part.astype(BF16)
    for g, part in enumerate(stack_high(grad, QUERY_TILE)):
        qd_ref[lanes + g * QUERY_TILE : lanes + (g + 1) * QUERY_TILE, :] = part.astype(BF16)
    deltas = []
    for a in range(2):
        turned = (grad[:, tile(a)] * norm_ref[:, tile(a)]).T
        deltas.append(jnp.sum(turned[0:HEAD_SIZE], axis=0, keepdims=True))
        deltas.append(jnp.sum(turned[HEAD_SIZE:], axis=0, keepdims=True))
    delta = jnp.concatenate(deltas, axis=1)
    lse = lse_ref[0, 0:1, :]
    dq_acc[...] = jnp.zeros_like(dq_acc)
    doc_row = jnp.concatenate([doc_ref[0:1, :]] * GROUP, axis=1)

    def visit(block, masked):
        first_row = sc_ref[2 * tiles + 1 + block] * KEY_BLOCK
        at_rows = pl.ds(pl.multiple_of(first_row, KEY_BLOCK), KEY_BLOCK)
        kv = kv_ref[at_rows, :]
        scores = dot_nt(kv, qd_ref[0:lanes, :])
        prob = jnp.exp(scores - lse)
        if masked:
            prob = jnp.where(visible_mask(block, start, doc_row), prob, 0.0)
        grad_prob = dot_nt(kv, qd_ref[lanes:, :])
        grad_scores = (prob * (grad_prob - delta)).astype(BF16)
        dkv_acc[at_rows, :] += dot_nn(grad_scores, qd_ref[0:lanes, :]) + dot_nn(
            prob.astype(BF16), qd_ref[lanes:, :]
        )
        dq_acc[...] += dot_tn(kv, grad_scores)

    def one(block, carry):
        full = (block * KEY_BLOCK + KEY_BLOCK - 1 <= start) & (block * KEY_BLOCK >= last_doc)

        @pl.when(full)
        def _():
            visit(block, False)

        @pl.when(jnp.logical_not(full))
        def _():
            visit(block, True)

        return carry

    lax.fori_loop(block_lo, block_hi, one, 0)
    low = low_half(QUERY_TILE)
    scale = 1.0 / math.sqrt(HEAD_SIZE)
    for a in range(2):
        even = dq_acc[:, (2 * a) * QUERY_TILE : (2 * a + 1) * QUERY_TILE].T
        odd = half_roll(dq_acc[:, (2 * a + 1) * QUERY_TILE : (2 * a + 2) * QUERY_TILE].T)
        dq_ref[:, tile(a)] = jnp.where(low, even, odd) * scale

    @pl.when(at == tiles - 1)
    def _():
        dkv_ref[...] = dkv_acc[...].astype(BF16)


def attend_back(scalars, q, grad, norm, lse, kv, doc_row, head, tokens=()):
    rows = q.shape[0]
    length = kv.shape[0]
    tiles = rows // QUERY_TILE
    lanes = GROUP * QUERY_TILE
    width = GROUP * HEAD_SIZE
    by_tile = pl.BlockSpec((QUERY_TILE, width), lambda t: (t, 0))
    by_head = pl.BlockSpec((QUERY_TILE, width), lambda t: (t, head))
    return pl.pallas_call(
        without(attend_back_kernel, 7, len(tokens)),
        grid=(tiles,),
        in_specs=[
            pl.BlockSpec(memory_space=pltpu.SMEM),
            by_head,
            by_head,
            by_tile,
            pl.BlockSpec((1, 8, lanes), lambda t: (t, 0, 0)),
            whole((length, LANES)),
            pl.BlockSpec((8, QUERY_TILE), lambda t: (0, t)),
            *unread(tokens),
        ],
        out_specs=[by_tile, whole((length, LANES))],
        out_shape=[
            jax.ShapeDtypeStruct((rows, width), F32),
            jax.ShapeDtypeStruct((length, LANES), BF16),
        ],
        scratch_shapes=[
            pltpu.VMEM((2 * lanes, LANES), BF16),
            pltpu.VMEM((length, LANES), F32),
            pltpu.VMEM((LANES, lanes), F32),
        ],
        compiler_params=params("arbitrary"),
        cost_estimate=lasting(26),
        name="attend_back",
    )(scalars, q, grad, norm, lse, kv, doc_row, *tokens)


def turn_lanes(x, cosine, sine):
    half = HEAD_SIZE // 2
    former = iota(x.shape, 1) % HEAD_SIZE < half
    other = jnp.where(former, -pltpu.roll(x, LANES - half, 1), pltpu.roll(x, half, 1))
    return x * cosine + other * sine


def rope_kernel(q_in_ref, kv_in_ref, cos_ref, sin_ref, q_ref, kv0_ref, kv1_ref):
    cosine, sine = cos_ref[...], sin_ref[...]
    scale = 1.0 / math.sqrt(HEAD_SIZE)
    for i in range(QUERY_HEADS * HEAD_SIZE // LANES):
        turned = turn_lanes(q_in_ref[:, tile(i)], cosine, sine).astype(BF16)
        q_ref[:, tile(i)] = (turned.astype(F32) * scale).astype(BF16)
    keys = turn_lanes(kv_in_ref[:, tile(0)], cosine, sine)
    values = kv_in_ref[:, tile(1)]
    low = iota(keys.shape, 1) < HEAD_SIZE
    kv0_ref[...] = jnp.where(low, keys, half_roll(values)).astype(BF16)
    kv1_ref[...] = jnp.where(low, half_roll(keys), values).astype(BF16)


def rope(q_raw, kv_raw, cosine, sine):
    rows = q_raw.shape[0]
    return pl.pallas_call(
        rope_kernel,
        out_shape=[
            jax.ShapeDtypeStruct((rows, QUERY_HEADS * HEAD_SIZE), BF16),
            jax.ShapeDtypeStruct((rows, LANES), BF16),
            jax.ShapeDtypeStruct((rows, LANES), BF16),
        ],
        compiler_params=pltpu.CompilerParams(vmem_limit_bytes=VMEM_LIMIT),
        cost_estimate=lasting(3),
        name="rope",
    )(q_raw, kv_raw, cosine, sine)


def rope_back_kernel(dq0_ref, dq1_ref, dkv0_ref, dkv1_ref, cos_ref, sin_ref, grad_ref):
    cosine, sine = cos_ref[...], -sin_ref[...]
    for head, dq_ref in enumerate((dq0_ref, dq1_ref)):
        for i in range(2):
            turned = turn_lanes(dq_ref[:, tile(i)], cosine, sine)
            grad_ref[:, tile(2 * head + i)] = turned.astype(BF16)
    first = dkv0_ref[...].astype(F32)
    second = dkv1_ref[...].astype(F32)
    low = iota(first.shape, 1) < HEAD_SIZE
    keys = jnp.where(low, first, half_roll(second))
    values = jnp.where(low, half_roll(first), second)
    grad_ref[:, tile(4)] = turn_lanes(keys, cosine, sine).astype(BF16)
    grad_ref[:, tile(5)] = values.astype(BF16)


def rope_back(dq0, dq1, dkv0, dkv1, cosine, sine):
    rows = dq0.shape[0]
    return pl.pallas_call(
        rope_back_kernel,
        out_shape=jax.ShapeDtypeStruct(
            (rows, QUERY_HEADS * HEAD_SIZE + KEY_VALUE_HEADS * LANES), BF16
        ),
        compiler_params=pltpu.CompilerParams(vmem_limit_bytes=VMEM_LIMIT),
        cost_estimate=lasting(3),
        name="rope_back",
    )(dq0, dq1, dkv0, dkv1, cosine, sine)


DEVICES = ("ctx", "fsdp")


def swap(block, axis, bit):
    count, width = lax.axis_size("ctx"), lax.axis_size("fsdp")
    partner = lambda c, f: (c ^ bit) * width + f if axis == "ctx" else c * width + (f ^ bit)
    route = [(c * width + f, partner(c, f)) for c in range(count) for f in range(width)]
    return lax.ppermute(block, DEVICES, route)


def take_rows(block, index, rows):
    return lax.dynamic_slice_in_dim(block, index * rows, rows, 0)


def after_kernel(*refs):
    pass


def after(block, *others):
    return pl.pallas_call(
        after_kernel,
        in_specs=[pl.BlockSpec(memory_space=pl.ANY)] * (1 + len(others)),
        out_specs=pl.BlockSpec(memory_space=pl.ANY),
        out_shape=jax.ShapeDtypeStruct(block.shape, block.dtype),
        input_output_aliases={0: 0},
        name="after",
    )(block, *others)


def place_kernel(parts, tokens, at_ref, *refs):
    count = 1 + max(part[0] for part in parts)
    outs = 1 + max(part[5] for part in parts)
    pieces, refs = refs[:count], refs[count + tokens :]
    out_refs, held, sems = refs[:outs], refs[outs:-1], refs[-1]
    come, leave = place_copies(parts, at_ref, pieces, out_refs, held, sems)
    for copy in come:
        copy.start()
    for i in range(count):
        come[i].wait()
        for piece, copy in leave:
            if piece == i:
                copy.start()
    for _, copy in leave:
        copy.wait()


def place(pieces, parts, offsets, shapes, tokens=()):
    size = sum(math.prod(piece.shape) for piece in pieces) * 4
    return pl.pallas_call(
        functools.partial(place_kernel, tuple(parts), len(tokens)),
        in_specs=[pl.BlockSpec(memory_space=pltpu.SMEM)]
        + [pl.BlockSpec(memory_space=pl.ANY)] * (len(pieces) + len(tokens)),
        out_specs=[pl.BlockSpec(memory_space=pl.ANY)] * len(shapes),
        out_shape=[jax.ShapeDtypeStruct(shape, BF16) for shape in shapes],
        scratch_shapes=[pltpu.VMEM(piece.shape, BF16) for piece in pieces]
        + [pltpu.SemaphoreType.DMA((len(pieces) + len(parts),))],
        compiler_params=pltpu.CompilerParams(vmem_limit_bytes=VMEM_LIMIT),
        cost_estimate=lasting(1 + size / 3e6),
        name="place",
    )(jnp.stack(offsets).astype(jnp.int32), *pieces, *tokens)


def move(block, axis, bit, start=(), arrive=()):
    sent = after(block, *start) if start else block
    got = swap(sent, axis, bit)
    return sent, after(got, *arrive) if arrive else got


def whole_parts(shard, other, near, columns, arrive=(), extra=0):
    rank, ranks = lax.axis_index("fsdp"), lax.axis_size("fsdp")
    rows = shard.shape[0] - extra
    pieces = [shard, other, near, move(near, "fsdp", 1, (), arrive)[1]]
    parts, offsets, shapes = [], [], {}
    for k in range(4):
        at = 0
        for width, out, shard_rows, first in columns:
            parts.append((k, 0, rows, at, width, out))
            offsets.append((rank ^ k) * shard_rows + first)
            shapes[out] = (ranks * shard_rows, width)
            at += width
        if extra:
            out = 1 + max(column[1] for column in columns)
            parts.append((k, rows, extra, 0, at, out))
            offsets.append((rank ^ k) * extra)
            shapes[out] = (ranks * extra, at)
    return pieces, parts, offsets, [shapes[out] for out in sorted(shapes)]


def product_kernel(blocks, adds, tail, halves, at_ref, *refs):
    left_refs, refs = refs[:blocks], refs[blocks:]
    grad_ref, refs = refs[0], refs[1:]
    add_refs, refs = refs[:adds], refs[adds:]
    tail_ref, refs = (refs[0], refs[1:]) if tail else (None, refs)
    rows = left_refs[0].shape[1]
    turned_ref, total_ref = refs[-2], refs[-1]

    @pl.when(pl.program_id(0) == 0)
    def _():
        for i, left_ref in enumerate(left_refs):
            turned = left_ref[...].astype(F32).T.astype(BF16)
            turned_ref[i * rows : (i + 1) * rows, :] = turned

    total = dot_nn(turned_ref[...], grad_ref[...])
    for add_ref in add_refs:
        total = total + add_ref[...].astype(F32)
    if tail or halves:
        total_ref[...] = total
    if tail:

        @pl.when(pl.program_id(0) == pl.num_programs(0) - 1)
        def _():
            total_ref[:, total_ref.shape[1] - LANES :] += tail_ref[...]

        total = total_ref[...]
    if not halves:
        refs[0][...] = total.astype(BF16)
        return
    kept_ref, sent_ref = refs[0], refs[1]
    half = rows // 2
    side = at_ref[blocks]
    for i in range(blocks):
        to = slice(i * half, (i + 1) * half)
        mine = pl.multiple_of(i * rows + side * half, half)
        theirs = pl.multiple_of(i * rows + (1 - side) * half, half)
        kept_ref[to, :] = total_ref[pl.ds(mine, half), :].astype(BF16)
        sent_ref[to, :] = total_ref[pl.ds(theirs, half), :].astype(BF16)


def product(left, which, grad, adds=(), halves=False, tokens=(), tail=None):
    tokens_count = len(tokens)
    tails = [] if tail is None else [tail]
    depth, width = grad.shape
    rows = left.shape[1] // lax.axis_size("fsdp")
    height = rows * len(which)
    span = max(w for w in range(LANES, min(width, 2049), LANES) if width % w == 0)
    span = span if 5 * span >= 2 * width else width
    rank, side = lax.axis_index("fsdp"), lax.axis_index("ctx") % 2
    at = jnp.stack([rank ^ k for k in which] + [side]).astype(jnp.int32)
    block_of = lambda i: pl.BlockSpec((depth, rows), lambda t, at: (0, at[i]))
    add_of = lambda block: pl.BlockSpec((height, span), lambda t, at: (block, t))
    outs = 2 if halves else 1
    shape = (height // outs, width)
    found = pl.pallas_call(
        without(
            functools.partial(product_kernel, len(which), len(adds), tail is not None, halves),
            2 + len(which) + len(adds) + len(tails),
            tokens_count,
        ),
        grid_spec=pltpu.PrefetchScalarGridSpec(
            num_scalar_prefetch=1,
            grid=(width // span,),
            in_specs=[block_of(i) for i in range(len(which))]
            + [pl.BlockSpec((depth, span), lambda t, at: (0, t))]
            + [add_of(block) for _, block in adds]
            + [whole((height, LANES)) for _ in tails]
            + unread(tokens),
            out_specs=[pl.BlockSpec((height // outs, span), lambda t, at: (0, t))] * outs,
            scratch_shapes=[
                pltpu.VMEM((height, depth), BF16),
                pltpu.VMEM((height, span), F32),
            ],
        ),
        out_shape=[jax.ShapeDtypeStruct(shape, BF16)] * outs,
        compiler_params=params("arbitrary"),
        cost_estimate=lasting(1 + height * width * 3e-6),
        name="product",
    )(at, *([left] * len(which)), grad, *[array for array, _ in adds], *tails, *tokens)
    return found if halves else found[0]


class Reduction:
    def __init__(self, left, grad, more=(None, None, None), tokens=()):
        self.left, self.grad, self.more = left, grad, more
        sent = product(left, (1, 3), grad, (), False, tokens, more[2])
        self.sent, self.got = move(sent, "fsdp", 1)

    def hold(self, *tokens):
        self.got = after(self.got, *tokens)

    def over_x(self, start=(), arrive=(), tokens=()):
        self.near = self.got
        sent = product(
            self.left, (2,), self.grad, [(self.got, 1)], False, tokens, self.more[1]
        )
        self.sent, self.got = move(sent, "fsdp", 2, start, arrive)

    def then_over_y(self, start=(), arrive=(), tokens=()):
        adds = [(self.near, 0), (self.got, 0)]
        self.kept, sent = product(self.left, (0,), self.grad, adds, True, tokens, self.more[0])
        self.sent, self.got = move(sent, "ctx", 1, start, arrive)

    def first_over_y(self, start=(), arrive=(), tokens=()):
        self.kept, sent = product(self.left, (0, 2), self.grad, [(self.got, 0)], True, tokens)
        self.sent, self.got = move(sent, "ctx", 1, start, arrive)

    def then_over_x(self, start=(), arrive=()):
        total = (self.kept.astype(F32) + self.got.astype(F32)).astype(BF16)
        half = total.shape[0] // 2
        self.kept = total[:half]
        self.sent, self.got = move(total[half:], "fsdp", 2, start, arrive)


def ctx_bits():
    bits = [1]
    while 2 * bits[-1] < lax.axis_size("ctx"):
        bits.append(2 * bits[-1])
    return bits


def spread_order():
    apart = jnp.arange(lax.axis_size("ctx"), dtype=jnp.int32) ^ lax.axis_index("ctx")
    where = jnp.zeros_like(apart)
    for k, bit in enumerate(reversed(ctx_bits())):
        where += ((apart // bit) % 2) << k
    return where


class Spread:
    def __init__(self, block):
        self.block, self.bits = block, ctx_bits()

    def step(self, arrive=()):
        _, got = move(self.block, "ctx", self.bits.pop(), (), arrive)
        self.block = jnp.concatenate([self.block, got], axis=0)

    def finish(self, arrive=()):
        while self.bits:
            self.step(arrive)
        return self.block


class BlockSums:
    def __init__(self, blocks):
        self.blocks, self.bits = blocks, ctx_bits()

    def step(self, start=(), arrive=()):
        half = self.blocks.shape[0] // 2
        bit = self.bits.pop(0)
        self.sent, got = move(self.blocks[half:], "ctx", bit, start, arrive)
        self.blocks = (self.blocks[:half].astype(F32) + got.astype(F32)).astype(BF16)

    def finish(self, start=()):
        while self.bits:
            self.step(start)
        return self.blocks


def stretches_of(shapes, rows):
    found, at = [], 0
    for index, (height, width) in enumerate(shapes):
        for first in range(0, height, rows):
            found.append((index, first, at))
            at += width
    return found, at


def fold_kernel(count, side_ref, *refs):
    new_ref, sent_ref = refs[2 * count :]
    half = new_ref.shape[0]
    mine = pl.multiple_of(side_ref[0] * half, half)
    theirs = pl.multiple_of((1 - side_ref[0]) * half, half)
    at = 0
    for i in range(count):
        kept_ref, got_ref = refs[2 * i], refs[2 * i + 1]
        height, width = kept_ref.shape
        for first in range(0, height, 2 * half):
            columns = slice(at, at + width)
            for row, out_ref in ((mine, new_ref), (theirs, sent_ref)):
                rows = pl.ds(first + row, half)
                total = kept_ref[rows, :].astype(F32) + got_ref[rows, :].astype(F32)
                out_ref[:, columns] = total.astype(BF16)
            at += width


def fold_pack(side, pairs):
    arrays = [array for pair in pairs for array in pair]
    rows = min(array.shape[0] for array in arrays)
    _, width = stretches_of([kept.shape for kept, _ in pairs], rows)
    shape = (rows // 2, width)
    return pl.pallas_call(
        functools.partial(fold_kernel, len(pairs)),
        in_specs=[pl.BlockSpec(memory_space=pltpu.SMEM)] + [whole(array.shape) for array in arrays],
        out_specs=[whole(shape)] * 2,
        out_shape=[jax.ShapeDtypeStruct(shape, BF16)] * 2,
        compiler_params=pltpu.CompilerParams(vmem_limit_bytes=VMEM_LIMIT),
        cost_estimate=lasting(2),
        name="fold",
    )(side.reshape(1), *arrays)


def join_kernel(side_ref, own_ref, got_ref, out_ref):
    half = own_ref.shape[0]
    out_ref[pl.ds(pl.multiple_of(side_ref[0] * half, half), half), :] = own_ref[...]
    out_ref[pl.ds(pl.multiple_of((1 - side_ref[0]) * half, half), half), :] = got_ref[...]


def join_pack(side, own, got):
    shape = (2 * own.shape[0], own.shape[1])
    return pl.pallas_call(
        join_kernel,
        in_specs=[pl.BlockSpec(memory_space=pltpu.SMEM)] + [whole(own.shape)] * 2,
        out_specs=whole(shape),
        out_shape=jax.ShapeDtypeStruct(shape, BF16),
        compiler_params=pltpu.CompilerParams(vmem_limit_bytes=VMEM_LIMIT),
        cost_estimate=lasting(2),
        name="join",
    )(side.reshape(1), own, got)


def unpack_kernel(parts, outs, side_ref, own_ref, got_ref, *out_refs):
    rows = own_ref.shape[0]
    for side in range(2):

        @pl.when(side_ref[0] == side)
        def _():
            for array, height, first, at in parts:
                for half, ref in ((side, own_ref), (1 - side, got_ref)):
                    row = half * (height // 2) + first
                    for out_ref, (source, top, end, left, right) in zip(out_refs, outs):
                        if source == array and top <= row < end:
                            to = slice(row - top, row - top + rows)
                            out_ref[to, :] = ref[:, at + left : at + right].astype(F32)


def unpack(side, own, got, shapes, outs):
    found, _ = stretches_of([(height // 2, width) for height, width in shapes], own.shape[0])
    parts = [(index, shapes[index][0], first, at) for index, first, at in found]
    out_shapes = [(end - top, right - left) for _, top, end, left, right in outs]
    return pl.pallas_call(
        functools.partial(unpack_kernel, parts, outs),
        in_specs=[pl.BlockSpec(memory_space=pltpu.SMEM)] + [whole(own.shape)] * 2,
        out_specs=[whole(shape) for shape in out_shapes],
        out_shape=[jax.ShapeDtypeStruct(shape, F32) for shape in out_shapes],
        compiler_params=pltpu.CompilerParams(vmem_limit_bytes=VMEM_LIMIT),
        cost_estimate=lasting(4),
        name="unpack",
    )(side.reshape(1), own, got)


class Pack:
    def __init__(self, pairs):
        self.pairs = pairs
        self.shapes = [(2 * kept.shape[0], kept.shape[1]) for kept, _ in pairs]

    def hold(self, *tokens):
        self.got = after(self.got, *tokens)

    def side(self, bit):
        return (lax.axis_index("ctx") // bit) % 2

    def over_z(self, start=(), arrive=()):
        self.kept, sent = fold_pack(self.side(2), self.pairs)
        self.sent, self.got = move(sent, "ctx", 2, start, arrive)

    def rest(self, start=(), arrive=()):
        self.own = (self.kept.astype(F32) + self.got.astype(F32)).astype(BF16)
        self.kept = None
        for bit in ctx_bits()[2:]:
            self.total()
            self.sent, self.got = move(self.own, "ctx", bit, start, arrive)
            self.kept = self.own

    def total(self):
        if self.kept is not None:
            self.own = (self.kept.astype(F32) + self.got.astype(F32)).astype(BF16)
            self.kept = None

    def back_z(self, start=(), arrive=()):
        self.total()
        self.sent, got = move(self.own, "ctx", 2, start, arrive)
        self.own = join_pack(self.side(2), self.own, got)

    def back_y(self, outs, start=(), arrive=()):
        self.sent, got = move(self.own, "ctx", 1, start, arrive)
        return unpack(self.side(1), self.own, got, self.shapes, outs)


def shift_along(block, axis, distance):
    devices = range(lax.axis_size(axis))
    route = [(i - distance, i) for i in devices if i - distance in devices]
    return lax.ppermute(block, axis, route)


def segment_starts(positions, starts):
    reached = starts[None, :] <= positions[:, None]
    return jnp.max(jnp.where(reached, starts[None, :], -1), axis=1)


class Scan:
    def __init__(self, own, send, upwards):
        self.own, self.send, self.upwards = own, send, upwards
        self.seen = None
        self.bits = ctx_bits()

    def step(self, arrive=()):
        bit = self.bits.pop(0)
        above = (lax.axis_index("ctx") // bit) % 2 == 1
        _, got = move(self.send, "ctx", bit, (), arrive)
        first = above if self.upwards else jnp.logical_not(above)
        self.own, self.send, self.seen = scan_step(
            first, self.own, self.seen, got, not self.bits
        )
        return self.send

    def finish(self, arrive=()):
        while self.bits:
            self.step(arrive)
        return self.seen


def outer_sum(left, right):
    return dot_tn(left, right)


def time_steps(left, right):
    return dot_nt(left, right)


def local(
    tokens,
    cotangent,
    doc_starts,
    gain_mix,
    w_z,
    w_xbc,
    w_dt,
    conv_w,
    conv_b,
    dt_bias,
    a_log,
    skip_factor,
    w_mo,
    w_q,
    key_value_weight,
    w_o,
    gain_ffn,
    w_gate,
    w_up,
    w_down,
):
    xbc_dt = jnp.pad(
        jnp.concatenate([w_xbc, w_dt], axis=1), ((0, 0), (0, LANES - MAMBA_HEADS))
    )
    small = jnp.concatenate(
        [v.reshape(-1) for v in (gain_mix, conv_w, conv_b, dt_bias, a_log, skip_factor, gain_ffn)]
    )
    wide = w_q.shape[1] + key_value_weight.shape[1]
    small_rows = 16
    small = jnp.pad(small, (0, small_rows * wide - small.shape[0])).reshape(small_rows, wide)
    shard_qkv = jnp.concatenate([jnp.concatenate([w_q, key_value_weight], axis=1), small], axis=0)
    near_qkv = swap(shard_qkv, "fsdp", 2)
    near_xbc = swap(xbc_dt, "fsdp", 2)
    side_by_side = lambda w, rows: [w[i : i + rows] for i in range(0, w.shape[0], rows)]
    rows_in = w_z.shape[0]
    shard_omo = jnp.concatenate([w_o, w_mo], axis=0)
    shard_zo = jnp.concatenate([w_z] + side_by_side(shard_omo, rows_in), axis=1)
    shard_ffn = jnp.concatenate([w_gate, w_up] + side_by_side(w_down, rows_in), axis=1)
    shard_zo = after(shard_zo, near_qkv)
    near_zo = swap(shard_zo, "fsdp", 2)
    shard_ffn = after(shard_ffn, near_qkv)
    near_ffn = swap(shard_ffn, "fsdp", 2)
    other_xbc, other_zo, other_ffn = [
        swap(shard, "fsdp", 1) for shard in (xbc_dt, shard_zo, shard_ffn)
    ]
    full_qkv, small_all = place(
        *whole_parts(
            shard_qkv,
            swap(shard_qkv, "fsdp", 1),
            near_qkv,
            [(shard_qkv.shape[1], 0, rows_in, 0)],
            (),
            small_rows,
        )
    )
    model = w_down.shape[1]

    def stretches(out, shard_rows):
        return [(model, out, shard_rows, first) for first in range(0, shard_rows, rows_in)]

    ranks = lax.axis_size("fsdp")
    small_all = small_all.reshape(ranks, -1).astype(F32)
    at = [0]

    def unpack(rows, width):
        part = small_all[:, at[0] : at[0] + rows * width].reshape(-1, rows, width)
        at[0] += rows * width
        return part.transpose(1, 0, 2).reshape(rows, -1)

    full_gain_mix = unpack(1, gain_mix.shape[0])[0]
    full_conv_w = unpack(CONV, conv_b.shape[0])
    full_conv_b = unpack(1, conv_b.shape[0])[0]
    full_dt_bias = unpack(1, dt_bias.shape[0])[0]
    full_a_log = unpack(1, dt_bias.shape[0])[0]
    full_skip = unpack(1, dt_bias.shape[0])[0]
    full_gain_ffn = unpack(1, gain_ffn.shape[0])[0]
    o_rows = w_o.shape[0]
    wide_in = xbc_dt.shape[1]
    ctx_rank = lax.axis_index("ctx")
    inputs = tokens[0].astype(F32)
    rows = inputs.shape[0]
    starts = doc_starts[0]
    base = ctx_rank * rows
    positions = base + jnp.arange(rows, dtype=jnp.int32)
    doc = segment_starts(positions, starts)
    doc_col = jnp.pad(doc, (0, 8))[:, None]
    doc_row = jnp.broadcast_to(doc[None, :], (8, rows))
    scalars = jnp.concatenate([doc[CHUNK - 1 :: CHUNK], base[None]])
    attn_scalars = jnp.concatenate(
        [doc[::QUERY_TILE], doc[QUERY_TILE - 1 :: QUERY_TILE], base[None], spread_order()]
    )
    half = HEAD_SIZE // 2
    freqs = ROPE_BASE ** (
        -2.0 * (jnp.arange(LANES, dtype=jnp.int32) % half).astype(F32) / HEAD_SIZE
    )
    angles = positions.astype(F32)[:, None] * freqs[None, :]
    cosine, sine = jnp.cos(angles), jnp.sin(angles)
    conv_pack = jnp.pad(
        jnp.concatenate([full_conv_w, full_conv_b[None]], axis=0), ((0, 3), (0, 0))
    )
    pad_heads = lambda v: jnp.pad(v, (0, LANES - MAMBA_HEADS))[None]
    head_pack = jnp.concatenate(
        [pad_heads(full_dt_bias), pad_heads(-jnp.exp(full_a_log)), jnp.zeros((6, LANES), F32)], axis=0
    )
    skip_wide = jnp.repeat(full_skip, MAMBA_HEAD_SIZE)[None]

    scale_one = lax.rsqrt(jnp.mean(inputs * inputs, axis=-1, keepdims=True) + EPSILON)
    normed = (inputs * scale_one * full_gain_mix[None, :]).astype(BF16)
    q_width = QUERY_HEADS * HEAD_SIZE
    qkv_raw = dot_nn(normed, full_qkv)
    query, kv_first, kv_second = rope(
        qkv_raw[:, :q_width], qkv_raw[:, q_width:], cosine, sine
    )
    spreads = [Spread(kv) for kv in (kv_first, kv_second)]
    full_xbc = place(
        *whole_parts(
            xbc_dt,
            other_xbc,
            after(near_xbc, query),
            [(xbc_dt.shape[1], 0, rows_in, 0)],
        ),
        [other_zo, other_ffn],
    )[0]
    for spread_kv in spreads:
        spread_kv.step()
        spread_kv.block = after(spread_kv.block, full_xbc)
        spread_kv.step()
    mixed_in = dot_nn(normed, full_xbc[:, :CHANNELS]).astype(BF16)
    dt_raw = dot_nn(normed, full_xbc[:, CHANNELS:])
    edge = shift_along(mixed_in[rows - 8 :], "ctx", 1).astype(F32)
    y_local, state_local, message, own_state, decay, c_mat = mamba_forward(
        scalars,
        edge,
        mixed_in,
        dt_raw,
        doc_col[:rows],
        conv_pack,
        head_pack,
        skip_wide,
        [spreads[0].block],
    )
    kv_all = [spreads[0].finish([message])]
    scan = Scan(own_state, message, True)
    first_send = scan.step([kv_all[0]])
    tokens = [first_send]
    attended = [attend(attn_scalars, query, kv_all[0], doc_row, 0, tokens)]
    first_done = attended[0][0]
    kv_all.append(spreads[1].finish([first_done]))
    carried = whole_parts(
        shard_zo,
        other_zo,
        after(near_zo, first_send),
        [(w_z.shape[1], 0, rows_in, 0)] + stretches(1, shard_omo.shape[0]),
    )
    tokens = [scan.step([first_done]), first_done]
    *second, full_z, full_omo = attend(
        attn_scalars, query, kv_all[1], doc_row, 1, tokens, carried
    )
    attended.append(second)
    second_done = attended[1][0]
    gate_z = dot_nn(normed, full_z)
    state_in = scan.finish([second_done])
    y_total, both, state_true = mamba_correct(
        y_local, state_local, c_mat, decay, state_in, gate_z, attended[0][0], attended[1][0]
    )
    full_gate_up, full_down = place(
        *whole_parts(
            shard_ffn,
            other_ffn,
            after(near_ffn, y_total),
            [(2 * w_gate.shape[1], 0, rows_in, 0)] + stretches(1, w_down.shape[0]),
        )
    )
    hidden = inputs + dot_nn(both, full_omo)
    gain_two = full_gain_ffn
    scale_two = lax.rsqrt(jnp.mean(hidden * hidden, axis=-1, keepdims=True) + EPSILON)
    normed_ffn = (hidden * scale_two * gain_two[None, :]).astype(BF16)
    gate_up = dot_nn(normed_ffn, full_gate_up)
    ff = gate_up.shape[1] // 2
    gate, upper = gate_up[:, :ff], gate_up[:, ff:]
    sig_gate = jax.nn.sigmoid(gate)
    silu_gate = gate * sig_gate
    activ = (silu_gate * upper).astype(BF16)
    result = hidden + dot_nn(activ, full_down)

    grad_out = cotangent[0]
    down = Reduction(activ, grad_out)
    grad_act = time_steps(grad_out, full_down)
    grad_gate = (grad_act * upper * sig_gate * (1.0 + gate * (1.0 - sig_gate))).astype(BF16)
    grad_up = (grad_act * silu_gate).astype(BF16)
    grad_gate_up = jnp.concatenate([grad_gate, grad_up], axis=1)
    gate_up_sum = Reduction(normed_ffn, grad_gate_up)
    grad_n2 = time_steps(grad_gate_up, full_gate_up)
    scaled_two = grad_n2 * gain_two[None, :]
    grad_hidden = (
        grad_out.astype(F32)
        + scale_two * scaled_two
        - hidden * scale_two**3 * jnp.mean(scaled_two * hidden, axis=-1, keepdims=True)
    )
    gate_up_sum.over_x()
    down.first_over_y(tokens=[gate_up_sum.sent])
    grad_hid_b = after(grad_hidden.astype(BF16), gate_up_sum.sent, down.sent)
    both_grad = time_steps(grad_hid_b, full_omo).astype(BF16)
    grad_y, grad_z, own_grad, grad_message, grad_attn = mamba_gate_back(
        both_grad, gate_z, y_total, c_mat, decay, own_state
    )
    omo = Reduction(both, grad_hid_b)
    z_sum = Reduction(normed, grad_z)
    scan = Scan(own_grad, grad_message, False)
    backs = []

    def back(j, tokens):
        backs.append(
            attend_back(
                attn_scalars,
                query,
                grad_attn,
                attended[j][1],
                attended[j][2],
                kv_all[j],
                doc_row,
                j,
                tokens,
            )
        )

    down.hold(grad_attn)
    down.then_over_x()
    backs = []

    def back(j, tokens):
        backs.append(
            attend_back(
                attn_scalars,
                query,
                grad_attn,
                attended[j][1],
                attended[j][2],
                kv_all[j],
                doc_row,
                j,
                tokens,
            )
        )

    scan.step()
    gate_up_sum.hold(scan.send)
    gate_up_sum.then_over_y()
    omo.first_over_y(tokens=[gate_up_sum.sent])
    z_sum.over_x()
    scan.step([gate_up_sum.sent])
    gate_up_sum.hold(scan.send)
    down.hold(scan.send)
    ffn = Pack([(gate_up_sum.kept, gate_up_sum.got), (down.kept, down.got)])
    ffn.over_z()
    back(0, [scan.send, ffn.sent, omo.sent, z_sum.sent])
    first_done = backs[0][0]
    for part in (ffn, omo, z_sum):
        part.hold(first_done)
    state_grad = scan.finish([first_done])
    ffn.rest()
    omo.then_over_x()
    z_sum.then_over_y()
    first_kv = BlockSums(backs[0][1])
    first_kv.sent = first_kv.blocks[first_kv.blocks.shape[0] // 2 :]
    grad_xbc, tail, edge_grad, grad_conv, grad_heads = mamba_back(
        scalars,
        edge,
        mixed_in,
        dt_raw,
        doc_col,
        doc_row,
        conv_pack,
        head_pack,
        skip_wide,
        grad_y,
        y_total,
        state_true,
        state_grad,
        [ffn.sent, z_sum.sent, omo.sent, first_kv.sent, first_done],
    )
    third_done = grad_heads
    for part in (ffn, omo, z_sum):
        part.hold(third_done)
    first_kv.step((), [third_done])
    mixer = Pack([(z_sum.kept, z_sum.got), (omo.kept, omo.got)])
    mixer.over_z()
    behind = shift_along(edge_grad, "ctx", -1)
    grad_xbc = lax.dynamic_update_slice(grad_xbc, (tail + behind).astype(BF16), (rows - 8, 0))
    fsdp_rank = lax.axis_index("fsdp")
    conv_width, heads_width = conv_b.shape[0], dt_bias.shape[0]
    small_width = -(-(conv_width * (CONV + 1) + heads_width * 3) // rows_in)
    small_at = CHANNELS + MAMBA_HEADS
    blocks = [
        g.reshape(g.shape[0], ranks, -1).transpose(1, 0, 2).reshape(ranks, -1)
        for g in (grad_conv[: CONV + 1], grad_heads[:3, :MAMBA_HEADS])
    ]
    small_grad = jnp.concatenate(blocks, axis=1)
    small_count = small_grad.shape[1]
    small_grad = jnp.pad(small_grad, ((0, 0), (0, small_width * rows_in - small_count)))
    small_grad = jnp.pad(
        small_grad.reshape(ranks, rows_in, small_width),
        ((0, 0), (0, 0), (MAMBA_HEADS, LANES - MAMBA_HEADS - small_width)),
    )
    block_of = lambda k: lax.dynamic_index_in_dim(small_grad, fsdp_rank ^ k, 0, False)
    more = [block_of(0), block_of(2), jnp.concatenate([block_of(1), block_of(3)], axis=0)]
    ffn.total()
    xbc_sum = Reduction(
        normed, grad_xbc, more, [ffn.own, z_sum.got, omo.got, first_kv.blocks]
    )
    xbc_sum.over_x()
    ffn.back_z((), [xbc_sum.sent])
    back(1, [xbc_sum.sent, mixer.sent, ffn.own, first_kv.blocks, third_done])
    second_done = backs[1][0]
    xbc_sum.hold(second_done)
    mixer.hold(second_done)
    first_kv.step((), [second_done])
    second_kv = BlockSums(backs[1][1])
    second_kv.step()
    kv_left = second_kv.sent
    y_in = [second_kv.blocks]
    xbc_sum.then_over_y()
    y_left = [xbc_sum.sent]
    xbc = Pack([(xbc_sum.kept, after(xbc_sum.got, *y_in))])
    second_kv.step(y_left)
    z_in = [second_kv.blocks]
    first_kv.step((), y_in)
    grad_kv0, grad_kv1 = first_kv.finish(), second_kv.finish()
    grad_qkv = rope_back(backs[0][0], backs[1][0], grad_kv0, grad_kv1, cosine, sine)
    qkv_sum = Reduction(normed, grad_qkv)
    core_left = [qkv_sum.sent]
    mixer.rest((), core_left)
    qkv_sum.over_x()
    x_left = [qkv_sum.sent]
    xbc.pairs = [(xbc_sum.kept, after(xbc_sum.got, *x_left))]
    xbc.over_z()
    ff = w_gate.shape[1]
    grad_w_gate, grad_w_up, grad_w_down = ffn.back_y(
        [
            (0, 0, rows_in, 0, ff),
            (0, 0, rows_in, ff, 2 * ff),
            (1, 0, w_down.shape[0], 0, model),
        ],
        [kv_left],
        x_left,
    )
    qkv_sum.then_over_y()
    y_left = [qkv_sum.sent]
    xbc.rest((), y_left)
    mixer.back_z((), y_left)
    qkv = Pack([(qkv_sum.kept, after(qkv_sum.got, mixer.own))])
    qkv.over_z()
    z_left = [qkv.sent]
    xbc.back_z((), z_left)
    omo_rows = shard_omo.shape[0]
    mixer_outs = [
        (0, 0, rows_in, 0, w_z.shape[1]),
        (1, 0, o_rows, 0, model),
        (1, o_rows, omo_rows, 0, model),
    ]
    qkv.rest()
    qkv.back_z()
    join_left = [qkv.own]
    last_left = [qkv.sent]
    grad_w_z, grad_w_o, grad_w_mo = mixer.back_y(mixer_outs, (), last_left)
    grad_w_q, grad_w_kv = qkv.back_y(
        [(0, 0, rows_in, 0, q_width), (0, 0, rows_in, q_width, qkv_raw.shape[1])],
        [grad_w_z],
    )
    grad_w_xbc, grad_w_dt = xbc.back_y(
        [(0, 0, rows_in, 0, CHANNELS), (0, 0, rows_in, CHANNELS, wide_in)], (), [qkv.sent]
    )
    small_own = grad_w_dt[:, small_at - CHANNELS : small_at - CHANNELS + small_width].reshape(-1)[:small_count]
    conv_own = small_own[: conv_width * (CONV + 1)].reshape(CONV + 1, conv_width)
    heads_own = small_own[conv_width * (CONV + 1) :].reshape(3, heads_width)
    grad_n1 = (
        time_steps(after(grad_z, *y_in), full_z)
        + time_steps(after(grad_xbc, *y_left), full_xbc)
        + time_steps(after(grad_qkv, *z_left), full_qkv)
    )
    scaled_one = grad_n1 * full_gain_mix[None, :]
    grad_tokens = (
        grad_hidden
        + scale_one * scaled_one
        - inputs * scale_one**3 * jnp.mean(scaled_one * inputs, axis=-1, keepdims=True)
    )
    row_sums = lambda grad, weight: jnp.sum(grad * weight.astype(F32), axis=1)
    grad_gain_ffn = (
        row_sums(grad_w_gate, w_gate) + row_sums(grad_w_up, w_up)
    ) / gain_ffn.astype(F32)
    grad_gain_mix = (
        row_sums(grad_w_z, w_z)
        + row_sums(grad_w_xbc, w_xbc)
        + row_sums(grad_w_dt[:, :MAMBA_HEADS], w_dt)
        + row_sums(grad_w_q, w_q)
        + row_sums(grad_w_kv, key_value_weight)
    ) / gain_mix.astype(F32)
    totals = (
        grad_gain_mix,
        grad_w_z,
        grad_w_xbc,
        grad_w_dt[:, :MAMBA_HEADS],
        conv_own[:CONV],
        conv_own[CONV],
        heads_own[0],
        heads_own[1],
        heads_own[2],
        grad_w_mo,
        grad_w_q,
        grad_w_kv,
        grad_w_o,
        grad_gain_ffn,
        grad_w_gate,
        grad_w_up,
        grad_w_down,
    )
    return (result.astype(BF16)[None], grad_tokens[None]) + totals


def solution(mesh):
    in_specs = (
        P("fsdp", "ctx", None),
        P("fsdp", "ctx", None),
        P("fsdp", None),
        P("fsdp"),
        P("fsdp", None),
        P("fsdp", None),
        P("fsdp", None),
        P(None, "fsdp"),
        P("fsdp"),
        P("fsdp"),
        P("fsdp"),
        P("fsdp"),
        P("fsdp", None),
        P("fsdp", None),
        P("fsdp", None),
        P("fsdp", None),
        P("fsdp"),
        P("fsdp", None),
        P("fsdp", None),
        P("fsdp", None),
    )
    out_specs = (
        P("fsdp", "ctx", None),
        P("fsdp", "ctx", None),
        P("fsdp"),
        P("fsdp", None),
        P("fsdp", None),
        P("fsdp", None),
        P(None, "fsdp"),
        P("fsdp"),
        P("fsdp"),
        P("fsdp"),
        P("fsdp"),
        P("fsdp", None),
        P("fsdp", None),
        P("fsdp", None),
        P("fsdp", None),
        P("fsdp"),
        P("fsdp", None),
        P("fsdp", None),
        P("fsdp", None),
    )
    return jax.shard_map(local, mesh=mesh, in_specs=in_specs, out_specs=out_specs, check_vma=False)
```

```python
import functools
import math

import jax
import jax.numpy as jnp
from jax import lax
from jax.experimental import pallas as pl
from jax.experimental.pallas import tpu as pltpu
from jax.sharding import PartitionSpec as P

MAMBA_HEADS = 24
MAMBA_HEAD_SIZE = 64
STATE_SIZE = 128
CONV = 4
QUERY_HEADS = 8
KEY_VALUE_HEADS = 2
HEAD_SIZE = 64
MAMBA_INNER = MAMBA_HEADS * MAMBA_HEAD_SIZE
CHANNELS = MAMBA_INNER + 2 * STATE_SIZE
LANES = 128
PAIRS = MAMBA_INNER // LANES
CHUNK = 128
KEY_BLOCK = 512
QUERY_TILE = 256
GROUP = QUERY_HEADS // KEY_VALUE_HEADS
MESSAGE_ROWS = STATE_SIZE + 16
VMEM_LIMIT = 56 * 1024 * 1024

EPSILON = 1e-06
ROPE_BASE = 10000.0
MASK_FILLER = -1e30
HIGHEST = lax.Precision.HIGHEST
F32 = jnp.float32
BF16 = jnp.bfloat16


def dot_nn(a, b, precision=None):
    return lax.dot_general(
        a, b, (((1,), (0,)), ((), ())), precision=precision, preferred_element_type=F32
    )


def dot_nt(a, b):
    return lax.dot_general(a, b, (((1,), (1,)), ((), ())), preferred_element_type=F32)


def dot_tn(a, b):
    return lax.dot_general(a, b, (((0,), (0,)), ((), ())), preferred_element_type=F32)


def iota(shape, dim):
    return lax.broadcasted_iota(jnp.int32, shape, dim)


def params(*semantics):
    return pltpu.CompilerParams(dimension_semantics=semantics, vmem_limit_bytes=VMEM_LIMIT)


def lasting(microseconds):
    return pl.CostEstimate(flops=int(microseconds * 1.15e9), bytes_accessed=0, transcendentals=0)


def without(kernel, at, count):
    def body(*refs):
        kernel(*refs[:at], *refs[at + count :])

    return body


def unread(arrays):
    return [pl.BlockSpec(memory_space=pl.ANY)] * len(arrays)


def whole(shape):
    return pl.BlockSpec(shape, lambda *_: (0,) * len(shape))


def low_half(rows):
    return iota((rows, LANES), 1) < MAMBA_HEAD_SIZE


def spread(values, pair, low):
    a = values[:, 2 * pair : 2 * pair + 1]
    b = values[:, 2 * pair + 1 : 2 * pair + 2]
    return jnp.where(low, a, b)


def tile(i):
    return slice(i * LANES, (i + 1) * LANES)


def split_pair(x, low):
    zero = jnp.zeros_like(x)
    return jnp.concatenate([jnp.where(low, x, zero), jnp.where(low, zero, x)], axis=0)


def fill_padded(xs_ref, edge_ref, mixed_ref):
    xs_ref[0:8, :] = edge_ref[...]
    xs_ref[8:, :] = mixed_ref[...].astype(F32)


def lag_masks(positions, doc):
    return [None] + [(positions - lag >= doc).astype(F32) for lag in range(1, CONV)]


def conv_tile(xs_ref, start, i, cw_ref, masks):
    window = xs_ref[pl.ds(start, CHUNK + 8), tile(i)]
    summed = cw_ref[4:5, tile(i)] + cw_ref[3:4, tile(i)] * window[8 : 8 + CHUNK]
    for lag in range(1, CONV):
        shifted = window[8 - lag : 8 - lag + CHUNK]
        summed = summed + cw_ref[3 - lag : 4 - lag, tile(i)] * (shifted * masks[lag])
    return summed


def softplus(v):
    return jnp.maximum(v, 0.0) + jnp.log1p(jnp.exp(-jnp.abs(v)))


def decay_sums(dt_ref, hp_ref):
    raw = dt_ref[...] + hp_ref[0:1, :]
    step = softplus(raw)
    log_decay = step * hp_ref[1:2, :]
    order = iota((CHUNK, CHUNK), 0) >= iota((CHUNK, CHUNK), 1)
    cumul = dot_nn(order.astype(F32), log_decay, HIGHEST)
    return raw, step, log_decay, cumul


def mamba_forward_kernel(
    sc_ref,
    edge_ref,
    mixed_ref,
    dt_ref,
    doc_ref,
    cw_ref,
    hp_ref,
    skip_ref,
    y_ref,
    sin_ref,
    msg_ref,
    own_ref,
    dec_ref,
    c_ref,
    xs_ref,
    xa_ref,
    state_ref,
    carry_ref,
):
    c = pl.program_id(0)
    count = pl.num_programs(0)

    @pl.when(c == 0)
    def _():
        fill_padded(xs_ref, edge_ref, mixed_ref)
        state_ref[...] = jnp.zeros_like(state_ref)
        carry_ref[...] = jnp.zeros_like(carry_ref)

    base = sc_ref[count]
    start = pl.multiple_of(c * CHUNK, CHUNK)
    first = base + start
    end_doc = sc_ref[c]
    doc = doc_ref[...]
    positions = first + iota((CHUNK, 1), 0)
    masks = lag_masks(positions, doc)
    for i in range(CHANNELS // LANES):
        summed = conv_tile(xs_ref, start, i, cw_ref, masks)
        xa_ref[:, tile(i)] = summed * jax.nn.sigmoid(summed)
    _, step, log_decay, cumul = decay_sums(dt_ref, hp_ref)
    cumul_t = cumul.T
    b_mat = xa_ref[:, tile(PAIRS)]
    c_mat = xa_ref[:, tile(PAIRS + 1)].astype(BF16)
    c_ref[...] = c_mat
    couple = dot_nt(c_mat, b_mat.astype(BF16))
    b_turned = b_mat.T.astype(BF16)
    col = first + iota((CHUNK, CHUNK), 1)
    row = first + iota((CHUNK, CHUNK), 0)
    couple = jnp.where((col <= row) & (col >= doc), couple, 0.0)
    carried = (doc < first).astype(F32)
    into = jnp.exp(cumul) * carried
    last = cumul[CHUNK - 1 : CHUNK, :]
    ending = jnp.exp(last - cumul) * (positions >= end_doc).astype(F32)
    keep = jnp.exp(last) * (end_doc < first).astype(F32)
    dec_ref[...] = jnp.where(doc < base, jnp.exp(cumul + carry_ref[0:1, :]), 0.0)
    low = low_half(CHUNK)
    low_row = low_half(1)
    for j in range(PAIRS):
        x = xa_ref[:, tile(j)]
        weighted = x * spread(step, j, low)
        mixing = []
        for h in (2 * j, 2 * j + 1):
            gap = jnp.minimum(cumul[:, h : h + 1] - cumul_t[h : h + 1, :], 0.0)
            mixing.append((couple * jnp.exp(gap)).astype(BF16))
        y = dot_nn(jnp.concatenate(mixing, axis=1), split_pair(weighted.astype(BF16), low))
        state = state_ref[:, tile(j)]
        sin_ref[0, :, tile(j)] = state.astype(BF16)
        y = y + dot_nn(c_mat, state.astype(BF16)) * spread(into, j, low)
        y_ref[:, tile(j)] = y + skip_ref[0:1, tile(j)] * x
        fresh = dot_nn(b_turned, (weighted * spread(ending, j, low)).astype(BF16))
        state_ref[:, tile(j)] = fresh + state * spread(keep, j, low_row)
    carry_ref[...] = carry_ref[...] + last

    @pl.when(c == count - 1)
    def _():
        msg_ref[0:STATE_SIZE, :] = state_ref[...].astype(BF16)
        own_ref[0:STATE_SIZE, :] = state_ref[...]
        through = jnp.exp(carry_ref[...]) * (end_doc < base).astype(F32)
        low8 = low_half(8)
        for j in range(PAIRS):
            wide = spread(through, j, low8)
            wide = jnp.concatenate([wide, wide], axis=0)
            msg_ref[STATE_SIZE:, tile(j)] = wide.astype(BF16)
            own_ref[STATE_SIZE:, tile(j)] = wide


def mamba_forward(
    scalars, edge, mixed, dt_raw, doc, conv_pack, head_pack, skip_wide, tokens=()
):
    rows = mixed.shape[0]
    count = rows // CHUNK
    by_chunk = lambda width: pl.BlockSpec((CHUNK, width), lambda c: (c, 0))
    return pl.pallas_call(
        without(mamba_forward_kernel, 8, len(tokens)),
        grid=(count,),
        in_specs=[
            pl.BlockSpec(memory_space=pltpu.SMEM),
            whole((8, CHANNELS)),
            whole((rows, CHANNELS)),
            by_chunk(LANES),
            by_chunk(1),
            whole((8, CHANNELS)),
            whole((8, LANES)),
            whole((1, MAMBA_INNER)),
            *unread(tokens),
        ],
        out_specs=[
            by_chunk(MAMBA_INNER),
            pl.BlockSpec((1, STATE_SIZE, MAMBA_INNER), lambda c: (c, 0, 0)),
            whole((MESSAGE_ROWS, MAMBA_INNER)),
            whole((MESSAGE_ROWS, MAMBA_INNER)),
            by_chunk(LANES),
            by_chunk(LANES),
        ],
        out_shape=[
            jax.ShapeDtypeStruct((rows, MAMBA_INNER), F32),
            jax.ShapeDtypeStruct((count, STATE_SIZE, MAMBA_INNER), BF16),
            jax.ShapeDtypeStruct((MESSAGE_ROWS, MAMBA_INNER), BF16),
            jax.ShapeDtypeStruct((MESSAGE_ROWS, MAMBA_INNER), F32),
            jax.ShapeDtypeStruct((rows, LANES), F32),
            jax.ShapeDtypeStruct((rows, LANES), BF16),
        ],
        scratch_shapes=[
            pltpu.VMEM((rows + 8, CHANNELS), F32),
            pltpu.VMEM((CHUNK, CHANNELS), F32),
            pltpu.VMEM((STATE_SIZE, MAMBA_INNER), F32),
            pltpu.VMEM((8, LANES), F32),
        ],
        compiler_params=params("arbitrary"),
        cost_estimate=lasting(13),
        name="mamba_forward",
    )(scalars, edge, mixed, dt_raw, doc, conv_pack, head_pack, skip_wide, *tokens)


QUARTERS = 4
BLOCK_TILES = 1 + PAIRS // QUARTERS


def attn_tile(i):
    return tile(i * BLOCK_TILES)


def gated_tile(j):
    per = PAIRS // QUARTERS
    return tile(j // per * BLOCK_TILES + 1 + j % per)


def mamba_correct_kernel(
    y_ref, sin_ref, c_ref, dec_ref, state_ref, z_ref, vec0_ref, vec1_ref, total_ref, both_ref, true_ref, edge_ref
):
    c = pl.program_id(0)

    @pl.when(c == 0)
    def _():
        edge_ref[...] = jnp.ones_like(edge_ref)

    low = low_half(CHUNK)
    low_row = low_half(1)
    decay = dec_ref[...]
    before = edge_ref[0:1, :]
    c_mat = c_ref[...]
    for j in range(PAIRS):
        state = state_ref[:, tile(j)]
        y = y_ref[:, tile(j)] + dot_nn(c_mat, state.astype(BF16)) * spread(decay, j, low)
        total_ref[:, tile(j)] = y
        z = z_ref[:, tile(j)].astype(F32)
        both_ref[:, gated_tile(j)] = (y * (z * jax.nn.sigmoid(z))).astype(BF16)
        true_ref[0, :, tile(j)] = (
            sin_ref[0, :, tile(j)].astype(F32) + state * spread(before, j, low_row)
        ).astype(BF16)
    for i, vec_ref in enumerate((vec0_ref, vec0_ref, vec1_ref, vec1_ref)):
        both_ref[:, attn_tile(i)] = vec_ref[:, tile(i % 2)]
    edge_ref[0:1, :] = decay[CHUNK - 1 : CHUNK, :]


def mamba_correct(y, sin, c_mat, decay, state_in, gate_z, vec0, vec1):
    rows = y.shape[0]
    count = rows // CHUNK
    by_chunk = lambda width: pl.BlockSpec((CHUNK, width), lambda c: (c, 0))
    states = pl.BlockSpec((1, STATE_SIZE, MAMBA_INNER), lambda c: (c, 0, 0))
    return pl.pallas_call(
        mamba_correct_kernel,
        grid=(count,),
        in_specs=[
            by_chunk(MAMBA_INNER),
            states,
            by_chunk(LANES),
            by_chunk(LANES),
            whole((STATE_SIZE, MAMBA_INNER)),
            by_chunk(MAMBA_INNER),
            by_chunk(2 * LANES),
            by_chunk(2 * LANES),
        ],
        out_specs=[by_chunk(MAMBA_INNER), by_chunk(QUARTERS * BLOCK_TILES * LANES), states],
        out_shape=[
            jax.ShapeDtypeStruct((rows, MAMBA_INNER), F32),
            jax.ShapeDtypeStruct((rows, QUARTERS * BLOCK_TILES * LANES), BF16),
            jax.ShapeDtypeStruct((count, STATE_SIZE, MAMBA_INNER), BF16),
        ],
        scratch_shapes=[pltpu.VMEM((8, LANES), F32)],
        compiler_params=params("arbitrary"),
        cost_estimate=lasting(8.5),
        name="mamba_correct",
    )(y, sin, c_mat, decay, state_in, gate_z, vec0, vec1)


def mamba_gate_back_kernel(
    both_ref, z_ref, y_ref, c_ref, dec_ref, own_ref, dy_ref, gz_ref, gsi_ref, gsb_ref, gvec_ref, acc_ref
):
    c = pl.program_id(0)

    @pl.when(c == 0)
    def _():
        acc_ref[...] = jnp.zeros_like(acc_ref)

    low = low_half(CHUNK)
    decay = dec_ref[...]
    c_turned = c_ref[...].astype(F32).T.astype(BF16)
    for j in range(PAIRS):
        z = z_ref[:, tile(j)].astype(F32)
        sig = jax.nn.sigmoid(z)
        silu = z * sig
        grad = both_ref[:, gated_tile(j)].astype(F32)
        gz_ref[:, tile(j)] = (grad * y_ref[:, tile(j)] * (sig + silu * (1.0 - sig))).astype(BF16)
        dy = (grad * silu).astype(BF16)
        dy_ref[:, tile(j)] = dy
        scaled = (dy.astype(F32) * spread(decay, j, low)).astype(BF16)
        acc_ref[:, tile(j)] += dot_nn(c_turned, scaled)
    for i in range(QUARTERS):
        gvec_ref[:, tile(i)] = both_ref[:, attn_tile(i)]

    @pl.when(c == pl.num_programs(0) - 1)
    def _():
        gsi_ref[0:STATE_SIZE, :] = acc_ref[...]
        gsb_ref[0:STATE_SIZE, :] = acc_ref[...].astype(BF16)
        gsi_ref[STATE_SIZE:, :] = own_ref[...]
        gsb_ref[STATE_SIZE:, :] = own_ref[...].astype(BF16)


def mamba_gate_back(both_grad, gate_z, total, c_mat, decay, own, tokens=()):
    rows = total.shape[0]
    by_chunk = lambda width: pl.BlockSpec((CHUNK, width), lambda c: (c, 0))
    return pl.pallas_call(
        without(mamba_gate_back_kernel, 6, len(tokens)),
        grid=(rows // CHUNK,),
        in_specs=[
            by_chunk(QUARTERS * BLOCK_TILES * LANES),
            by_chunk(MAMBA_INNER),
            by_chunk(MAMBA_INNER),
            by_chunk(LANES),
            by_chunk(LANES),
            pl.BlockSpec((16, MAMBA_INNER), lambda c: (STATE_SIZE // 16, 0)),
            *unread(tokens),
        ],
        out_specs=[
            by_chunk(MAMBA_INNER),
            by_chunk(MAMBA_INNER),
            whole((MESSAGE_ROWS, MAMBA_INNER)),
            whole((MESSAGE_ROWS, MAMBA_INNER)),
            by_chunk(QUARTERS * LANES),
        ],
        out_shape=[
            jax.ShapeDtypeStruct((rows, MAMBA_INNER), BF16),
            jax.ShapeDtypeStruct((rows, MAMBA_INNER), BF16),
            jax.ShapeDtypeStruct((MESSAGE_ROWS, MAMBA_INNER), F32),
            jax.ShapeDtypeStruct((MESSAGE_ROWS, MAMBA_INNER), BF16),
            jax.ShapeDtypeStruct((rows, QUARTERS * LANES), BF16),
        ],
        scratch_shapes=[pltpu.VMEM((STATE_SIZE, MAMBA_INNER), F32)],
        compiler_params=params("arbitrary"),
        cost_estimate=lasting(7.5),
        name="mamba_gate_back",
    )(both_grad, gate_z, total, c_mat, decay, own, *tokens)


def picks(pair):
    channel = iota((LANES, LANES), 0)
    head = iota((LANES, LANES), 1)
    return (head == 2 * pair + channel // MAMBA_HEAD_SIZE).astype(BF16)


def head_sums(product, select):
    high = product.astype(BF16)
    rest = (product - high.astype(F32)).astype(BF16)
    return dot_nn(high, select) + dot_nn(rest, select)


def mamba_back_kernel(
    sc_ref,
    edge_ref,
    mixed_ref,
    dt_ref,
    doc_ref,
    doc_row_ref,
    cw_ref,
    hp_ref,
    skip_ref,
    dy_ref,
    y_ref,
    sin_ref,
    ds_end_ref,
    gmix_ref,
    tail_ref,
    edge_grad_ref,
    gconv_ref,
    ghead_ref,
    xs_ref,
    xa_ref,
    slope_ref,
    grad_ref,
    ds_ref,
    rows_ref,
):
    step_at = pl.program_id(0)
    count = pl.num_programs(0)
    c = count - 1 - step_at
    rows = count * CHUNK

    @pl.when(step_at == 0)
    def _():
        fill_padded(xs_ref, edge_ref, mixed_ref)
        ds_ref[...] = ds_end_ref[...]
        grad_ref[pl.ds(rows, 8), :] = jnp.zeros((8, CHANNELS), F32)
        gconv_ref[...] = jnp.zeros_like(gconv_ref)
        ghead_ref[...] = jnp.zeros_like(ghead_ref)
        rows_ref[...] = jnp.zeros_like(rows_ref)

    base = sc_ref[count]
    start = pl.multiple_of(c * CHUNK, CHUNK)
    first = base + start
    end_doc = sc_ref[c]
    doc_window = doc_ref[pl.ds(start, CHUNK + 8), :]
    doc = doc_window[0:CHUNK]
    positions_window = first + iota((CHUNK + 8, 1), 0)
    positions = positions_window[0:CHUNK]
    masks_window = lag_masks(positions_window, doc_window)
    masks = [None] + [m[0:CHUNK] for m in masks_window[1:]]
    for i in range(CHANNELS // LANES):
        summed = conv_tile(xs_ref, start, i, cw_ref, masks)
        sig = jax.nn.sigmoid(summed)
        act = summed * sig
        xa_ref[:, tile(i)] = act
        slope_ref[:, tile(i)] = sig + act * (1.0 - sig)
    raw, step, log_decay, cumul = decay_sums(dt_ref, hp_ref)
    cumul_t = cumul.T
    b_mat = xa_ref[:, tile(PAIRS)].astype(BF16)
    c_f32 = xa_ref[:, tile(PAIRS + 1)]
    c_mat = c_f32.astype(BF16)
    c_turned = c_f32.T.astype(BF16)
    key = first + iota((CHUNK, CHUNK), 0)
    query = first + iota((CHUNK, CHUNK), 1)
    visible = (key <= query) & (key >= doc_row_ref[0:1, :])
    couple = jnp.where(visible, dot_nt(b_mat, c_mat), 0.0)
    carried = (doc < first).astype(F32)
    into = jnp.exp(cumul) * carried
    last = cumul[CHUNK - 1 : CHUNK, :]
    ending = jnp.exp(last - cumul) * (positions >= end_doc).astype(F32)
    keep = jnp.exp(last) * (end_doc < first).astype(F32)
    low = low_half(CHUNK)
    low_row = low_half(1)
    grad_couple = jnp.zeros((CHUNK, CHUNK), F32)
    grad_b = jnp.zeros((CHUNK, STATE_SIZE), F32)
    grad_c = jnp.zeros((CHUNK, STATE_SIZE), F32)
    grad_cumul = jnp.zeros((CHUNK, LANES), F32)
    grad_step = jnp.zeros((CHUNK, LANES), F32)
    end_sums = jnp.zeros((8, LANES), F32)
    for j in range(PAIRS):
        select = picks(j)
        x = xa_ref[:, tile(j)]
        step_wide = spread(step, j, low)
        weighted = x * step_wide
        weighted_b = weighted.astype(BF16)
        dy = dy_ref[:, tile(j)]
        dy_f32 = dy.astype(F32)
        grad_mixing = dot_nt(split_pair(weighted_b, low), dy)
        mixing = []
        for side, h in enumerate((2 * j, 2 * j + 1)):
            gap = jnp.minimum(cumul_t[h : h + 1, :] - cumul[:, h : h + 1], 0.0)
            fade = jnp.exp(gap)
            mixing.append((couple * fade).astype(BF16))
            grad_couple += grad_mixing[side * CHUNK : (side + 1) * CHUNK] * fade
        grad_weighted = dot_nn(jnp.concatenate(mixing, axis=1), split_pair(dy, low))
        ending_wide = spread(ending, j, low)
        grad_state = ds_ref[:, tile(j)]
        grad_state_b = grad_state.astype(BF16)
        state = sin_ref[0, :, tile(j)]
        through_state = ending_wide * dot_nn(b_mat, grad_state_b)
        grad_weighted = grad_weighted + through_state
        dy_into = (dy_f32 * spread(into, j, low)).astype(BF16)
        grad_c += dot_nt(dy_into, state)
        grad_b += dot_nt((weighted * ending_wide).astype(BF16), grad_state_b)
        keep_wide = spread(keep, j, low_row)
        weighted_f32 = weighted_b.astype(F32)
        to_end = jnp.sum(weighted_f32 * through_state, axis=0, keepdims=True) + keep_wide * jnp.sum(
            grad_state * state.astype(F32), axis=0, keepdims=True
        )
        ds_ref[:, tile(j)] = keep_wide * grad_state + dot_nn(c_turned, dy_into)
        skip = skip_ref[0:1, tile(j)]
        grad_x = step_wide * grad_weighted + skip * dy_f32
        grad_ref[pl.ds(start, CHUNK), tile(j)] = grad_x * slope_ref[:, tile(j)]
        rows_ref[0:1, tile(j)] += jnp.sum(dy_f32 * x, axis=0, keepdims=True)
        in_out = dy_f32 * (y_ref[:, tile(j)] - skip * x) - weighted_f32 * grad_weighted
        grad_cumul += head_sums(in_out, select)
        grad_step += head_sums(grad_weighted * x, select)
        end_sums += head_sums(jnp.broadcast_to(to_end, (8, LANES)), select)
    grad_couple = jnp.where(visible, grad_couple, 0.0).astype(BF16)
    grad_b += dot_nn(grad_couple, c_mat)
    grad_c += dot_tn(grad_couple, b_mat)
    grad_ref[pl.ds(start, CHUNK), tile(PAIRS)] = grad_b * slope_ref[:, tile(PAIRS)]
    grad_ref[pl.ds(start, CHUNK), tile(PAIRS + 1)] = grad_c * slope_ref[:, tile(PAIRS + 1)]
    later = (iota((CHUNK, CHUNK), 0) <= iota((CHUNK, CHUNK), 1)).astype(F32)
    grad_log = dot_nn(later, grad_cumul, HIGHEST) + end_sums[0:1, :]
    grad_raw = (grad_step + grad_log * hp_ref[1:2, :]) * jax.nn.sigmoid(raw)
    gmix_ref[:, tile(CHANNELS // LANES)] = grad_raw.astype(BF16)
    ghead_ref[0:1, :] += jnp.sum(grad_raw, axis=0, keepdims=True)
    ghead_ref[1:2, :] += jnp.sum(grad_log * log_decay, axis=0, keepdims=True)
    for i in range(CHANNELS // LANES):
        window = grad_ref[pl.ds(start, CHUNK + 8), tile(i)]
        own = window[0:CHUNK]
        padded = xs_ref[pl.ds(start, CHUNK + 8), tile(i)]
        total = cw_ref[3:4, tile(i)] * own
        gconv_ref[4:5, tile(i)] += jnp.sum(own, axis=0, keepdims=True)
        gconv_ref[3:4, tile(i)] += jnp.sum(own * padded[8 : 8 + CHUNK], axis=0, keepdims=True)
        for lag in range(1, CONV):
            masked = window * masks_window[lag]
            total = total + cw_ref[3 - lag : 4 - lag, tile(i)] * masked[lag : lag + CHUNK]
            gconv_ref[3 - lag : 4 - lag, tile(i)] += jnp.sum(
                masked[0:CHUNK] * padded[8 - lag : 8 - lag + CHUNK], axis=0, keepdims=True
            )
        gmix_ref[:, tile(i)] = total.astype(BF16)

        @pl.when(step_at == 0)
        def _():
            tail_ref[:, tile(i)] = total[CHUNK - 8 :]

        @pl.when(step_at == count - 1)
        def _():
            ahead = jnp.zeros((8, LANES), F32)
            for lag in range(1, CONV):
                head = jnp.concatenate(
                    [jnp.zeros((8, LANES), F32), window[0:8] * masks_window[lag][0:8]], axis=0
                )
                ahead = ahead + cw_ref[3 - lag : 4 - lag, tile(i)] * head[lag : lag + 8]
            edge_grad_ref[:, tile(i)] = ahead

    @pl.when(step_at == count - 1)
    def _():
        total = jnp.zeros((8, LANES), F32)
        for j in range(PAIRS):
            total += head_sums(rows_ref[:, tile(j)], picks(j))
        ghead_ref[2:3, :] = total[0:1, :]


def mamba_back(
    scalars,
    edge,
    mixed,
    dt_raw,
    doc,
    doc_row,
    conv_pack,
    head_pack,
    skip_wide,
    dy,
    y,
    sin,
    ds_end,
    tokens=(),
):
    rows = mixed.shape[0]
    count = rows // CHUNK
    by_chunk = lambda width: pl.BlockSpec((CHUNK, width), lambda i: (count - 1 - i, 0))
    return pl.pallas_call(
        without(mamba_back_kernel, 13, len(tokens)),
        grid=(count,),
        in_specs=[
            pl.BlockSpec(memory_space=pltpu.SMEM),
            whole((8, CHANNELS)),
            whole((rows, CHANNELS)),
            by_chunk(LANES),
            whole((rows + 8, 1)),
            pl.BlockSpec((8, CHUNK), lambda i: (0, count - 1 - i)),
            whole((8, CHANNELS)),
            whole((8, LANES)),
            whole((1, MAMBA_INNER)),
            by_chunk(MAMBA_INNER),
            by_chunk(MAMBA_INNER),
            pl.BlockSpec((1, STATE_SIZE, MAMBA_INNER), lambda i: (count - 1 - i, 0, 0)),
            whole((STATE_SIZE, MAMBA_INNER)),
            *unread(tokens),
        ],
        out_specs=[
            by_chunk(CHANNELS + LANES),
            whole((8, CHANNELS)),
            whole((8, CHANNELS)),
            whole((8, CHANNELS)),
            whole((8, LANES)),
        ],
        out_shape=[
            jax.ShapeDtypeStruct((rows, CHANNELS + LANES), BF16),
            jax.ShapeDtypeStruct((8, CHANNELS), F32),
            jax.ShapeDtypeStruct((8, CHANNELS), F32),
            jax.ShapeDtypeStruct((8, CHANNELS), F32),
            jax.ShapeDtypeStruct((8, LANES), F32),
        ],
        scratch_shapes=[
            pltpu.VMEM((rows + 8, CHANNELS), F32),
            pltpu.VMEM((CHUNK, CHANNELS), F32),
            pltpu.VMEM((CHUNK, CHANNELS), F32),
            pltpu.VMEM((rows + 8, CHANNELS), F32),
            pltpu.VMEM((STATE_SIZE, MAMBA_INNER), F32),
            pltpu.VMEM((8, MAMBA_INNER), F32),
        ],
        compiler_params=params("arbitrary"),
        cost_estimate=lasting(25),
        name="mamba_back",
    )(
        scalars,
        edge,
        mixed,
        dt_raw,
        doc,
        doc_row,
        conv_pack,
        head_pack,
        skip_wide,
        dy,
        y,
        sin,
        ds_end,
        *tokens,
    )


def scan_step_kernel(begins, ends, flag_ref, *refs):
    total_ref, refs = refs[0], refs[1:]
    seen_ref, refs = (None, refs) if begins else (refs[0], refs[1:])
    got_ref, out_ref = refs[0], refs[-1]
    first = flag_ref[0] == 1
    rows = slice(0, STATE_SIZE)
    rest = slice(STATE_SIZE, MESSAGE_ROWS)
    one = STATE_SIZE
    for j in range(PAIRS):
        got = got_ref[:, tile(j)].astype(F32)
        if begins:
            out_ref[rows, tile(j)] = jnp.where(first, got[rows], 0.0)
            out_ref[rest, tile(j)] = jnp.where(first, got[rest], 1.0)
        else:
            seen = seen_ref[:, tile(j)]
            passed = seen[rows] + seen[one : one + 1] * got[rows]
            out_ref[rows, tile(j)] = jnp.where(first, passed, seen[rows])
            out_ref[rest, tile(j)] = jnp.where(first, seen[rest] * got[rest], seen[rest])
        if not ends:
            new_ref, send_ref = refs[1:3]
            total = total_ref[:, tile(j)]
            mine, theirs = total[one : one + 1], got[one : one + 1]
            state = jnp.where(first, mine * got[rows] + total[rows], theirs * total[rows] + got[rows])
            new_ref[rows, tile(j)] = state
            send_ref[rows, tile(j)] = state.astype(BF16)
            factor = total[rest] * got[rest]
            new_ref[rest, tile(j)] = factor
            send_ref[rest, tile(j)] = factor.astype(BF16)


def scan_step(first, total, seen, got, ends):
    shape = (MESSAGE_ROWS, MAMBA_INNER)
    ins = [total, got] if seen is None else [total, seen, got]
    outs = [F32] if ends else [F32, BF16, F32]
    specs = [whole(shape)] * len(ins)
    if ends:
        specs[0] = pl.BlockSpec(memory_space=pl.ANY)
    found = pl.pallas_call(
        functools.partial(scan_step_kernel, seen is None, ends),
        in_specs=[pl.BlockSpec(memory_space=pltpu.SMEM)] + specs,
        out_specs=[whole(shape)] * len(outs),
        out_shape=[jax.ShapeDtypeStruct(shape, kind) for kind in outs],
        compiler_params=pltpu.CompilerParams(vmem_limit_bytes=VMEM_LIMIT),
        cost_estimate=lasting(2.5),
        name="scan_step",
    )(first.astype(jnp.int32).reshape(1), *ins)
    return (None, None, found[0]) if ends else found


def half_roll(x):
    return pltpu.roll(x, HEAD_SIZE, 1)


def stack_low(block, rows):
    low = low_half(rows)
    parts = []
    for a in range(2):
        pair = block[:, tile(a)]
        parts.append(jnp.where(low, pair, 0.0))
        parts.append(jnp.where(low, half_roll(pair), 0.0))
    return parts


def stack_high(block, rows):
    low = low_half(rows)
    parts = []
    for a in range(2):
        pair = block[:, tile(a)]
        parts.append(jnp.where(low, 0.0, half_roll(pair)))
        parts.append(jnp.where(low, 0.0, pair))
    return parts


def tile_bounds(sc_ref, at, tiles):
    first_doc = sc_ref[at]
    last_doc = sc_ref[tiles + at]
    start = sc_ref[2 * tiles] + at * QUERY_TILE
    block_lo = first_doc // KEY_BLOCK
    block_hi = (start + QUERY_TILE - 1) // KEY_BLOCK + 1
    return start, last_doc, block_lo, block_hi


def visible_mask(block, start, doc_row):
    lanes = GROUP * QUERY_TILE
    key = block * KEY_BLOCK + iota((KEY_BLOCK, lanes), 0)
    query = start + iota((1, lanes), 1) % QUERY_TILE
    return (key <= query) & (key >= doc_row)


def attend_kernel(
    sc_ref, q_ref, kv_ref, doc_ref, vec_ref, norm_ref, lse_ref, qz_ref, max_ref, acc_ref
):
    at = pl.program_id(0)
    tiles = pl.num_programs(0)
    start, last_doc, block_lo, block_hi = tile_bounds(sc_ref, at, tiles)
    for g, part in enumerate(stack_low(q_ref[...].astype(F32), QUERY_TILE)):
        qz_ref[g * QUERY_TILE : (g + 1) * QUERY_TILE, :] = part.astype(BF16)
    max_ref[...] = jnp.full_like(max_ref, MASK_FILLER)
    acc_ref[...] = jnp.zeros_like(acc_ref)
    doc_row = jnp.concatenate([doc_ref[0:1, :]] * GROUP, axis=1)

    def visit(block, masked):
        at_rows = sc_ref[2 * tiles + 1 + block] * KEY_BLOCK
        kv = kv_ref[pl.ds(pl.multiple_of(at_rows, KEY_BLOCK), KEY_BLOCK), :]
        values = jnp.where(low_half(KEY_BLOCK), jnp.ones_like(kv), kv)
        scores = dot_nt(kv, qz_ref[...])
        if masked:
            scores = jnp.where(visible_mask(block, start, doc_row), scores, MASK_FILLER)
        before = max_ref[0:1, :]
        top = jnp.maximum(before, jnp.max(scores, axis=0, keepdims=True))
        prob = jnp.exp(scores - top)
        fade = jnp.exp(before - top)
        max_ref[0:1, :] = top
        acc_ref[...] = acc_ref[...] * fade + dot_tn(values, prob.astype(BF16))

    def one(block, carry):
        full = (block * KEY_BLOCK + KEY_BLOCK - 1 <= start) & (block * KEY_BLOCK >= last_doc)

        @pl.when(full)
        def _():
            visit(block, False)

        @pl.when(jnp.logical_not(full))
        def _():
            visit(block, True)

        return carry

    lax.fori_loop(block_lo, block_hi, one, 0)
    total = acc_ref[0:1, :]
    lse_ref[0] = jnp.broadcast_to(max_ref[0:1, :] + jnp.log(total), lse_ref.shape[1:])
    scaled = acc_ref[...] / total
    low = low_half(QUERY_TILE)
    for a in range(2):
        even = half_roll(scaled[:, (2 * a) * QUERY_TILE : (2 * a + 1) * QUERY_TILE].T)
        odd = scaled[:, (2 * a + 1) * QUERY_TILE : (2 * a + 2) * QUERY_TILE].T
        both = jnp.where(low, even, odd)
        norm_ref[:, tile(a)] = both
        vec_ref[:, tile(a)] = both.astype(BF16)


def carrying(kernel, ins, outs, parts, pieces):
    def body(*refs):
        own_ins, refs = refs[:ins], refs[ins:]
        at_ref, piece_refs, refs = refs[0], refs[1 : 1 + pieces], refs[1 + pieces :]
        own_outs, refs = refs[:outs], refs[outs:]
        places = 1 + max(part[5] for part in parts)
        place_refs, refs = refs[:places], refs[places:]
        own_scratch, held, sems = refs[: -pieces - 1], refs[-pieces - 1 : -1], refs[-1]
        step, last = pl.program_id(0), pl.num_programs(0) - 1
        come, leave = place_copies(parts, at_ref, piece_refs, place_refs, held, sems)

        @pl.when(step == 0)
        def _():
            for copy in come:
                copy.start()

        kernel(*own_ins, *own_outs, *own_scratch)

        @pl.when(step == 0)
        def _():
            for copy in come:
                copy.wait()
            for _, copy in leave:
                copy.start()

        @pl.when(step == last)
        def _():
            for _, copy in leave:
                copy.wait()

    return body


def place_copies(parts, at_ref, pieces, out_refs, held, sems):
    come = [
        pltpu.make_async_copy(piece, here, sems.at[i])
        for i, (piece, here) in enumerate(zip(pieces, held))
    ]
    leave = []
    for k, (piece, row, rows, col, cols, out) in enumerate(parts):
        here = held[piece].at[pl.ds(row, rows), pl.ds(col, cols)]
        to = out_refs[out].at[pl.ds(pl.multiple_of(at_ref[k], 16), rows), :]
        leave.append((piece, pltpu.make_async_copy(here, to, sems.at[len(pieces) + k])))
    return come, leave


def attend(scalars, q, kv, doc_row, head, tokens=(), carried=None):
    rows = q.shape[0]
    length = kv.shape[0]
    tiles = rows // QUERY_TILE
    lanes = GROUP * QUERY_TILE
    width = GROUP * HEAD_SIZE
    by_tile = pl.BlockSpec((QUERY_TILE, width), lambda t: (t, 0))
    kernel = attend_kernel
    more_in, more_out, more_shape, more_scratch, more = [], [], [], [], []
    if carried:
        pieces, parts, offsets, shapes = carried
        kernel = carrying(kernel, 4, 3, parts, len(pieces))
        more_in = [pl.BlockSpec(memory_space=pltpu.SMEM)] + unread(pieces)
        more_out = unread(shapes)
        more_shape = [jax.ShapeDtypeStruct(shape, BF16) for shape in shapes]
        more_scratch = [pltpu.VMEM(piece.shape, BF16) for piece in pieces]
        more_scratch.append(pltpu.SemaphoreType.DMA((len(pieces) + len(parts),)))
        more = [jnp.stack(offsets).astype(jnp.int32), *pieces]
    return pl.pallas_call(
        without(kernel, 4 + len(more_in), len(tokens)),
        grid=(tiles,),
        in_specs=[
            pl.BlockSpec(memory_space=pltpu.SMEM),
            pl.BlockSpec((QUERY_TILE, width), lambda t: (t, head)),
            whole((length, LANES)),
            pl.BlockSpec((8, QUERY_TILE), lambda t: (0, t)),
            *more_in,
            *unread(tokens),
        ],
        out_specs=[by_tile, by_tile, pl.BlockSpec((1, 8, lanes), lambda t: (t, 0, 0)), *more_out],
        out_shape=[
            jax.ShapeDtypeStruct((rows, width), BF16),
            jax.ShapeDtypeStruct((rows, width), F32),
            jax.ShapeDtypeStruct((tiles, 8, lanes), F32),
            *more_shape,
        ],
        scratch_shapes=[
            pltpu.VMEM((lanes, LANES), BF16),
            pltpu.VMEM((8, lanes), F32),
            pltpu.VMEM((LANES, lanes), F32),
            *more_scratch,
        ],
        compiler_params=params("arbitrary"),
        cost_estimate=lasting(18),
        name="attend",
    )(scalars, q, kv, doc_row, *more, *tokens)


def attend_back_kernel(
    sc_ref, q_ref, do_ref, norm_ref, lse_ref, kv_ref, doc_ref, dq_ref, dkv_ref, qd_ref, dkv_acc, dq_acc
):
    at = pl.program_id(0)
    tiles = pl.num_programs(0)
    lanes = GROUP * QUERY_TILE
    start, last_doc, block_lo, block_hi = tile_bounds(sc_ref, at, tiles)

    @pl.when(at == 0)
    def _():
        dkv_acc[...] = jnp.zeros_like(dkv_acc)

    grad = do_ref[...].astype(F32)
    for g, part in enumerate(stack_low(q_ref[...].astype(F32), QUERY_TILE)):
        qd_ref[g * QUERY_TILE : (g + 1) * QUERY_TILE, :] = part.astype(BF16)
    for g, part in enumerate(stack_high(grad, QUERY_TILE)):
        qd_ref[lanes + g * QUERY_TILE : lanes + (g + 1) * QUERY_TILE, :] = part.astype(BF16)
    deltas = []
    for a in range(2):
        turned = (grad[:, tile(a)] * norm_ref[:, tile(a)]).T
        deltas.append(jnp.sum(turned[0:HEAD_SIZE], axis=0, keepdims=True))
        deltas.append(jnp.sum(turned[HEAD_SIZE:], axis=0, keepdims=True))
    delta = jnp.concatenate(deltas, axis=1)
    lse = lse_ref[0, 0:1, :]
    dq_acc[...] = jnp.zeros_like(dq_acc)
    doc_row = jnp.concatenate([doc_ref[0:1, :]] * GROUP, axis=1)

    def visit(block, masked):
        first_row = sc_ref[2 * tiles + 1 + block] * KEY_BLOCK
        at_rows = pl.ds(pl.multiple_of(first_row, KEY_BLOCK), KEY_BLOCK)
        kv = kv_ref[at_rows, :]
        scores = dot_nt(kv, qd_ref[0:lanes, :])
        prob = jnp.exp(scores - lse)
        if masked:
            prob = jnp.where(visible_mask(block, start, doc_row), prob, 0.0)
        grad_prob = dot_nt(kv, qd_ref[lanes:, :])
        grad_scores = (prob * (grad_prob - delta)).astype(BF16)
        dkv_acc[at_rows, :] += dot_nn(grad_scores, qd_ref[0:lanes, :]) + dot_nn(
            prob.astype(BF16), qd_ref[lanes:, :]
        )
        dq_acc[...] += dot_tn(kv, grad_scores)

    def one(block, carry):
        full = (block * KEY_BLOCK + KEY_BLOCK - 1 <= start) & (block * KEY_BLOCK >= last_doc)

        @pl.when(full)
        def _():
            visit(block, False)

        @pl.when(jnp.logical_not(full))
        def _():
            visit(block, True)

        return carry

    lax.fori_loop(block_lo, block_hi, one, 0)
    low = low_half(QUERY_TILE)
    scale = 1.0 / math.sqrt(HEAD_SIZE)
    for a in range(2):
        even = dq_acc[:, (2 * a) * QUERY_TILE : (2 * a + 1) * QUERY_TILE].T
        odd = half_roll(dq_acc[:, (2 * a + 1) * QUERY_TILE : (2 * a + 2) * QUERY_TILE].T)
        dq_ref[:, tile(a)] = jnp.where(low, even, odd) * scale

    @pl.when(at == tiles - 1)
    def _():
        dkv_ref[...] = dkv_acc[...].astype(BF16)


def attend_back(scalars, q, grad, norm, lse, kv, doc_row, head, tokens=()):
    rows = q.shape[0]
    length = kv.shape[0]
    tiles = rows // QUERY_TILE
    lanes = GROUP * QUERY_TILE
    width = GROUP * HEAD_SIZE
    by_tile = pl.BlockSpec((QUERY_TILE, width), lambda t: (t, 0))
    by_head = pl.BlockSpec((QUERY_TILE, width), lambda t: (t, head))
    return pl.pallas_call(
        without(attend_back_kernel, 7, len(tokens)),
        grid=(tiles,),
        in_specs=[
            pl.BlockSpec(memory_space=pltpu.SMEM),
            by_head,
            by_head,
            by_tile,
            pl.BlockSpec((1, 8, lanes), lambda t: (t, 0, 0)),
            whole((length, LANES)),
            pl.BlockSpec((8, QUERY_TILE), lambda t: (0, t)),
            *unread(tokens),
        ],
        out_specs=[by_tile, whole((length, LANES))],
        out_shape=[
            jax.ShapeDtypeStruct((rows, width), F32),
            jax.ShapeDtypeStruct((length, LANES), BF16),
        ],
        scratch_shapes=[
            pltpu.VMEM((2 * lanes, LANES), BF16),
            pltpu.VMEM((length, LANES), F32),
            pltpu.VMEM((LANES, lanes), F32),
        ],
        compiler_params=params("arbitrary"),
        cost_estimate=lasting(26),
        name="attend_back",
    )(scalars, q, grad, norm, lse, kv, doc_row, *tokens)


def turn_lanes(x, cosine, sine):
    half = HEAD_SIZE // 2
    former = iota(x.shape, 1) % HEAD_SIZE < half
    other = jnp.where(former, -pltpu.roll(x, LANES - half, 1), pltpu.roll(x, half, 1))
    return x * cosine + other * sine


def rope_kernel(q_in_ref, kv_in_ref, cos_ref, sin_ref, q_ref, kv0_ref, kv1_ref):
    cosine, sine = cos_ref[...], sin_ref[...]
    scale = 1.0 / math.sqrt(HEAD_SIZE)
    for i in range(QUERY_HEADS * HEAD_SIZE // LANES):
        turned = turn_lanes(q_in_ref[:, tile(i)], cosine, sine).astype(BF16)
        q_ref[:, tile(i)] = (turned.astype(F32) * scale).astype(BF16)
    keys = turn_lanes(kv_in_ref[:, tile(0)], cosine, sine)
    values = kv_in_ref[:, tile(1)]
    low = iota(keys.shape, 1) < HEAD_SIZE
    kv0_ref[...] = jnp.where(low, keys, half_roll(values)).astype(BF16)
    kv1_ref[...] = jnp.where(low, half_roll(keys), values).astype(BF16)


def rope(q_raw, kv_raw, cosine, sine):
    rows = q_raw.shape[0]
    return pl.pallas_call(
        rope_kernel,
        out_shape=[
            jax.ShapeDtypeStruct((rows, QUERY_HEADS * HEAD_SIZE), BF16),
            jax.ShapeDtypeStruct((rows, LANES), BF16),
            jax.ShapeDtypeStruct((rows, LANES), BF16),
        ],
        compiler_params=pltpu.CompilerParams(vmem_limit_bytes=VMEM_LIMIT),
        cost_estimate=lasting(3),
        name="rope",
    )(q_raw, kv_raw, cosine, sine)


def rope_back_kernel(dq0_ref, dq1_ref, dkv0_ref, dkv1_ref, cos_ref, sin_ref, grad_ref):
    cosine, sine = cos_ref[...], -sin_ref[...]
    for head, dq_ref in enumerate((dq0_ref, dq1_ref)):
        for i in range(2):
            turned = turn_lanes(dq_ref[:, tile(i)], cosine, sine)
            grad_ref[:, tile(2 * head + i)] = turned.astype(BF16)
    first = dkv0_ref[...].astype(F32)
    second = dkv1_ref[...].astype(F32)
    low = iota(first.shape, 1) < HEAD_SIZE
    keys = jnp.where(low, first, half_roll(second))
    values = jnp.where(low, half_roll(first), second)
    grad_ref[:, tile(4)] = turn_lanes(keys, cosine, sine).astype(BF16)
    grad_ref[:, tile(5)] = values.astype(BF16)


def rope_back(dq0, dq1, dkv0, dkv1, cosine, sine):
    rows = dq0.shape[0]
    return pl.pallas_call(
        rope_back_kernel,
        out_shape=jax.ShapeDtypeStruct(
            (rows, QUERY_HEADS * HEAD_SIZE + KEY_VALUE_HEADS * LANES), BF16
        ),
        compiler_params=pltpu.CompilerParams(vmem_limit_bytes=VMEM_LIMIT),
        cost_estimate=lasting(3),
        name="rope_back",
    )(dq0, dq1, dkv0, dkv1, cosine, sine)


DEVICES = ("ctx", "fsdp")


def swap(block, axis, bit):
    count, width = lax.axis_size("ctx"), lax.axis_size("fsdp")
    partner = lambda c, f: (c ^ bit) * width + f if axis == "ctx" else c * width + (f ^ bit)
    route = [(c * width + f, partner(c, f)) for c in range(count) for f in range(width)]
    return lax.ppermute(block, DEVICES, route)


def take_rows(block, index, rows):
    return lax.dynamic_slice_in_dim(block, index * rows, rows, 0)


def after_kernel(*refs):
    pass


def after(block, *others):
    return pl.pallas_call(
        after_kernel,
        in_specs=[pl.BlockSpec(memory_space=pl.ANY)] * (1 + len(others)),
        out_specs=pl.BlockSpec(memory_space=pl.ANY),
        out_shape=jax.ShapeDtypeStruct(block.shape, block.dtype),
        input_output_aliases={0: 0},
        name="after",
    )(block, *others)


def place_kernel(parts, tokens, at_ref, *refs):
    count = 1 + max(part[0] for part in parts)
    outs = 1 + max(part[5] for part in parts)
    pieces, refs = refs[:count], refs[count + tokens :]
    out_refs, held, sems = refs[:outs], refs[outs:-1], refs[-1]
    come, leave = place_copies(parts, at_ref, pieces, out_refs, held, sems)
    for copy in come:
        copy.start()
    for i in range(count):
        come[i].wait()
        for piece, copy in leave:
            if piece == i:
                copy.start()
    for _, copy in leave:
        copy.wait()


def place(pieces, parts, offsets, shapes, tokens=()):
    size = sum(math.prod(piece.shape) for piece in pieces) * 4
    return pl.pallas_call(
        functools.partial(place_kernel, tuple(parts), len(tokens)),
        in_specs=[pl.BlockSpec(memory_space=pltpu.SMEM)]
        + [pl.BlockSpec(memory_space=pl.ANY)] * (len(pieces) + len(tokens)),
        out_specs=[pl.BlockSpec(memory_space=pl.ANY)] * len(shapes),
        out_shape=[jax.ShapeDtypeStruct(shape, BF16) for shape in shapes],
        scratch_shapes=[pltpu.VMEM(piece.shape, BF16) for piece in pieces]
        + [pltpu.SemaphoreType.DMA((len(pieces) + len(parts),))],
        compiler_params=pltpu.CompilerParams(vmem_limit_bytes=VMEM_LIMIT),
        cost_estimate=lasting(1 + size / 3e6),
        name="place",
    )(jnp.stack(offsets).astype(jnp.int32), *pieces, *tokens)


def move(block, axis, bit, start=(), arrive=()):
    sent = after(block, *start) if start else block
    got = swap(sent, axis, bit)
    return sent, after(got, *arrive) if arrive else got


def whole_parts(shard, other, near, columns, arrive=(), extra=0):
    rank, ranks = lax.axis_index("fsdp"), lax.axis_size("fsdp")
    rows = shard.shape[0] - extra
    pieces = [shard, other, near, move(near, "fsdp", 1, (), arrive)[1]]
    parts, offsets, shapes = [], [], {}
    for k in range(4):
        at = 0
        for width, out, shard_rows, first in columns:
            parts.append((k, 0, rows, at, width, out))
            offsets.append((rank ^ k) * shard_rows + first)
            shapes[out] = (ranks * shard_rows, width)
            at += width
        if extra:
            out = 1 + max(column[1] for column in columns)
            parts.append((k, rows, extra, 0, at, out))
            offsets.append((rank ^ k) * extra)
            shapes[out] = (ranks * extra, at)
    return pieces, parts, offsets, [shapes[out] for out in sorted(shapes)]


def product_kernel(blocks, adds, tail, halves, at_ref, *refs):
    left_refs, refs = refs[:blocks], refs[blocks:]
    grad_ref, refs = refs[0], refs[1:]
    add_refs, refs = refs[:adds], refs[adds:]
    tail_ref, refs = (refs[0], refs[1:]) if tail else (None, refs)
    rows = left_refs[0].shape[1]
    turned_ref, total_ref = refs[-2], refs[-1]

    @pl.when(pl.program_id(0) == 0)
    def _():
        for i, left_ref in enumerate(left_refs):
            turned = left_ref[...].astype(F32).T.astype(BF16)
            turned_ref[i * rows : (i + 1) * rows, :] = turned

    total = dot_nn(turned_ref[...], grad_ref[...])
    for add_ref in add_refs:
        total = total + add_ref[...].astype(F32)
    if tail or halves:
        total_ref[...] = total
    if tail:

        @pl.when(pl.program_id(0) == pl.num_programs(0) - 1)
        def _():
            total_ref[:, total_ref.shape[1] - LANES :] += tail_ref[...]

        total = total_ref[...]
    if not halves:
        refs[0][...] = total.astype(BF16)
        return
    kept_ref, sent_ref = refs[0], refs[1]
    half = rows // 2
    side = at_ref[blocks]
    for i in range(blocks):
        to = slice(i * half, (i + 1) * half)
        mine = pl.multiple_of(i * rows + side * half, half)
        theirs = pl.multiple_of(i * rows + (1 - side) * half, half)
        kept_ref[to, :] = total_ref[pl.ds(mine, half), :].astype(BF16)
        sent_ref[to, :] = total_ref[pl.ds(theirs, half), :].astype(BF16)


def product(left, which, grad, adds=(), halves=False, tokens=(), tail=None):
    tokens_count = len(tokens)
    tails = [] if tail is None else [tail]
    depth, width = grad.shape
    rows = left.shape[1] // lax.axis_size("fsdp")
    height = rows * len(which)
    span = max(w for w in range(LANES, min(width, 2049), LANES) if width % w == 0)
    span = span if 5 * span >= 2 * width else width
    rank, side = lax.axis_index("fsdp"), lax.axis_index("ctx") % 2
    at = jnp.stack([rank ^ k for k in which] + [side]).astype(jnp.int32)
    block_of = lambda i: pl.BlockSpec((depth, rows), lambda t, at: (0, at[i]))
    add_of = lambda block: pl.BlockSpec((height, span), lambda t, at: (block, t))
    outs = 2 if halves else 1
    shape = (height // outs, width)
    found = pl.pallas_call(
        without(
            functools.partial(product_kernel, len(which), len(adds), tail is not None, halves),
            2 + len(which) + len(adds) + len(tails),
            tokens_count,
        ),
        grid_spec=pltpu.PrefetchScalarGridSpec(
            num_scalar_prefetch=1,
            grid=(width // span,),
            in_specs=[block_of(i) for i in range(len(which))]
            + [pl.BlockSpec((depth, span), lambda t, at: (0, t))]
            + [add_of(block) for _, block in adds]
            + [whole((height, LANES)) for _ in tails]
            + unread(tokens),
            out_specs=[pl.BlockSpec((height // outs, span), lambda t, at: (0, t))] * outs,
            scratch_shapes=[
                pltpu.VMEM((height, depth), BF16),
                pltpu.VMEM((height, span), F32),
            ],
        ),
        out_shape=[jax.ShapeDtypeStruct(shape, BF16)] * outs,
        compiler_params=params("arbitrary"),
        cost_estimate=lasting(1 + height * width * 3e-6),
        name="product",
    )(at, *([left] * len(which)), grad, *[array for array, _ in adds], *tails, *tokens)
    return found if halves else found[0]


class Reduction:
    def __init__(self, left, grad, more=(None, None, None), tokens=()):
        self.left, self.grad, self.more = left, grad, more
        sent = product(left, (1, 3), grad, (), False, tokens, more[2])
        self.sent, self.got = move(sent, "fsdp", 1)

    def hold(self, *tokens):
        self.got = after(self.got, *tokens)

    def over_x(self, start=(), arrive=(), tokens=()):
        self.near = self.got
        sent = product(
            self.left, (2,), self.grad, [(self.got, 1)], False, tokens, self.more[1]
        )
        self.sent, self.got = move(sent, "fsdp", 2, start, arrive)

    def then_over_y(self, start=(), arrive=(), tokens=()):
        adds = [(self.near, 0), (self.got, 0)]
        self.kept, sent = product(self.left, (0,), self.grad, adds, True, tokens, self.more[0])
        self.sent, self.got = move(sent, "ctx", 1, start, arrive)

    def first_over_y(self, start=(), arrive=(), tokens=()):
        self.kept, sent = product(self.left, (0, 2), self.grad, [(self.got, 0)], True, tokens)
        self.sent, self.got = move(sent, "ctx", 1, start, arrive)

    def then_over_x(self, start=(), arrive=()):
        total = (self.kept.astype(F32) + self.got.astype(F32)).astype(BF16)
        half = total.shape[0] // 2
        self.kept = total[:half]
        self.sent, self.got = move(total[half:], "fsdp", 2, start, arrive)


def ctx_bits():
    bits = [1]
    while 2 * bits[-1] < lax.axis_size("ctx"):
        bits.append(2 * bits[-1])
    return bits


def spread_order():
    apart = jnp.arange(lax.axis_size("ctx"), dtype=jnp.int32) ^ lax.axis_index("ctx")
    where = jnp.zeros_like(apart)
    for k, bit in enumerate(reversed(ctx_bits())):
        where += ((apart // bit) % 2) << k
    return where


class Spread:
    def __init__(self, block):
        self.block, self.bits = block, ctx_bits()

    def step(self, arrive=()):
        _, got = move(self.block, "ctx", self.bits.pop(), (), arrive)
        self.block = jnp.concatenate([self.block, got], axis=0)

    def finish(self, arrive=()):
        while self.bits:
            self.step(arrive)
        return self.block


class BlockSums:
    def __init__(self, blocks):
        self.blocks, self.bits = blocks, ctx_bits()

    def step(self, start=(), arrive=()):
        half = self.blocks.shape[0] // 2
        bit = self.bits.pop(0)
        self.sent, got = move(self.blocks[half:], "ctx", bit, start, arrive)
        self.blocks = (self.blocks[:half].astype(F32) + got.astype(F32)).astype(BF16)

    def finish(self, start=()):
        while self.bits:
            self.step(start)
        return self.blocks


def stretches_of(shapes, rows):
    found, at = [], 0
    for index, (height, width) in enumerate(shapes):
        for first in range(0, height, rows):
            found.append((index, first, at))
            at += width
    return found, at


def fold_kernel(count, side_ref, *refs):
    new_ref, sent_ref = refs[2 * count :]
    half = new_ref.shape[0]
    mine = pl.multiple_of(side_ref[0] * half, half)
    theirs = pl.multiple_of((1 - side_ref[0]) * half, half)
    at = 0
    for i in range(count):
        kept_ref, got_ref = refs[2 * i], refs[2 * i + 1]
        height, width = kept_ref.shape
        for first in range(0, height, 2 * half):
            columns = slice(at, at + width)
            for row, out_ref in ((mine, new_ref), (theirs, sent_ref)):
                rows = pl.ds(first + row, half)
                total = kept_ref[rows, :].astype(F32) + got_ref[rows, :].astype(F32)
                out_ref[:, columns] = total.astype(BF16)
            at += width


def fold_pack(side, pairs):
    arrays = [array for pair in pairs for array in pair]
    rows = min(array.shape[0] for array in arrays)
    _, width = stretches_of([kept.shape for kept, _ in pairs], rows)
    shape = (rows // 2, width)
    return pl.pallas_call(
        functools.partial(fold_kernel, len(pairs)),
        in_specs=[pl.BlockSpec(memory_space=pltpu.SMEM)] + [whole(array.shape) for array in arrays],
        out_specs=[whole(shape)] * 2,
        out_shape=[jax.ShapeDtypeStruct(shape, BF16)] * 2,
        compiler_params=pltpu.CompilerParams(vmem_limit_bytes=VMEM_LIMIT),
        cost_estimate=lasting(2),
        name="fold",
    )(side.reshape(1), *arrays)


def join_kernel(side_ref, own_ref, got_ref, out_ref):
    half = own_ref.shape[0]
    out_ref[pl.ds(pl.multiple_of(side_ref[0] * half, half), half), :] = own_ref[...]
    out_ref[pl.ds(pl.multiple_of((1 - side_ref[0]) * half, half), half), :] = got_ref[...]


def join_pack(side, own, got):
    shape = (2 * own.shape[0], own.shape[1])
    return pl.pallas_call(
        join_kernel,
        in_specs=[pl.BlockSpec(memory_space=pltpu.SMEM)] + [whole(own.shape)] * 2,
        out_specs=whole(shape),
        out_shape=jax.ShapeDtypeStruct(shape, BF16),
        compiler_params=pltpu.CompilerParams(vmem_limit_bytes=VMEM_LIMIT),
        cost_estimate=lasting(2),
        name="join",
    )(side.reshape(1), own, got)


def unpack_kernel(parts, outs, side_ref, own_ref, got_ref, *out_refs):
    rows = own_ref.shape[0]
    for side in range(2):

        @pl.when(side_ref[0] == side)
        def _():
            for array, height, first, at in parts:
                for half, ref in ((side, own_ref), (1 - side, got_ref)):
                    row = half * (height // 2) + first
                    for out_ref, (source, top, end, left, right) in zip(out_refs, outs):
                        if source == array and top <= row < end:
                            to = slice(row - top, row - top + rows)
                            out_ref[to, :] = ref[:, at + left : at + right].astype(F32)


def unpack(side, own, got, shapes, outs):
    found, _ = stretches_of([(height // 2, width) for height, width in shapes], own.shape[0])
    parts = [(index, shapes[index][0], first, at) for index, first, at in found]
    out_shapes = [(end - top, right - left) for _, top, end, left, right in outs]
    return pl.pallas_call(
        functools.partial(unpack_kernel, parts, outs),
        in_specs=[pl.BlockSpec(memory_space=pltpu.SMEM)] + [whole(own.shape)] * 2,
        out_specs=[whole(shape) for shape in out_shapes],
        out_shape=[jax.ShapeDtypeStruct(shape, F32) for shape in out_shapes],
        compiler_params=pltpu.CompilerParams(vmem_limit_bytes=VMEM_LIMIT),
        cost_estimate=lasting(4),
        name="unpack",
    )(side.reshape(1), own, got)


class Pack:
    def __init__(self, pairs):
        self.pairs = pairs
        self.shapes = [(2 * kept.shape[0], kept.shape[1]) for kept, _ in pairs]

    def hold(self, *tokens):
        self.got = after(self.got, *tokens)

    def side(self, bit):
        return (lax.axis_index("ctx") // bit) % 2

    def over_z(self, start=(), arrive=()):
        self.kept, sent = fold_pack(self.side(2), self.pairs)
        self.sent, self.got = move(sent, "ctx", 2, start, arrive)

    def rest(self, start=(), arrive=()):
        self.own = (self.kept.astype(F32) + self.got.astype(F32)).astype(BF16)
        self.kept = None
        for bit in ctx_bits()[2:]:
            self.total()
            self.sent, self.got = move(self.own, "ctx", bit, start, arrive)
            self.kept = self.own

    def total(self):
        if self.kept is not None:
            self.own = (self.kept.astype(F32) + self.got.astype(F32)).astype(BF16)
            self.kept = None

    def back_z(self, start=(), arrive=()):
        self.total()
        self.sent, got = move(self.own, "ctx", 2, start, arrive)
        self.own = join_pack(self.side(2), self.own, got)

    def back_y(self, outs, start=(), arrive=()):
        self.sent, got = move(self.own, "ctx", 1, start, arrive)
        return unpack(self.side(1), self.own, got, self.shapes, outs)


def shift_along(block, axis, distance):
    devices = range(lax.axis_size(axis))
    route = [(i - distance, i) for i in devices if i - distance in devices]
    return lax.ppermute(block, axis, route)


def segment_starts(positions, starts):
    reached = starts[None, :] <= positions[:, None]
    return jnp.max(jnp.where(reached, starts[None, :], -1), axis=1)


class Scan:
    def __init__(self, own, send, upwards):
        self.own, self.send, self.upwards = own, send, upwards
        self.seen = None
        self.bits = ctx_bits()

    def step(self, arrive=()):
        bit = self.bits.pop(0)
        above = (lax.axis_index("ctx") // bit) % 2 == 1
        _, got = move(self.send, "ctx", bit, (), arrive)
        first = above if self.upwards else jnp.logical_not(above)
        self.own, self.send, self.seen = scan_step(
            first, self.own, self.seen, got, not self.bits
        )
        return self.send

    def finish(self, arrive=()):
        while self.bits:
            self.step(arrive)
        return self.seen


def outer_sum(left, right):
    return dot_tn(left, right)


def time_steps(left, right):
    return dot_nt(left, right)


def local(
    tokens,
    cotangent,
    doc_starts,
    gain_mix,
    w_z,
    w_xbc,
    w_dt,
    conv_w,
    conv_b,
    dt_bias,
    a_log,
    skip_factor,
    w_mo,
    w_q,
    key_value_weight,
    w_o,
    gain_ffn,
    w_gate,
    w_up,
    w_down,
):
    xbc_dt = jnp.pad(
        jnp.concatenate([w_xbc, w_dt], axis=1), ((0, 0), (0, LANES - MAMBA_HEADS))
    )
    small = jnp.concatenate(
        [v.reshape(-1) for v in (gain_mix, conv_w, conv_b, dt_bias, a_log, skip_factor, gain_ffn)]
    )
    wide = w_q.shape[1] + key_value_weight.shape[1]
    small_rows = 16
    small = jnp.pad(small, (0, small_rows * wide - small.shape[0])).reshape(small_rows, wide)
    shard_qkv = jnp.concatenate([jnp.concatenate([w_q, key_value_weight], axis=1), small], axis=0)
    near_qkv = swap(shard_qkv, "fsdp", 2)
    near_xbc = swap(xbc_dt, "fsdp", 2)
    side_by_side = lambda w, rows: [w[i : i + rows] for i in range(0, w.shape[0], rows)]
    rows_in = w_z.shape[0]
    shard_omo = jnp.concatenate([w_o, w_mo], axis=0)
    shard_zo = jnp.concatenate([w_z] + side_by_side(shard_omo, rows_in), axis=1)
    shard_ffn = jnp.concatenate([w_gate, w_up] + side_by_side(w_down, rows_in), axis=1)
    shard_zo = after(shard_zo, near_qkv)
    near_zo = swap(shard_zo, "fsdp", 2)
    shard_ffn = after(shard_ffn, near_qkv)
    near_ffn = swap(shard_ffn, "fsdp", 2)
    other_xbc, other_zo, other_ffn = [
        swap(shard, "fsdp", 1) for shard in (xbc_dt, shard_zo, shard_ffn)
    ]
    full_qkv, small_all = place(
        *whole_parts(
            shard_qkv,
            swap(shard_qkv, "fsdp", 1),
            near_qkv,
            [(shard_qkv.shape[1], 0, rows_in, 0)],
            (),
            small_rows,
        )
    )
    model = w_down.shape[1]

    def stretches(out, shard_rows):
        return [(model, out, shard_rows, first) for first in range(0, shard_rows, rows_in)]

    ranks = lax.axis_size("fsdp")
    small_all = small_all.reshape(ranks, -1).astype(F32)
    at = [0]

    def unpack(rows, width):
        part = small_all[:, at[0] : at[0] + rows * width].reshape(-1, rows, width)
        at[0] += rows * width
        return part.transpose(1, 0, 2).reshape(rows, -1)

    full_gain_mix = unpack(1, gain_mix.shape[0])[0]
    full_conv_w = unpack(CONV, conv_b.shape[0])
    full_conv_b = unpack(1, conv_b.shape[0])[0]
    full_dt_bias = unpack(1, dt_bias.shape[0])[0]
    full_a_log = unpack(1, dt_bias.shape[0])[0]
    full_skip = unpack(1, dt_bias.shape[0])[0]
    full_gain_ffn = unpack(1, gain_ffn.shape[0])[0]
    o_rows = w_o.shape[0]
    wide_in = xbc_dt.shape[1]
    ctx_rank = lax.axis_index("ctx")
    inputs = tokens[0].astype(F32)
    rows = inputs.shape[0]
    starts = doc_starts[0]
    base = ctx_rank * rows
    positions = base + jnp.arange(rows, dtype=jnp.int32)
    doc = segment_starts(positions, starts)
    doc_col = jnp.pad(doc, (0, 8))[:, None]
    doc_row = jnp.broadcast_to(doc[None, :], (8, rows))
    scalars = jnp.concatenate([doc[CHUNK - 1 :: CHUNK], base[None]])
    attn_scalars = jnp.concatenate(
        [doc[::QUERY_TILE], doc[QUERY_TILE - 1 :: QUERY_TILE], base[None], spread_order()]
    )
    half = HEAD_SIZE // 2
    freqs = ROPE_BASE ** (
        -2.0 * (jnp.arange(LANES, dtype=jnp.int32) % half).astype(F32) / HEAD_SIZE
    )
    angles = positions.astype(F32)[:, None] * freqs[None, :]
    cosine, sine = jnp.cos(angles), jnp.sin(angles)
    conv_pack = jnp.pad(
        jnp.concatenate([full_conv_w, full_conv_b[None]], axis=0), ((0, 3), (0, 0))
    )
    pad_heads = lambda v: jnp.pad(v, (0, LANES - MAMBA_HEADS))[None]
    head_pack = jnp.concatenate(
        [pad_heads(full_dt_bias), pad_heads(-jnp.exp(full_a_log)), jnp.zeros((6, LANES), F32)], axis=0
    )
    skip_wide = jnp.repeat(full_skip, MAMBA_HEAD_SIZE)[None]

    scale_one = lax.rsqrt(jnp.mean(inputs * inputs, axis=-1, keepdims=True) + EPSILON)
    normed = (inputs * scale_one * full_gain_mix[None, :]).astype(BF16)
    q_width = QUERY_HEADS * HEAD_SIZE
    qkv_raw = dot_nn(normed, full_qkv)
    query, kv_first, kv_second = rope(
        qkv_raw[:, :q_width], qkv_raw[:, q_width:], cosine, sine
    )
    spreads = [Spread(kv) for kv in (kv_first, kv_second)]
    full_xbc = place(
        *whole_parts(
            xbc_dt,
            other_xbc,
            after(near_xbc, query),
            [(xbc_dt.shape[1], 0, rows_in, 0)],
        ),
        [other_zo, other_ffn],
    )[0]
    for spread_kv in spreads:
        spread_kv.step()
        spread_kv.block = after(spread_kv.block, full_xbc)
        spread_kv.step()
    mixed_in = dot_nn(normed, full_xbc[:, :CHANNELS]).astype(BF16)
    dt_raw = dot_nn(normed, full_xbc[:, CHANNELS:])
    edge = shift_along(mixed_in[rows - 8 :], "ctx", 1).astype(F32)
    y_local, state_local, message, own_state, decay, c_mat = mamba_forward(
        scalars,
        edge,
        mixed_in,
        dt_raw,
        doc_col[:rows],
        conv_pack,
        head_pack,
        skip_wide,
        [spreads[0].block],
    )
    kv_all = [spreads[0].finish([message])]
    scan = Scan(own_state, message, True)
    first_send = scan.step([kv_all[0]])
    tokens = [first_send]
    attended = [attend(attn_scalars, query, kv_all[0], doc_row, 0, tokens)]
    first_done = attended[0][0]
    kv_all.append(spreads[1].finish([first_done]))
    carried = whole_parts(
        shard_zo,
        other_zo,
        after(near_zo, first_send),
        [(w_z.shape[1], 0, rows_in, 0)] + stretches(1, shard_omo.shape[0]),
    )
    tokens = [scan.step([first_done]), first_done]
    *second, full_z, full_omo = attend(
        attn_scalars, query, kv_all[1], doc_row, 1, tokens, carried
    )
    attended.append(second)
    second_done = attended[1][0]
    gate_z = dot_nn(normed, full_z).astype(BF16)
    state_in = scan.finish([second_done])
    y_total, both, state_true = mamba_correct(
        y_local, state_local, c_mat, decay, state_in, gate_z, attended[0][0], attended[1][0]
    )
    full_gate_up, full_down = place(
        *whole_parts(
            shard_ffn,
            other_ffn,
            after(near_ffn, y_total),
            [(2 * w_gate.shape[1], 0, rows_in, 0)] + stretches(1, w_down.shape[0]),
        )
    )
    hidden = inputs + dot_nn(both, full_omo)
    gain_two = full_gain_ffn
    scale_two = lax.rsqrt(jnp.mean(hidden * hidden, axis=-1, keepdims=True) + EPSILON)
    normed_ffn = (hidden * scale_two * gain_two[None, :]).astype(BF16)
    gate_up = dot_nn(normed_ffn, full_gate_up)
    ff = gate_up.shape[1] // 2
    gate, upper = gate_up[:, :ff], gate_up[:, ff:]
    sig_gate = jax.nn.sigmoid(gate)
    silu_gate = gate * sig_gate
    activ = (silu_gate * upper).astype(BF16)
    result = hidden + dot_nn(activ, full_down)

    grad_out = cotangent[0]
    down = Reduction(activ, grad_out)
    grad_act = time_steps(grad_out, full_down)
    grad_gate = (grad_act * upper * sig_gate * (1.0 + gate * (1.0 - sig_gate))).astype(BF16)
    grad_up = (grad_act * silu_gate).astype(BF16)
    grad_gate_up = jnp.concatenate([grad_gate, grad_up], axis=1)
    gate_up_sum = Reduction(normed_ffn, grad_gate_up)
    grad_n2 = time_steps(grad_gate_up, full_gate_up)
    scaled_two = grad_n2 * gain_two[None, :]
    grad_hidden = (
        grad_out.astype(F32)
        + scale_two * scaled_two
        - hidden * scale_two**3 * jnp.mean(scaled_two * hidden, axis=-1, keepdims=True)
    )
    gate_up_sum.over_x()
    down.first_over_y(tokens=[gate_up_sum.sent])
    grad_hid_b = after(grad_hidden.astype(BF16), gate_up_sum.sent, down.sent)
    both_grad = time_steps(grad_hid_b, full_omo).astype(BF16)
    grad_y, grad_z, own_grad, grad_message, grad_attn = mamba_gate_back(
        both_grad, gate_z, y_total, c_mat, decay, own_state
    )
    omo = Reduction(both, grad_hid_b)
    z_sum = Reduction(normed, grad_z)
    scan = Scan(own_grad, grad_message, False)
    backs = []

    def back(j, tokens):
        backs.append(
            attend_back(
                attn_scalars,
                query,
                grad_attn,
                attended[j][1],
                attended[j][2],
                kv_all[j],
                doc_row,
                j,
                tokens,
            )
        )

    down.hold(grad_attn)
    down.then_over_x()
    backs = []

    def back(j, tokens):
        backs.append(
            attend_back(
                attn_scalars,
                query,
                grad_attn,
                attended[j][1],
                attended[j][2],
                kv_all[j],
                doc_row,
                j,
                tokens,
            )
        )

    scan.step()
    gate_up_sum.hold(scan.send)
    gate_up_sum.then_over_y()
    omo.first_over_y(tokens=[gate_up_sum.sent])
    z_sum.over_x()
    scan.step([gate_up_sum.sent])
    gate_up_sum.hold(scan.send)
    down.hold(scan.send)
    ffn = Pack([(gate_up_sum.kept, gate_up_sum.got), (down.kept, down.got)])
    ffn.over_z()
    back(0, [scan.send, ffn.sent, omo.sent, z_sum.sent])
    first_done = backs[0][0]
    for part in (ffn, omo, z_sum):
        part.hold(first_done)
    state_grad = scan.finish([first_done])
    ffn.rest()
    omo.then_over_x()
    z_sum.then_over_y()
    first_kv = BlockSums(backs[0][1])
    first_kv.sent = first_kv.blocks[first_kv.blocks.shape[0] // 2 :]
    grad_xbc, tail, edge_grad, grad_conv, grad_heads = mamba_back(
        scalars,
        edge,
        mixed_in,
        dt_raw,
        doc_col,
        doc_row,
        conv_pack,
        head_pack,
        skip_wide,
        grad_y,
        y_total,
        state_true,
        state_grad,
        [ffn.sent, z_sum.sent, omo.sent, first_kv.sent, first_done],
    )
    third_done = grad_heads
    for part in (ffn, omo, z_sum):
        part.hold(third_done)
    first_kv.step((), [third_done])
    mixer = Pack([(z_sum.kept, z_sum.got), (omo.kept, omo.got)])
    mixer.over_z()
    behind = shift_along(edge_grad, "ctx", -1)
    grad_xbc = lax.dynamic_update_slice(grad_xbc, (tail + behind).astype(BF16), (rows - 8, 0))
    fsdp_rank = lax.axis_index("fsdp")
    conv_width, heads_width = conv_b.shape[0], dt_bias.shape[0]
    small_width = -(-(conv_width * (CONV + 1) + heads_width * 3) // rows_in)
    small_at = CHANNELS + MAMBA_HEADS
    blocks = [
        g.reshape(g.shape[0], ranks, -1).transpose(1, 0, 2).reshape(ranks, -1)
        for g in (grad_conv[: CONV + 1], grad_heads[:3, :MAMBA_HEADS])
    ]
    small_grad = jnp.concatenate(blocks, axis=1)
    small_count = small_grad.shape[1]
    small_grad = jnp.pad(small_grad, ((0, 0), (0, small_width * rows_in - small_count)))
    small_grad = jnp.pad(
        small_grad.reshape(ranks, rows_in, small_width),
        ((0, 0), (0, 0), (MAMBA_HEADS, LANES - MAMBA_HEADS - small_width)),
    )
    block_of = lambda k: lax.dynamic_index_in_dim(small_grad, fsdp_rank ^ k, 0, False)
    more = [block_of(0), block_of(2), jnp.concatenate([block_of(1), block_of(3)], axis=0)]
    ffn.total()
    xbc_sum = Reduction(
        normed, grad_xbc, more, [ffn.own, z_sum.got, omo.got, first_kv.blocks]
    )
    xbc_sum.over_x()
    ffn.back_z((), [xbc_sum.sent])
    back(1, [xbc_sum.sent, mixer.sent, ffn.own, first_kv.blocks, third_done])
    second_done = backs[1][0]
    xbc_sum.hold(second_done)
    mixer.hold(second_done)
    first_kv.step((), [second_done])
    second_kv = BlockSums(backs[1][1])
    second_kv.step()
    kv_left = second_kv.sent
    y_in = [second_kv.blocks]
    xbc_sum.then_over_y()
    y_left = [xbc_sum.sent]
    xbc = Pack([(xbc_sum.kept, after(xbc_sum.got, *y_in))])
    second_kv.step(y_left)
    z_in = [second_kv.blocks]
    first_kv.step((), y_in)
    grad_kv0, grad_kv1 = first_kv.finish(), second_kv.finish()
    grad_qkv = rope_back(backs[0][0], backs[1][0], grad_kv0, grad_kv1, cosine, sine)
    qkv_sum = Reduction(normed, grad_qkv)
    core_left = [qkv_sum.sent]
    mixer.rest((), core_left)
    qkv_sum.over_x()
    x_left = [qkv_sum.sent]
    xbc.pairs = [(xbc_sum.kept, after(xbc_sum.got, *x_left))]
    xbc.over_z()
    ff = w_gate.shape[1]
    grad_w_gate, grad_w_up, grad_w_down = ffn.back_y(
        [
            (0, 0, rows_in, 0, ff),
            (0, 0, rows_in, ff, 2 * ff),
            (1, 0, w_down.shape[0], 0, model),
        ],
        [kv_left],
        x_left,
    )
    qkv_sum.then_over_y()
    y_left = [qkv_sum.sent]
    xbc.rest((), y_left)
    mixer.back_z((), y_left)
    qkv = Pack([(qkv_sum.kept, after(qkv_sum.got, mixer.own))])
    qkv.over_z()
    z_left = [qkv.sent]
    xbc.back_z((), z_left)
    omo_rows = shard_omo.shape[0]
    mixer_outs = [
        (0, 0, rows_in, 0, w_z.shape[1]),
        (1, 0, o_rows, 0, model),
        (1, o_rows, omo_rows, 0, model),
    ]
    qkv.rest()
    qkv.back_z()
    join_left = [qkv.own]
    last_left = [qkv.sent]
    grad_w_z, grad_w_o, grad_w_mo = mixer.back_y(mixer_outs, (), last_left)
    grad_w_q, grad_w_kv = qkv.back_y(
        [(0, 0, rows_in, 0, q_width), (0, 0, rows_in, q_width, qkv_raw.shape[1])],
        [grad_w_z],
    )
    grad_w_xbc, grad_w_dt = xbc.back_y(
        [(0, 0, rows_in, 0, CHANNELS), (0, 0, rows_in, CHANNELS, wide_in)], (), [qkv.sent]
    )
    small_own = grad_w_dt[:, small_at - CHANNELS : small_at - CHANNELS + small_width].reshape(-1)[:small_count]
    conv_own = small_own[: conv_width * (CONV + 1)].reshape(CONV + 1, conv_width)
    heads_own = small_own[conv_width * (CONV + 1) :].reshape(3, heads_width)
    grad_n1 = (
        time_steps(after(grad_z, *y_in), full_z)
        + time_steps(after(grad_xbc, *y_left), full_xbc)
        + time_steps(after(grad_qkv, *z_left), full_qkv)
    )
    scaled_one = grad_n1 * full_gain_mix[None, :]
    grad_tokens = (
        grad_hidden
        + scale_one * scaled_one
        - inputs * scale_one**3 * jnp.mean(scaled_one * inputs, axis=-1, keepdims=True)
    )
    row_sums = lambda grad, weight: jnp.sum(grad * weight.astype(F32), axis=1)
    grad_gain_ffn = (
        row_sums(grad_w_gate, w_gate) + row_sums(grad_w_up, w_up)
    ) / gain_ffn.astype(F32)
    grad_gain_mix = (
        row_sums(grad_w_z, w_z)
        + row_sums(grad_w_xbc, w_xbc)
        + row_sums(grad_w_dt[:, :MAMBA_HEADS], w_dt)
        + row_sums(grad_w_q, w_q)
        + row_sums(grad_w_kv, key_value_weight)
    ) / gain_mix.astype(F32)
    totals = (
        grad_gain_mix,
        grad_w_z,
        grad_w_xbc,
        grad_w_dt[:, :MAMBA_HEADS],
        conv_own[:CONV],
        conv_own[CONV],
        heads_own[0],
        heads_own[1],
        heads_own[2],
        grad_w_mo,
        grad_w_q,
        grad_w_kv,
        grad_w_o,
        grad_gain_ffn,
        grad_w_gate,
        grad_w_up,
        grad_w_down,
    )
    return (result.astype(BF16)[None], grad_tokens[None]) + totals


def solution(mesh):
    in_specs = (
        P("fsdp", "ctx", None),
        P("fsdp", "ctx", None),
        P("fsdp", None),
        P("fsdp"),
        P("fsdp", None),
        P("fsdp", None),
        P("fsdp", None),
        P(None, "fsdp"),
        P("fsdp"),
        P("fsdp"),
        P("fsdp"),
        P("fsdp"),
        P("fsdp", None),
        P("fsdp", None),
        P("fsdp", None),
        P("fsdp", None),
        P("fsdp"),
        P("fsdp", None),
        P("fsdp", None),
        P("fsdp", None),
    )
    out_specs = (
        P("fsdp", "ctx", None),
        P("fsdp", "ctx", None),
        P("fsdp"),
        P("fsdp", None),
        P("fsdp", None),
        P("fsdp", None),
        P(None, "fsdp"),
        P("fsdp"),
        P("fsdp"),
        P("fsdp"),
        P("fsdp"),
        P("fsdp", None),
        P("fsdp", None),
        P("fsdp", None),
        P("fsdp", None),
        P("fsdp"),
        P("fsdp", None),
        P("fsdp", None),
        P("fsdp", None),
    )
    return jax.shard_map(local, mesh=mesh, in_specs=in_specs, out_specs=out_specs, check_vma=False)
```
